128 devices in a mesh: bx: 8 (over z, core), by: 16 (over y, x).
Axes of the slice: x: 4, y: 4, z: 4, core: 2. Of those that a mesh axis runs over, the one named last changes fastest.
Arguments:
- tracer: float32 [16, 1024, 4096], P(None, 'by', 'bx'), may hold values from -6 to 6
- u_east: float32 [16, 1024, 4096], P(None, 'by', 'bx'), may hold values from -1.5 to 1.5
- v_north: float32 [16, 1024, 4096], P(None, 'by', 'bx'), may hold values from -1.5 to 1.5
- kmt: int32 [1024, 4096], P('by', 'bx'), may hold values from 0 to 16, as said below
- dest: int32 [16, 32], P('by', 'bx'), may hold values from -1 to 7, as said below
- dz: float32 [16], replicated, may hold values from 0.02 to 0.12
- wind: float32 [1024, 4096], P('by', 'bx'), may hold values from -6 to 6
Outputs:
- tracer_out: float32 [16, 1024, 4096], P(None, 'by', 'bx')
- barotropic: float32 [2, 1024, 8192], P(None, 'by', 'bx')
The draws below stay inside these ranges and needn't reach their ends.
Inputs may be any that keep to these rules, and one draw needn't show every extreme that they name: kmt is 0 on the first and last latitude rows and on every cell of a block whose dest is -1. `dest`: the 4 entries of one device that are not -1 are distinct.
All inputs are finite; a program needn't handle non-finite values.
Results may differ from the reference program's by a relative error of at most 0.0001.
Values sent between devices are 32-bit elements; how exact they have to be, the bound alone decides.
A program may use at most 192 MiB of HBM per device.

```python
import math
import jax
import jax.numpy as jnp
from jax import lax

KL = 16
CY = 64
BS = 128
BPD = 4
SUB = 2
ITERS = 4
NX = 4096
NY = 1024
BTC = 8192
N_BX = 8
N_BY = 16


def land_blocks(key):
    landkey = jax.random.fold_in(key, 11)
    return jax.random.randint(landkey, (N_BY, N_BX * BPD), 0, 8) == 0


def draw_kmt(key, part):
    land = land_blocks(key)
    key = jax.random.fold_in(key, 1)
    levels = jax.random.randint(key, (NY, NX), 0, KL + 1)
    land_cells = jnp.repeat(jnp.repeat(land, CY, axis=0), BS, axis=1)
    row_index = jnp.arange(NY)[:, None]
    polar = (row_index == 0) | (row_index == NY - 1)
    return jnp.where(land_cells | polar, 0, levels).astype(jnp.int32)


def draw_dest(key, part):
    land = land_blocks(key)
    key = jax.random.fold_in(key, 2)
    device_keys = jax.random.split(key, N_BY * N_BX)
    chosen = jax.vmap(lambda single: jax.random.permutation(single, N_BX)[:BPD])(device_keys)
    owners = chosen.reshape(N_BY, N_BX * BPD)
    return jnp.where(land, -1, owners).astype(jnp.int32)


def level_of(rng, extent, shards, smallest, high):
    factor_of = 1.0
    for position, shards_of in shards:
        draws = jax.random.uniform(jax.random.fold_in(jax.random.fold_in(rng, 6), position), (shards_of,), jnp.float32, smallest / len(shards), high / len(shards))
        factor_of = factor_of * jnp.repeat(jnp.exp(draws), extent[position] // shards_of).reshape((-1,) + (1,) * (len(extent) - 1 - position))
    return factor_of


def normal_values(stream_key, extent, scale, reach, cuts=(), dtype=jnp.bfloat16):
    array = scale * jax.random.normal(stream_key, extent, jnp.float32)
    if cuts:
        array = array * level_of(stream_key, extent, cuts, -0.22, 0.18)
    return jnp.clip(array, -reach, reach).astype(dtype)


def setup_inputs(seed: int = 0) -> dict:
    key_list = jax.random.split(jax.random.key(seed), 8)
    tracer = normal_values(key_list[0], (KL, NY, NX), 1.0, 6.0, ((1, 16), (2, 8)), jnp.float32)
    u_east = normal_values(key_list[1], (KL, NY, NX), 0.1, 1.5, ((1, 16), (2, 8)), jnp.float32)
    v_north = normal_values(key_list[2], (KL, NY, NX), 0.1, 1.5, ((1, 16), (2, 8)), jnp.float32)
    kmt = draw_kmt(jax.random.fold_in(key_list[7], 71), 0)
    dest = draw_dest(jax.random.fold_in(key_list[7], 71), 0)
    dz = jnp.clip(jnp.exp(jax.random.uniform(key_list[5], (KL,), jnp.float32, math.log(0.02), math.log(0.12))), 0.02, 0.12)
    wind = normal_values(key_list[6], (NY, NX), 1.0, 6.0, ((0, 16), (1, 8)), jnp.float32)
    return dict(tracer=tracer, u_east=u_east, v_north=v_north, kmt=kmt, dest=dest, dz=dz, wind=wind)


KAPPA = 0.12
SIGMA = 0.2
OFFSETS = ((-1, -1, 0.5), (-1, 0, 1.0), (-1, 1, 0.5), (0, -1, 1.0), (0, 1, 1.0), (1, -1, 0.5), (1, 0, 1.0), (1, 1, 0.5))


def pad_grid(field):
    field = jnp.concatenate([field[..., -1:], field, field[..., :1]], axis=-1)
    border = jnp.zeros_like(field[..., :1, :])
    return jnp.concatenate([border, field, border], axis=-2)


def advance(field, east, north, wet):
    flux_east = wet[:, :, :-1] * wet[:, :, 1:] * (east[:, :, :-1] * (field[:, :, :-1] + field[:, :, 1:]) * 0.5 - KAPPA * (field[:, :, 1:] - field[:, :, :-1]))
    flux_north = wet[:, :-1, :] * wet[:, 1:, :] * (north[:, :-1, :] * (field[:, :-1, :] + field[:, 1:, :]) * 0.5 - KAPPA * (field[:, 1:, :] - field[:, :-1, :]))
    spread = (flux_east[:, 1:-1, 1:] - flux_east[:, 1:-1, :-1]) + (flux_north[:, 1:, 1:-1] - flux_north[:, :-1, 1:-1])
    return field[:, 1:-1, 1:-1] - wet[:, 1:-1, 1:-1] * spread


def coefficients(depth_pad, ocean_pad):
    row_count = depth_pad.shape[0] - 2
    col_count = depth_pad.shape[1] - 2
    center_depth = depth_pad[1:-1, 1:-1]
    center_ocean = ocean_pad[1:-1, 1:-1]
    couplings = []
    diagonal = jnp.full((row_count, col_count), SIGMA, jnp.float32)
    for row_off, col_off, weight in OFFSETS:
        near_depth = depth_pad[1 + row_off:1 + row_off + row_count, 1 + col_off:1 + col_off + col_count]
        near_ocean = ocean_pad[1 + row_off:1 + row_off + row_count, 1 + col_off:1 + col_off + col_count]
        coupling = weight * 0.5 * (center_depth + near_depth) * center_ocean * near_ocean
        couplings.append(coupling)
        diagonal = diagonal + coupling
    return tuple(couplings), diagonal


def apply_operator(padded, couplings, diagonal):
    row_count, col_count = diagonal.shape
    result = diagonal * padded[1:-1, 1:-1]
    for (row_off, col_off, weight), coupling in zip(OFFSETS, couplings):
        result = result - coupling * padded[1 + row_off:1 + row_off + row_count, 1 + col_off:1 + col_off + col_count]
    return result


def reference(tracer, u_east, v_north, kmt, dest, dz, wind):
    wet = (lax.broadcasted_iota(jnp.int32, tracer.shape, 0) < kmt[None]).astype(jnp.float32)
    field = tracer
    east_pad = pad_grid(u_east)
    north_pad = pad_grid(v_north)
    wet_pad = pad_grid(wet)
    for step in range(SUB):
        field = advance(pad_grid(field), east_pad, north_pad, wet_pad)
    depth = jnp.sum(dz[:, None, None] * wet, axis=0)
    ocean = wet[0]
    couplings, diagonal = coefficients(pad_grid(depth), pad_grid(ocean))
    rhs = ocean * (wind + jnp.sum(dz[:, None, None] * wet * field, axis=0))
    solution = jnp.zeros_like(rhs)
    residual = rhs
    precond = residual / diagonal
    direction = precond
    norm_now = jnp.sum(residual * precond)
    for step in range(ITERS):
        image = apply_operator(pad_grid(direction), couplings, diagonal)
        alpha = norm_now / jnp.sum(direction * image)
        solution = solution + alpha * direction
        residual = residual - alpha * image
        precond = residual / diagonal
        norm_next = jnp.sum(residual * precond)
        direction = precond + (norm_next / norm_now) * direction
        norm_now = norm_next
    stacked = jnp.stack([solution, residual]).reshape(2, N_BY, CY, N_BX, BPD, BS)
    owners = dest.reshape(N_BY, N_BX, BPD)
    targets = lax.broadcasted_iota(jnp.int32, (1, 1, 1, N_BX, 1, 1), 3)
    gathered = jnp.zeros((2, N_BY, CY, N_BX, N_BX, BS), jnp.float32)
    for block in range(BPD):
        match = owners[:, :, block][None, :, None, None, :, None] == targets
        gathered = gathered + jnp.where(match, stacked[:, :, :, :, block, :][:, :, :, None, :, :], 0.0)
    return field, gathered.reshape(2, NY, BTC)
```

```python
import functools

import jax
import jax.numpy as jnp
from jax import lax
from jax.experimental import pallas as pl
from jax.experimental.pallas import tpu as pltpu
from jax.sharding import PartitionSpec as P

BS = 128
ITERS = 4
KAPPA = 0.12
SIGMA = 0.2
CENTRE = 1.0 / 3.0
HALF = 2.0 / 3.0
MESH = pl.DeviceIdType.MESH
ROWS = 64
COLS = 512
XR = ROWS + 8
XC = COLS + 128
STRIPS = ROWS // 8
F32 = jnp.float32
SIDES = ((0, 1), (0, -1), (1, 0), (-1, 0), (1, 1), (-1, 1), (1, -1), (-1, -1))


def strip(r):
    return pl.ds(8 * r, 8)


def rim(ref, side):
    dx, dy = SIDES[side]
    rows = {1: pl.ds(ROWS - 8, 8), -1: pl.ds(0, 8), 0: pl.ds(0, ROWS)}[dy]
    cols = {1: pl.ds(COLS - 128, 128), -1: pl.ds(0, 128), 0: pl.ds(0, COLS)}[dx]
    return ref.at[rows, cols]


def extend(ext, rims):
    from_s, from_n, from_w, from_e, from_sw, from_se, from_nw, from_ne = rims
    low = lax.broadcasted_iota(jnp.int32, (8, COLS), 0) < 4
    ext[ROWS:XR, 0:COLS] = jnp.where(low, from_n[...], from_s[...])
    east = lax.broadcasted_iota(jnp.int32, (ROWS, 128), 1) < 64
    ext[0:ROWS, COLS:XC] = jnp.where(east, from_e[...], from_w[...])
    east8 = lax.broadcasted_iota(jnp.int32, (8, 128), 1) < 64
    low8 = lax.broadcasted_iota(jnp.int32, (8, 128), 0) < 4
    ext[ROWS:XR, COLS:XC] = jnp.where(
        low8,
        jnp.where(east8, from_ne[...], from_nw[...]),
        jnp.where(east8, from_se[...], from_sw[...]),
    )


def spread_rows(get, count):
    sub = lax.broadcasted_iota(jnp.int32, (8, XC), 0)
    x = [get(r) for r in range(count)]
    up = [pltpu.roll(v, 7, 0) for v in x]
    down = [pltpu.roll(v, 1, 0) for v in x]
    out = []
    for r in range(count):
        north = jnp.where(sub == 7, up[(r + 1) % count], up[r])
        south = jnp.where(sub == 0, down[(r - 1) % count], down[r])
        out.append(x[r] + x[r] + (north + south))
    return out


def spread_cols(v):
    return v + v + (pltpu.roll(v, 1, 1) + pltpu.roll(v, XC - 1, 1))


def kernel(
    nx,
    ny,
    levels,
    tracer,
    u_east,
    v_north,
    kmt,
    dest,
    dz,
    wind,
    tracer_out,
    barotropic,
    c_x,
    u_x,
    v_x,
    k_x,
    ke_x,
    kn_x,
    wind_v,
    ae,
    be,
    an,
    bn,
    c1,
    c2,
    rhs,
    depth,
    inv,
    diag,
    basis,
    krim,
    zrim_row,
    zrim_col,
    zrim_corner,
    krim_row,
    krim_col,
    krim_corner,
    up_send,
    dn_send,
    col_send,
    up_recv,
    dn_recv,
    col_recv,
    ne_recv,
    nw_recv,
    se_recv,
    sw_recv,
    part,
    sums_x,
    part2,
    sums_y,
    stage,
    load_sem,
    out_sem,
    ks,
    kr,
    rs,
    rr,
    zs,
    zr,
    xs,
    xr,
    ys,
    yr,
    ds,
    dr,
):
    mx = lax.axis_index("bx")
    my = lax.axis_index("by")

    def peer(dx, dy):
        return (lax.rem(mx + dx + nx, nx), lax.rem(my + dy + ny, ny))

    inner = (slice(None), pl.ds(0, ROWS), pl.ds(0, COLS))
    loads = [
        pltpu.make_async_copy(tracer, c_x.at[inner], load_sem.at[0]),
        pltpu.make_async_copy(u_east, u_x.at[inner], load_sem.at[1]),
        pltpu.make_async_copy(v_north, v_x.at[inner], load_sem.at[2]),
        pltpu.make_async_copy(kmt, k_x.at[pl.ds(0, ROWS), pl.ds(0, COLS)], load_sem.at[3]),
        pltpu.make_async_copy(wind, wind_v, load_sem.at[4]),
    ]
    for copy in loads:
        copy.start()

    barrier = pltpu.get_barrier_semaphore()
    peers = [peer(off, 0) for off in range(1, nx)]
    peers += [peer(0, off) for off in range(1, ny)]
    peers += [peer(dx, dy) for dx, dy in SIDES[4:]]
    for target in peers:
        pl.semaphore_signal(barrier, inc=1, device_id=target, device_id_type=MESH)
    pl.semaphore_wait(barrier, len(peers))

    def remote(src, dst, send, recv, dx, dy):
        return pltpu.make_async_remote_copy(
            src_ref=src, dst_ref=dst, send_sem=send, recv_sem=recv, device_id=peer(dx, dy), device_id_type=MESH
        )

    def rim_refs(row, col, corner):
        return [row.at[0], row.at[1], col.at[0], col.at[1]] + [corner.at[i] for i in range(4)]

    k_rims = rim_refs(krim_row, krim_col, krim_corner)
    k_sends = [remote(rim(kmt, s), k_rims[s], ks.at[s], kr.at[s], *SIDES[s]) for s in range(8)]
    for copy in k_sends:
        copy.start()

    for copy in loads:
        copy.wait()
    lane = lax.broadcasted_iota(jnp.int32, (ROWS, 128), 1)
    west = lane < 64
    group = ((lane + 4) & 127) >> 3
    slot = ((lane + 4) & 7) - 4
    packed = [jnp.zeros((ROWS, 128), F32) for _ in range(3)]
    for k in range(levels):
        up_send[0, k : k + 1, :] = c_x[k, ROWS - 2 : ROWS - 1, 0:COLS]
        up_send[1, k : k + 1, :] = v_x[k, ROWS - 2 : ROWS - 1, 0:COLS]
        up_send[2, k : k + 1, :] = u_x[k, ROWS - 1 : ROWS, 0:COLS]
        up_send[3, k : k + 1, :] = c_x[k, ROWS - 1 : ROWS, 0:COLS]
        up_send[4, k : k + 1, :] = v_x[k, ROWS - 1 : ROWS, 0:COLS]
        dn_send[0, k : k + 1, :] = c_x[k, 1:2, 0:COLS]
        dn_send[1, k : k + 1, :] = v_x[k, 0:1, 0:COLS]
        dn_send[2, k : k + 1, :] = u_x[k, 0:1, 0:COLS]
        dn_send[3, k : k + 1, :] = c_x[k, 0:1, 0:COLS]
    first, last = pl.ds(0, 128), pl.ds(COLS - 128, 128)
    r_sends = [
        remote(up_send, up_recv, rs.at[0], rr.at[0], 0, 1),
        remote(dn_send, dn_recv, rs.at[1], rr.at[1], 0, -1),
        remote(up_send.at[pl.ds(2, 3), :, last], ne_recv, rs.at[2], rr.at[2], 1, 1),
        remote(up_send.at[pl.ds(3, 2), :, first], nw_recv, rs.at[3], rr.at[3], -1, 1),
        remote(dn_send.at[pl.ds(2, 2), :, last], se_recv, rs.at[4], rr.at[4], 1, -1),
        remote(dn_send.at[pl.ds(3, 1), :, first], sw_recv, rs.at[5], rr.at[5], -1, -1),
    ]
    for copy in r_sends:
        copy.start()
    for k in range(levels):
        for i, field in enumerate((c_x, u_x, v_x)):
            ends = jnp.where(west, field[k, 0:ROWS, 0:128], field[k, 0:ROWS, COLS - 128 : COLS])
            if k:
                ends = pltpu.roll(ends, 8 * k, 1)
            packed[i] = jnp.where(group == k, ends, packed[i])
    pu, pv = pltpu.roll(packed[1], 2, 1), pltpu.roll(packed[2], 3, 1)
    col_send[0] = jnp.where(slot < 0, packed[0], jnp.where(slot < 2, pu, pv))
    col_send[1] = jnp.where(slot < 2, packed[0], jnp.where(slot == 2, pu, pv))
    c_sends = [
        remote(col_send.at[0], col_recv.at[0], rs.at[6], rr.at[6], 1, 0),
        remote(col_send.at[1], col_recv.at[1], rs.at[7], rr.at[7], -1, 0),
    ]
    for copy in c_sends:
        copy.start()

    for copy in k_sends:
        copy.wait()
    extend(k_x, k_rims)
    sub = lax.broadcasted_iota(jnp.int32, (8, XC), 0)
    k_up = [pltpu.roll(k_x[strip(r), :], 7, 0) for r in range(STRIPS + 1)]
    for r in range(STRIPS + 1):
        here = k_x[strip(r), :]
        ke_x[strip(r), :] = jnp.minimum(here, pltpu.roll(here, XC - 1, 1))
        kn_x[strip(r), :] = jnp.minimum(here, jnp.where(sub == 7, k_up[(r + 1) % (STRIPS + 1)], k_up[r]))
        total = jnp.zeros((8, XC), F32)
        for k in range(levels):
            total = total + jnp.where(here > k, dz[k], 0.0)
        depth[strip(r), :] = total

    def ocean_of(r):
        return jnp.where(k_x[strip(r), :] > 0, 1.0, 0.0).astype(F32)

    rows_o = spread_rows(ocean_of, STRIPS + 1)
    rows_d = spread_rows(lambda r: depth[strip(r), :], STRIPS + 1)
    for r in range(STRIPS + 1):
        d = depth[strip(r), :]
        o = ocean_of(r)
        total = d * spread_cols(rows_o[r]) + spread_cols(rows_d[r]) - 8.0 * d
        full = SIGMA + 0.25 * o * total
        diag[strip(r), :] = full
        inv[strip(r), :] = o / full

    for copy in r_sends:
        copy.wait()
    for copy in c_sends:
        copy.wait()
    from_w, from_e = col_recv[0], col_recv[1]
    wide = [
        jnp.where(slot < 0, from_w, from_e),
        jnp.where(slot < 0, pltpu.roll(from_w, 126, 1), pltpu.roll(from_e, 126, 1)),
        jnp.where(slot < 0, pltpu.roll(from_w, 125, 1), pltpu.roll(from_e, 125, 1)),
    ]
    west16 = lax.broadcasted_iota(jnp.int32, (levels, 128), 1) < 64
    c_n = jnp.where(west16, sw_recv[0], se_recv[1])
    u_n = se_recv[0]
    c_s = jnp.where(west16, nw_recv[0], ne_recv[1])
    u_s = ne_recv[0]
    v_s = jnp.where(west16, nw_recv[1], ne_recv[2])
    n0, n1, s2, s1 = ROWS, ROWS + 1, XR - 2, XR - 1
    for k in range(levels):
        for i, field in enumerate((c_x, u_x, v_x)):
            field[k, 0:ROWS, COLS:XC] = pltpu.roll(wide[i], 128 - 8 * k, 1) if k else wide[i]
        for field, row, box, idx in (
            (c_x, n0, dn_recv, 3),
            (c_x, n1, dn_recv, 0),
            (c_x, s2, up_recv, 0),
            (c_x, s1, up_recv, 3),
            (u_x, n0, dn_recv, 2),
            (u_x, s1, up_recv, 2),
            (v_x, n0, dn_recv, 1),
            (v_x, s2, up_recv, 1),
            (v_x, s1, up_recv, 4),
        ):
            field[k, row : row + 1, 0:COLS] = box[idx, k : k + 1, :]
        c_x[k, n0 : n0 + 1, COLS:XC] = c_n[k : k + 1]
        u_x[k, n0 : n0 + 1, COLS:XC] = u_n[k : k + 1]
        c_x[k, s1 : s1 + 1, COLS:XC] = c_s[k : k + 1]
        u_x[k, s1 : s1 + 1, COLS:XC] = u_s[k : k + 1]
        v_x[k, s1 : s1 + 1, COLS:XC] = v_s[k : k + 1]

    rhs[...] = wind_v[...]

    def advance(get, put, width, count):
        def north_flux(r, c, up, nxt):
            c_north = jnp.where(sub == 7, nxt, up)
            return an[strip(r), :] * c + bn[strip(r), :] * c_north

        c = [get(r) for r in range(STRIPS + 1)]
        up = [pltpu.roll(v, 7, 0) for v in c]
        flux = north_flux(STRIPS, c[STRIPS], up[STRIPS], up[0])
        below = pltpu.roll(flux, 1, 0)
        for r in range(count):
            flux = north_flux(r, c[r], up[r], up[(r + 1) % (STRIPS + 1)])
            down = pltpu.roll(flux, 1, 0)
            flux_e = ae[strip(r), :] * c[r] + be[strip(r), :] * pltpu.roll(c[r], XC - 1, 1)
            spread = flux_e - pltpu.roll(flux_e, 1, 1)
            spread = spread + (flux - jnp.where(sub == 0, below, down))
            put(r, (c[r] - spread)[:, :width])
            below = down

    def level(k, carry):
        for r in range(STRIPS + 1):
            half_u, half_v = 0.5 * u_x[k, strip(r), :], 0.5 * v_x[k, strip(r), :]
            wet_e, wet_n = ke_x[strip(r), :] > k, kn_x[strip(r), :] > k
            ae[strip(r), :] = jnp.where(wet_e, half_u + KAPPA, 0.0)
            be[strip(r), :] = jnp.where(wet_e, half_u - KAPPA, 0.0)
            an[strip(r), :] = jnp.where(wet_n, half_v + KAPPA, 0.0)
            bn[strip(r), :] = jnp.where(wet_n, half_v - KAPPA, 0.0)

        def put1(r, value):
            c1[strip(r), :] = value

        def put2(r, value):
            c2[k, strip(r), :] = value
            wet = k_x[strip(r), 0:COLS] > k
            rhs[strip(r), :] = rhs[strip(r), :] + jnp.where(wet, dz[k] * value, 0.0)

        advance(lambda r: c_x[k, strip(r), :], put1, XC, STRIPS + 1)
        advance(lambda r: c1[strip(r), :], put2, COLS, STRIPS)
        pltpu.make_async_copy(c2.at[k], tracer_out.at[k], out_sem.at[k]).start()
        return carry

    lax.fori_loop(0, levels, level, 0)

    for r in range(STRIPS):
        start = jnp.where(k_x[strip(r), 0:COLS] > 0, rhs[strip(r), :], 0.0)
        basis[0, strip(r), 0:COLS] = start * inv[strip(r), 0:COLS]
    z_rims = rim_refs(zrim_row, zrim_col, zrim_corner)
    z_sends = [remote(rim(basis.at[0], s), z_rims[s], zs.at[s], zr.at[s], *SIDES[s]) for s in range(8)]
    for copy in z_sends:
        copy.start()
    for copy in z_sends:
        copy.wait()
    extend(basis.at[0], z_rims)

    moments = [jnp.zeros((8, 128), F32) for _ in range(8)]

    def inner_product(i, j):
        total = jnp.zeros((8, 128), F32)
        for r in range(STRIPS):
            product = diag[strip(r), 0:COLS] * basis[i, strip(r), 0:COLS] * basis[j, strip(r), 0:COLS]
            for m in range(COLS // 128):
                total = total + product[:, 128 * m : 128 * (m + 1)]
        return total

    moments[0] = inner_product(0, 0)
    for step in range(ITERS):
        rows_x = spread_rows(lambda r: basis[step, strip(r), :], STRIPS + 1)
        rows_dx = spread_rows(lambda r: depth[strip(r), :] * basis[step, strip(r), :], STRIPS + 1)
        for r in range(STRIPS + 1):
            d, x = depth[strip(r), :], basis[step, strip(r), :]
            image = d * spread_cols(rows_x[r]) + spread_cols(rows_dx[r]) - 8.0 * (d * x)
            scale = (0.25 / HALF) * inv[strip(r), :]
            following = scale * image - (CENTRE / HALF) * x
            if step:
                following = following + following - basis[step - 1, strip(r), :]
            basis[step + 1, strip(r), :] = following
        moments[2 * step + 1] = inner_product(step, step + 1)
        if step < ITERS - 1:
            moments[2 * step + 2] = inner_product(step + 1, step + 1)

    row8 = lax.broadcasted_iota(jnp.int32, (8, 128), 0)
    mine = jnp.zeros((8, 128), F32)
    for m in range(8):
        mine = jnp.where(row8 == m, jnp.sum(moments[m], axis=0, keepdims=True), mine)
    part[...] = mine
    x_sends = [remote(part, sums_x.at[off], xs.at[off], xr.at[off], off, 0) for off in range(1, nx)]
    for copy in x_sends:
        copy.start()
    total = mine
    for off in range(1, nx):
        x_sends[off - 1].wait()
        total = total + sums_x[off]
    part2[...] = total
    y_sends = [remote(part2, sums_y.at[off], ys.at[off], yr.at[off], 0, off) for off in range(1, ny)]
    for copy in y_sends:
        copy.start()
    for off in range(1, ny):
        y_sends[off - 1].wait()
        total = total + sums_y[off]
    total = jnp.sum(total, axis=1, keepdims=True)
    g = [total[m : m + 1, 0:1] for m in range(8)]

    nu = [g[0], g[1]]
    for m in range(2, 8):
        nu.append(g[m] + g[m] - nu[m % 2])
    gram = {}
    for i in range(ITERS):
        for j in range(ITERS + 1):
            gram[i, j] = 0.5 * (nu[i + j] + nu[abs(i - j)]) if i and j else nu[i + j]

    def dot(a, b):
        terms = []
        for i, first_c in enumerate(a):
            inside = None
            for j, second_c in enumerate(b):
                term = gram[min(i, j), max(i, j)] * second_c
                inside = term if inside is None else inside + term
            terms.append(first_c * inside)
        return functools.reduce(lambda p, q: p + q, terms)

    one = jnp.ones((1, 1), F32)
    zero = jnp.zeros((1, 1), F32)
    z, direction, x = [one], [one], [zero] * ITERS
    norm = dot(z, z)
    for step in range(ITERS):
        image = [(1.0 - CENTRE) * v for v in direction] + [zero]
        for i, v in enumerate(direction):
            if i == 0:
                image[1] = image[1] - HALF * v
            else:
                image[i + 1] = image[i + 1] - (0.5 * HALF) * v
                image[i - 1] = image[i - 1] - (0.5 * HALF) * v
        alpha = norm / dot(direction, image)
        for i, v in enumerate(direction):
            x[i] = x[i] + alpha * v
        z = [v - alpha * w for v, w in zip(z + [zero], image)]
        if step < ITERS - 1:
            following = dot(z, z)
            ratio = following / norm
            direction = [v + ratio * w for v, w in zip(z, direction + [zero])]
            norm = following

    for r in range(STRIPS):
        y = [basis[i, strip(r), 0:COLS] for i in range(ITERS + 1)]
        answer = sum(x[i] * y[i] for i in range(ITERS))
        left = diag[strip(r), 0:COLS] * sum(z[i] * y[i] for i in range(ITERS + 1))
        c1[strip(r), 0:COLS] = answer
        ae[strip(r), 0:COLS] = left
    blocks = COLS // BS
    order = sorted(range(nx), key=lambda off: -min(off, nx - off))
    place = pl.ds(pl.multiple_of(mx * BS, BS), BS)
    d_sends = []
    for off in order:
        target = lax.rem(mx + off, nx)
        for f, field in enumerate((c1, ae)):
            chosen = jnp.zeros((ROWS, BS), F32)
            for m in range(blocks):
                chosen = jnp.where(dest[0, m] == target, field[0:ROWS, m * BS : (m + 1) * BS], chosen)
            stage[off, f] = chosen
        if off:
            copy = remote(stage.at[off], barotropic.at[:, :, place], ds.at[off], dr.at[off], off, 0)
        else:
            copy = pltpu.make_async_copy(stage.at[0], barotropic.at[:, :, place], ds.at[0])
        copy.start()
        d_sends.append(copy)
    for copy in d_sends:
        copy.wait()
    for k in range(levels):
        pltpu.make_async_copy(c2.at[k], tracer_out.at[k], out_sem.at[k]).wait()


def on_device(tracer, u_east, v_north, kmt, dest, dz, wind):
    nx, ny = lax.axis_size("bx"), lax.axis_size("by")
    levels = tracer.shape[0]
    ext3 = pltpu.VMEM((levels, XR, XC), F32)
    ext = pltpu.VMEM((XR, XC), F32)
    ext_i = pltpu.VMEM((XR, XC), jnp.int32)
    flat = pltpu.VMEM((ROWS, COLS), F32)

    def rims(dtype):
        return [
            pltpu.VMEM((2, 8, COLS), dtype),
            pltpu.VMEM((2, ROWS, 128), dtype),
            pltpu.VMEM((4, 8, 128), dtype),
        ]

    scratch = [ext3, ext3, ext3, ext_i, ext_i, ext_i, flat, ext, ext, ext, ext, ext]
    scratch += [pltpu.VMEM((levels, ROWS, COLS), F32), flat, ext, ext, ext]
    scratch += [pltpu.VMEM((ITERS + 1, XR, XC), F32), pltpu.VMEM((8, 128), F32)]
    scratch += rims(F32) + rims(jnp.int32)
    scratch += [
        pltpu.VMEM((5, levels, COLS), F32),
        pltpu.VMEM((4, levels, COLS), F32),
        pltpu.VMEM((2, ROWS, 128), F32),
        pltpu.VMEM((5, levels, COLS), F32),
        pltpu.VMEM((4, levels, COLS), F32),
        pltpu.VMEM((2, ROWS, 128), F32),
        pltpu.VMEM((3, levels, 128), F32),
        pltpu.VMEM((2, levels, 128), F32),
        pltpu.VMEM((2, levels, 128), F32),
        pltpu.VMEM((1, levels, 128), F32),
        pltpu.VMEM((8, 128), F32),
        pltpu.VMEM((nx, 8, 128), F32),
        pltpu.VMEM((8, 128), F32),
        pltpu.VMEM((ny, 8, 128), F32),
        pltpu.VMEM((nx, 2, ROWS, BS), F32),
    ]
    counts = [5, levels] + [8] * 6 + [nx, nx, ny, ny, nx, nx]
    scratch += [pltpu.SemaphoreType.DMA((n,)) for n in counts]
    anywhere = pl.BlockSpec(memory_space=pl.ANY)
    scalars = pl.BlockSpec(memory_space=pltpu.SMEM)
    return pl.pallas_call(
        functools.partial(kernel, nx, ny, levels),
        out_shape=(
            jax.ShapeDtypeStruct(tracer.shape, F32),
            jax.ShapeDtypeStruct((2, ROWS, nx * BS), F32),
        ),
        in_specs=[anywhere] * 4 + [scalars] * 2 + [anywhere],
        out_specs=(anywhere, anywhere),
        scratch_shapes=scratch,
        compiler_params=pltpu.CompilerParams(
            collective_id=0, has_side_effects=True, vmem_limit_bytes=48 * 1024 * 1024
        ),
    )(tracer, u_east, v_north, kmt, dest, dz, wind)


def solution(mesh):
    in_specs = (
        P(None, "by", "bx"),
        P(None, "by", "bx"),
        P(None, "by", "bx"),
        P("by", "bx"),
        P("by", "bx"),
        P(),
        P("by", "bx"),
    )
    out_specs = (P(None, "by", "bx"), P(None, "by", "bx"))
    return jax.shard_map(
        on_device, mesh=mesh, in_specs=in_specs, out_specs=out_specs, check_vma=False
    )
```

```python
import functools

import jax
import jax.numpy as jnp
from jax import lax
from jax.experimental import pallas as pl
from jax.experimental.pallas import tpu as pltpu
from jax.sharding import PartitionSpec as P

BS = 128
ITERS = 4
KAPPA = 0.12
SIGMA = 0.2
CENTRE = 1.0 / 3.0
HALF = 2.0 / 3.0
MESH = pl.DeviceIdType.MESH
ROWS = 64
COLS = 512
XR = ROWS + 8
XC = COLS + 128
STRIPS = ROWS // 8
F32 = jnp.float32
SIDES = ((0, 1), (0, -1), (1, 0), (-1, 0), (1, 1), (-1, 1), (1, -1), (-1, -1))


def strip(r):
    return pl.ds(8 * r, 8)


def rim(ref, side):
    dx, dy = SIDES[side]
    rows = {1: pl.ds(ROWS - 8, 8), -1: pl.ds(0, 8), 0: pl.ds(0, ROWS)}[dy]
    cols = {1: pl.ds(COLS - 128, 128), -1: pl.ds(0, 128), 0: pl.ds(0, COLS)}[dx]
    return ref.at[rows, cols]


def extend(ext, rims):
    from_s, from_n, from_w, from_e, from_sw, from_se, from_nw, from_ne = rims
    low = lax.broadcasted_iota(jnp.int32, (8, COLS), 0) < 4
    ext[ROWS:XR, 0:COLS] = jnp.where(low, from_n[...], from_s[...])
    east = lax.broadcasted_iota(jnp.int32, (ROWS, 128), 1) < 64
    ext[0:ROWS, COLS:XC] = jnp.where(east, from_e[...], from_w[...])
    east8 = lax.broadcasted_iota(jnp.int32, (8, 128), 1) < 64
    low8 = lax.broadcasted_iota(jnp.int32, (8, 128), 0) < 4
    ext[ROWS:XR, COLS:XC] = jnp.where(
        low8,
        jnp.where(east8, from_ne[...], from_nw[...]),
        jnp.where(east8, from_se[...], from_sw[...]),
    )


def spread_rows(get, count):
    sub = lax.broadcasted_iota(jnp.int32, (8, XC), 0)
    x = [get(r) for r in range(count)]
    up = [pltpu.roll(v, 7, 0) for v in x]
    down = [pltpu.roll(v, 1, 0) for v in x]
    out = []
    for r in range(count):
        north = jnp.where(sub == 7, up[(r + 1) % count], up[r])
        south = jnp.where(sub == 0, down[(r - 1) % count], down[r])
        out.append(x[r] + x[r] + (north + south))
    return out


def spread_cols(v):
    return v + v + (pltpu.roll(v, 1, 1) + pltpu.roll(v, XC - 1, 1))


def kernel(
    nx,
    ny,
    levels,
    tracer,
    u_east,
    v_north,
    kmt,
    dest_in,
    dz_in,
    wind,
    tracer_out,
    barotropic,
    c0,
    u0,
    v0,
    c1,
    c2,
    k_x,
    ke,
    kn,
    rhs,
    ae,
    be,
    an,
    bn,
    depth,
    inv,
    diag,
    basis,
    answer,
    left,
    dest,
    dz,
    zrim_row,
    zrim_col,
    zrim_corner,
    krim_row,
    krim_col,
    krim_corner,
    up_send,
    dn_send,
    col_send,
    up_recv,
    dn_recv,
    col_recv,
    rows1,
    rows1_recv,
    cols1,
    cols1_recv,
    row_flux,
    part,
    sums_x,
    part2,
    sums_y,
    stage,
    load_sem,
    out_sem,
    ks,
    kr,
    rs,
    rr,
    zs,
    zr,
    xs,
    xr,
    ys,
    yr,
    ds,
    dr,
):
    mx = lax.axis_index("bx")
    my = lax.axis_index("by")
    pending = []

    def peer(dx, dy):
        return (lax.rem(mx + dx + nx, nx), lax.rem(my + dy + ny, ny))

    def send(src, dst, send_sem, recv_sem, dx, dy):
        copy = pltpu.make_async_remote_copy(
            src_ref=src, dst_ref=dst, send_sem=send_sem, recv_sem=recv_sem, device_id=peer(dx, dy), device_id_type=MESH
        )
        copy.start()
        pending.append(copy)
        return copy

    loads = [
        pltpu.make_async_copy(kmt, k_x.at[pl.ds(0, ROWS), pl.ds(0, COLS)], load_sem.at[0]),
        pltpu.make_async_copy(dest_in, dest, load_sem.at[1]),
        pltpu.make_async_copy(dz_in, dz, load_sem.at[2]),
        pltpu.make_async_copy(tracer, c0, load_sem.at[3]),
        pltpu.make_async_copy(u_east, u0, load_sem.at[4]),
        pltpu.make_async_copy(v_north, v0, load_sem.at[5]),
        pltpu.make_async_copy(wind, rhs, load_sem.at[6]),
    ]
    for copy in loads:
        copy.start()

    barrier = pltpu.get_barrier_semaphore()
    peers = [peer(dx, dy) for dx, dy in SIDES]
    peers += [peer(off, 0) for off in range(2, nx - 1)]
    peers += [peer(0, off) for off in range(2, ny - 1)]
    for target in peers:
        pl.semaphore_signal(barrier, inc=1, device_id=target, device_id_type=MESH)

    loads[0].wait()
    sub = lax.broadcasted_iota(jnp.int32, (8, COLS), 0)
    lane_row = lax.broadcasted_iota(jnp.int32, (8, COLS), 1)
    k_up = [pltpu.roll(k_x[strip(r), 0:COLS], 7, 0) for r in range(STRIPS)]
    for r in range(STRIPS):
        here = k_x[strip(r), 0:COLS]
        east = jnp.where(lane_row == COLS - 1, 0, pltpu.roll(here, COLS - 1, 1))
        north = jnp.where(sub == 7, k_up[r + 1] if r + 1 < STRIPS else 0, k_up[r])
        ke[strip(r), :] = jnp.minimum(here, east)
        kn[strip(r), :] = jnp.minimum(here, north)
    for copy in loads[1:]:
        copy.wait()

    lane = lax.broadcasted_iota(jnp.int32, (ROWS, 128), 1)
    west = lane < 64
    group = ((lane + 4) & 127) >> 3
    slot = ((lane + 4) & 7) - 4

    def ends(field, k):
        return jnp.where(west, field[k, :, 0:128], field[k, :, COLS - 128 : COLS])

    def turned(value, lanes):
        return pltpu.roll(value, lanes % 128, 1) if lanes % 128 else value

    packed = jnp.zeros((ROWS, 128), F32)
    for k in range(levels):
        up_send[0, k : k + 1, :] = c0[k, ROWS - 1 : ROWS, :]
        up_send[1, k : k + 1, :] = v0[k, ROWS - 1 : ROWS, :]
        dn_send[k : k + 1, :] = c0[k, 0:1, :]
        both = jnp.where(slot == -2, turned(u0[k, :, COLS - 128 : COLS], 8 * k - 1), turned(ends(c0, k), 8 * k))
        packed = jnp.where(group == k, both, packed)
    col_send[...] = packed
    pl.semaphore_wait(barrier, len(peers))
    from_s = send(up_send, up_recv, rs.at[0], rr.at[0], 0, 1)
    from_n = send(dn_send, dn_recv, rs.at[1], rr.at[1], 0, -1)
    from_w = send(col_send, col_recv.at[0], rs.at[2], rr.at[2], 1, 0)
    from_e = send(col_send, col_recv.at[1], rs.at[3], rr.at[3], -1, 0)

    def rim_refs(row, col, corner):
        return [row.at[0], row.at[1], col.at[0], col.at[1]] + [corner.at[i] for i in range(4)]

    k_rims = rim_refs(krim_row, krim_col, krim_corner)
    k_sends = [send(rim(kmt, s), k_rims[s], ks.at[s], kr.at[s], *SIDES[s]) for s in range(8)]

    def advance(get, k, put):
        def north_flux(r, c, up, nxt):
            return an[k, strip(r), :] * c + bn[k, strip(r), :] * jnp.where(sub == 7, nxt, up)

        below = jnp.zeros((8, COLS), F32)
        c, up = get(0), pltpu.roll(get(0), 7, 0)
        for r in range(STRIPS):
            if r + 1 < STRIPS:
                c_next = get(r + 1)
                up_next = pltpu.roll(c_next, 7, 0)
            flux = north_flux(r, c, up, up_next)
            down = pltpu.roll(flux, 1, 0)
            flux_e = ae[k, strip(r), :] * c + be[k, strip(r), :] * pltpu.roll(c, COLS - 1, 1)
            spread = flux_e - pltpu.roll(flux_e, 1, 1)
            spread = spread + (flux - jnp.where(sub == 0, below, down))
            put(r, c - spread)
            below, c, up = down, c_next, up_next

    def first_step(k, carry):
        for r in range(STRIPS):
            half_u, half_v = 0.5 * u0[k, strip(r), :], 0.5 * v0[k, strip(r), :]
            wet_e, wet_n = ke[strip(r), :] > k, kn[strip(r), :] > k
            ae[k, strip(r), :] = jnp.where(wet_e, half_u + KAPPA, 0.0)
            be[k, strip(r), :] = jnp.where(wet_e, half_u - KAPPA, 0.0)
            an[k, strip(r), :] = jnp.where(wet_n, half_v + KAPPA, 0.0)
            bn[k, strip(r), :] = jnp.where(wet_n, half_v - KAPPA, 0.0)

        def put(r, value):
            c1[k, strip(r), :] = value

        advance(lambda r: c0[k, strip(r), :], k, put)
        return carry

    lax.fori_loop(0, levels, first_step, 0)

    for copy in k_sends:
        copy.wait_recv()
    extend(k_x, k_rims)
    level16 = lax.broadcasted_iota(jnp.int32, (levels, COLS), 0)
    wet_n = jnp.minimum(k_x[ROWS - 1 : ROWS, 0:COLS], k_x[ROWS : ROWS + 1, 0:COLS]) > level16
    wet_s = jnp.minimum(k_x[0:1, 0:COLS], k_x[XR - 1 : XR, 0:COLS]) > level16
    wet_e = jnp.minimum(k_x[0:ROWS, COLS - 1 : COLS], k_x[0:ROWS, COLS : COLS + 1]) > group
    wet_w = jnp.minimum(k_x[0:ROWS, 0:1], k_x[0:ROWS, XC - 1 : XC]) > group

    def face(velocity, here, there, wet):
        half = 0.5 * velocity
        return jnp.where(wet, (half + KAPPA) * here + (half - KAPPA) * there, 0.0)

    def rim_rows(north_row, south_row, own_north, own_south):
        row_flux[0] = face(up_send[1], own_north, north_row, wet_n)
        row_flux[1] = face(up_recv[1], south_row, own_south, wet_s)

    def rim_cols(own, westward, eastward):
        out = face(turned(col_send[...], 1), own, turned(eastward, -1), wet_e)
        into = face(turned(col_recv[0], 2), turned(westward, 1), own, wet_w)
        return jnp.where(slot == -1, -out, jnp.where(slot == 0, into, 0.0))

    for copy in (from_s, from_n, from_w, from_e):
        copy.wait_recv()
    rim_rows(dn_recv[...], up_recv[0], up_send[0], dn_send[...])
    flux_cols = rim_cols(col_send[...], col_recv[0], col_recv[1])

    def correct(field, k, flux):
        change = turned(flux, -8 * k)
        field[k, :, 0:128] = field[k, :, 0:128] + jnp.where(lane == 0, change, 0.0)
        field[k, :, COLS - 128 : COLS] = field[k, :, COLS - 128 : COLS] + jnp.where(lane == 127, change, 0.0)
        field[k, 0:1, :] = field[k, 0:1, :] + row_flux[1, k : k + 1, :]
        field[k, ROWS - 1 : ROWS, :] = field[k, ROWS - 1 : ROWS, :] - row_flux[0, k : k + 1, :]

    packed = jnp.zeros((ROWS, 128), F32)
    for k in range(levels):
        correct(c1, k, flux_cols)
        rows1[0, k : k + 1, :] = c1[k, ROWS - 1 : ROWS, :]
        rows1[1, k : k + 1, :] = c1[k, 0:1, :]
        packed = jnp.where(group == k, turned(ends(c1, k), 8 * k), packed)
    cols1[...] = packed
    from_s = send(rows1.at[0], rows1_recv.at[0], rs.at[4], rr.at[4], 0, 1)
    from_n = send(rows1.at[1], rows1_recv.at[1], rs.at[5], rr.at[5], 0, -1)
    from_w = send(cols1, cols1_recv.at[0], rs.at[6], rr.at[6], 1, 0)
    from_e = send(cols1, cols1_recv.at[1], rs.at[7], rr.at[7], -1, 0)

    def second_step(k, carry):
        def put(r, value):
            c2[k, strip(r), :] = value
            wet = k_x[strip(r), 0:COLS] > k
            rhs[strip(r), :] = rhs[strip(r), :] + jnp.where(wet, dz[k] * value, 0.0)

        advance(lambda r: c1[k, strip(r), :], k, put)
        return carry

    lax.fori_loop(0, levels, second_step, 0)

    subx = lax.broadcasted_iota(jnp.int32, (8, XC), 0)
    for r in range(STRIPS + 1):
        here = k_x[strip(r), :]
        total = jnp.zeros((8, XC), F32)
        for k in range(levels):
            total = total + jnp.where(here > k, dz[k], 0.0)
        depth[strip(r), :] = total

    def ocean_of(r):
        return jnp.where(k_x[strip(r), :] > 0, 1.0, 0.0).astype(F32)

    rows_o = spread_rows(ocean_of, STRIPS + 1)
    rows_d = spread_rows(lambda r: depth[strip(r), :], STRIPS + 1)
    for r in range(STRIPS + 1):
        d = depth[strip(r), :]
        o = ocean_of(r)
        total = d * spread_cols(rows_o[r]) + spread_cols(rows_d[r]) - 8.0 * d
        full = SIGMA + 0.25 * o * total
        diag[strip(r), :] = full
        inv[strip(r), :] = o / full

    for copy in (from_s, from_n, from_w, from_e):
        copy.wait_recv()
    rim_rows(rows1_recv[1], rows1_recv[0], rows1[0], rows1[1])
    flux_cols = rim_cols(cols1[...], cols1_recv[0], cols1_recv[1])
    dz_rows = jnp.zeros((levels, 128), F32)
    dz_cols = jnp.zeros((ROWS, 128), F32)
    for k in range(levels):
        dz_rows = jnp.where(level16[:, 0:128] == k, dz[k], dz_rows)
        dz_cols = jnp.where(group == k, dz[k], dz_cols)
    dz_rows = jnp.concatenate([dz_rows] * (COLS // 128), axis=1)
    weighted = dz_cols * flux_cols
    change_w = jnp.sum(jnp.where(slot == 0, weighted, 0.0), axis=1, keepdims=True)
    change_e = jnp.sum(jnp.where(slot == -1, weighted, 0.0), axis=1, keepdims=True)
    rhs[:, 0:128] = rhs[:, 0:128] + jnp.where(lane == 0, change_w, 0.0)
    rhs[:, COLS - 128 : COLS] = rhs[:, COLS - 128 : COLS] + jnp.where(lane == 127, change_e, 0.0)
    rhs[0:1, :] = rhs[0:1, :] + jnp.sum(dz_rows * row_flux[1], axis=0, keepdims=True)
    rhs[ROWS - 1 : ROWS, :] = rhs[ROWS - 1 : ROWS, :] - jnp.sum(dz_rows * row_flux[0], axis=0, keepdims=True)

    for r in range(STRIPS):
        start = jnp.where(k_x[strip(r), 0:COLS] > 0, rhs[strip(r), :], 0.0)
        basis[0, strip(r), 0:COLS] = start * inv[strip(r), 0:COLS]
    z_rims = rim_refs(zrim_row, zrim_col, zrim_corner)
    z_sends = [send(rim(basis.at[0], s), z_rims[s], zs.at[s], zr.at[s], *SIDES[s]) for s in range(8)]
    for k in range(levels):
        correct(c2, k, flux_cols)
    write = pltpu.make_async_copy(c2, tracer_out, out_sem)
    write.start()
    for copy in z_sends:
        copy.wait_recv()
    extend(basis.at[0], z_rims)

    moments = [jnp.zeros((8, 128), F32) for _ in range(8)]

    def inner_product(i, j):
        total = jnp.zeros((8, 128), F32)
        for r in range(STRIPS):
            product = diag[strip(r), 0:COLS] * basis[i, strip(r), 0:COLS] * basis[j, strip(r), 0:COLS]
            for m in range(COLS // 128):
                total = total + product[:, 128 * m : 128 * (m + 1)]
        return total

    moments[0] = inner_product(0, 0)
    for step in range(ITERS):
        rows_x = spread_rows(lambda r: basis[step, strip(r), :], STRIPS + 1)
        rows_dx = spread_rows(lambda r: depth[strip(r), :] * basis[step, strip(r), :], STRIPS + 1)
        for r in range(STRIPS + 1):
            d, x = depth[strip(r), :], basis[step, strip(r), :]
            image = d * spread_cols(rows_x[r]) + spread_cols(rows_dx[r]) - 8.0 * (d * x)
            scale = (0.25 / HALF) * inv[strip(r), :]
            following = scale * image - (CENTRE / HALF) * x
            if step:
                following = following + following - basis[step - 1, strip(r), :]
            basis[step + 1, strip(r), :] = following
        moments[2 * step + 1] = inner_product(step, step + 1)
        if step < ITERS - 1:
            moments[2 * step + 2] = inner_product(step + 1, step + 1)

    row8 = lax.broadcasted_iota(jnp.int32, (8, 128), 0)
    mine = jnp.zeros((8, 128), F32)
    for m in range(8):
        mine = jnp.where(row8 == m, jnp.sum(moments[m], axis=0, keepdims=True), mine)
    part[...] = mine
    x_sends = [send(part, sums_x.at[off], xs.at[off], xr.at[off], off, 0) for off in range(1, nx)]
    total = mine
    for off in range(1, nx):
        x_sends[off - 1].wait_recv()
        total = total + sums_x[off]
    part2[...] = total
    y_sends = [send(part2, sums_y.at[off], ys.at[off], yr.at[off], 0, off) for off in range(1, ny)]
    for off in range(1, ny):
        y_sends[off - 1].wait_recv()
        total = total + sums_y[off]
    total = jnp.sum(total, axis=1, keepdims=True)
    g = [total[m : m + 1, 0:1] for m in range(8)]

    nu = [g[0], g[1]]
    for m in range(2, 8):
        nu.append(g[m] + g[m] - nu[m % 2])
    gram = {}
    for i in range(ITERS):
        for j in range(ITERS + 1):
            gram[i, j] = 0.5 * (nu[i + j] + nu[abs(i - j)]) if i and j else nu[i + j]

    def dot(a, b):
        terms = []
        for i, first_c in enumerate(a):
            inside = None
            for j, second_c in enumerate(b):
                term = gram[min(i, j), max(i, j)] * second_c
                inside = term if inside is None else inside + term
            terms.append(first_c * inside)
        return functools.reduce(lambda p, q: p + q, terms)

    one = jnp.ones((1, 1), F32)
    zero = jnp.zeros((1, 1), F32)
    z, direction, x = [one], [one], [zero] * ITERS
    norm = dot(z, z)
    for step in range(ITERS):
        image = [(1.0 - CENTRE) * v for v in direction] + [zero]
        for i, v in enumerate(direction):
            if i == 0:
                image[1] = image[1] - HALF * v
            else:
                image[i + 1] = image[i + 1] - (0.5 * HALF) * v
                image[i - 1] = image[i - 1] - (0.5 * HALF) * v
        alpha = norm / dot(direction, image)
        for i, v in enumerate(direction):
            x[i] = x[i] + alpha * v
        z = [v - alpha * w for v, w in zip(z + [zero], image)]
        if step < ITERS - 1:
            following = dot(z, z)
            ratio = following / norm
            direction = [v + ratio * w for v, w in zip(z, direction + [zero])]
            norm = following

    for r in range(STRIPS):
        y = [basis[i, strip(r), 0:COLS] for i in range(ITERS + 1)]
        answer[strip(r), :] = sum(x[i] * y[i] for i in range(ITERS))
        left[strip(r), :] = diag[strip(r), 0:COLS] * sum(z[i] * y[i] for i in range(ITERS + 1))
    blocks = COLS // BS
    order = sorted(range(nx), key=lambda off: -min(off, nx - off))
    place = pl.ds(pl.multiple_of(mx * BS, BS), BS)
    d_sends = []
    for off in order:
        target = lax.rem(mx + off, nx)
        for f, field in enumerate((answer, left)):
            chosen = jnp.zeros((ROWS, BS), F32)
            for m in range(blocks):
                chosen = jnp.where(dest[0, m] == target, field[0:ROWS, m * BS : (m + 1) * BS], chosen)
            stage[off, f] = chosen
        if off:
            d_sends.append(send(stage.at[off], barotropic.at[:, :, place], ds.at[off], dr.at[off], off, 0))
        else:
            own = pltpu.make_async_copy(stage.at[0], barotropic.at[:, :, place], ds.at[0])
            own.start()
    for copy in d_sends:
        copy.wait_recv()
    own.wait()
    write.wait()
    for copy in pending:
        copy.wait_send()


def on_device(tracer, u_east, v_north, kmt, dest, dz, wind):
    nx, ny = lax.axis_size("bx"), lax.axis_size("by")
    levels = tracer.shape[0]
    slab = pltpu.VMEM((levels, ROWS, COLS), F32)
    ext = pltpu.VMEM((XR, XC), F32)
    flat = pltpu.VMEM((ROWS, COLS), F32)
    flat_i = pltpu.VMEM((ROWS, COLS), jnp.int32)
    rows = pltpu.VMEM((levels, COLS), F32)
    rows2 = pltpu.VMEM((2, levels, COLS), F32)
    cols = pltpu.VMEM((ROWS, 128), F32)
    cols2 = pltpu.VMEM((2, ROWS, 128), F32)

    def rims(dtype):
        return [
            pltpu.VMEM((2, 8, COLS), dtype),
            pltpu.VMEM((2, ROWS, 128), dtype),
            pltpu.VMEM((4, 8, 128), dtype),
        ]

    scratch = [slab] * 5 + [pltpu.VMEM((XR, XC), jnp.int32), flat_i, flat_i, flat] + [slab] * 4
    scratch += [ext, ext, ext, pltpu.VMEM((ITERS + 1, XR, XC), F32), flat, flat]
    scratch += [pltpu.SMEM(dest.shape, jnp.int32), pltpu.SMEM(dz.shape, F32)]
    scratch += rims(F32) + rims(jnp.int32)
    scratch += [rows2, rows, cols, rows2, rows, cols2]
    scratch += [rows2, rows2, cols, cols2, rows2]
    scratch += [
        pltpu.VMEM((8, 128), F32),
        pltpu.VMEM((nx, 8, 128), F32),
        pltpu.VMEM((8, 128), F32),
        pltpu.VMEM((ny, 8, 128), F32),
        pltpu.VMEM((nx, 2, ROWS, BS), F32),
    ]
    counts = [7, None] + [8] * 6 + [nx, nx, ny, ny, nx, nx]
    scratch += [pltpu.SemaphoreType.DMA((n,)) if n else pltpu.SemaphoreType.DMA for n in counts]
    anywhere = pl.BlockSpec(memory_space=pl.ANY)
    hbm = pl.BlockSpec(memory_space=pltpu.HBM)
    return pl.pallas_call(
        functools.partial(kernel, nx, ny, levels),
        out_shape=(
            jax.ShapeDtypeStruct(tracer.shape, F32),
            jax.ShapeDtypeStruct((2, ROWS, nx * BS), F32),
        ),
        in_specs=[hbm] * 7,
        out_specs=(anywhere, anywhere),
        scratch_shapes=scratch,
        compiler_params=pltpu.CompilerParams(
            collective_id=0, has_side_effects=True, vmem_limit_bytes=32 * 1024 * 1024
        ),
    )(*[pltpu.with_memory_space_constraint(x, pltpu.HBM) for x in (tracer, u_east, v_north, kmt, dest, dz, wind)])


def solution(mesh):
    in_specs = (
        P(None, "by", "bx"),
        P(None, "by", "bx"),
        P(None, "by", "bx"),
        P("by", "bx"),
        P("by", "bx"),
        P(),
        P("by", "bx"),
    )
    out_specs = (P(None, "by", "bx"), P(None, "by", "bx"))
    return jax.shard_map(
        on_device, mesh=mesh, in_specs=in_specs, out_specs=out_specs, check_vma=False
    )
```

```python
import functools

import jax
import jax.numpy as jnp
from jax import lax
from jax.experimental import pallas as pl
from jax.experimental.pallas import tpu as pltpu
from jax.sharding import PartitionSpec as P

BS = 128
ITERS = 4
KAPPA = 0.12
SIGMA = 0.2
CENTRE = 1.0 / 3.0
HALF = 2.0 / 3.0
MESH = pl.DeviceIdType.MESH
ROWS = 64
COLS = 512
XR = ROWS + 8
XC = COLS + 128
STRIPS = ROWS // 8
F32 = jnp.float32
SIDES = ((0, 1), (0, -1), (1, 0), (-1, 0), (1, 1), (-1, 1), (1, -1), (-1, -1))


def strip(r):
    return pl.ds(8 * r, 8)


def rim(ref, side):
    dx, dy = SIDES[side]
    rows = {1: pl.ds(ROWS - 8, 8), -1: pl.ds(0, 8), 0: pl.ds(0, ROWS)}[dy]
    cols = {1: pl.ds(COLS - 128, 128), -1: pl.ds(0, 128), 0: pl.ds(0, COLS)}[dx]
    return ref.at[rows, cols]


def extend(ext, rims):
    from_s, from_n, from_w, from_e, from_sw, from_se, from_nw, from_ne = rims
    low = lax.broadcasted_iota(jnp.int32, (8, COLS), 0) < 4
    ext[ROWS:XR, 0:COLS] = jnp.where(low, from_n[...], from_s[...])
    east = lax.broadcasted_iota(jnp.int32, (ROWS, 128), 1) < 64
    ext[0:ROWS, COLS:XC] = jnp.where(east, from_e[...], from_w[...])
    east8 = lax.broadcasted_iota(jnp.int32, (8, 128), 1) < 64
    low8 = lax.broadcasted_iota(jnp.int32, (8, 128), 0) < 4
    ext[ROWS:XR, COLS:XC] = jnp.where(
        low8,
        jnp.where(east8, from_ne[...], from_nw[...]),
        jnp.where(east8, from_se[...], from_sw[...]),
    )


def spread_rows(get, count, inner=False):
    x = [get(r) for r in range(count)]
    sub = lax.broadcasted_iota(jnp.int32, x[0].shape, 0)
    up = [pltpu.roll(v, 7, 0) for v in x]
    down = [pltpu.roll(v, 1, 0) for v in x]
    out, within = [], []
    for r in range(count):
        north = jnp.where(sub == 7, up[(r + 1) % count], up[r])
        south = jnp.where(sub == 0, down[(r - 1) % count], down[r])
        out.append(x[r] + x[r] + (north + south))
        if r == 0:
            south = jnp.where(sub == 0, 0.0, down[r])
        if r == count - 2:
            north = jnp.where(sub == 7, 0.0, up[r])
        within.append(x[r] + x[r] + (north + south) if r in (0, count - 2) else out[r])
    return (out, within) if inner else out


def spread_cols(v):
    return v + v + (pltpu.roll(v, 1, 1) + pltpu.roll(v, XC - 1, 1))


def kernel(
    nx,
    ny,
    levels,
    tracer,
    u_east,
    v_north,
    kmt,
    dest_in,
    dz_in,
    wind,
    tracer_out,
    barotropic,
    c0,
    u0,
    v0,
    c1,
    c2,
    k_x,
    ke,
    kn,
    rhs,
    ae,
    be,
    an,
    bn,
    depth,
    inv,
    diag,
    basis,
    dest,
    dz,
    zrim_row,
    zrim_col,
    zrim_corner,
    krim_row,
    krim_col,
    krim_corner,
    up_send,
    dn_send,
    col_send,
    up_recv,
    dn_recv,
    col_recv,
    rows1,
    rows1_recv,
    cols1,
    cols1_recv,
    row_flux,
    part,
    sums_x,
    part2,
    sums_y,
    still_out,
    still,
    first_out,
    slots,
    edge_rows,
    edges_out,
    edges,
    full,
    stage,
    load_sem,
    out_sem,
    ks,
    kr,
    rs,
    rr,
    zs,
    zr,
    xs,
    xr,
    ys,
    yr,
    ds,
    dr,
    fs,
    fr,
    es,
    er,
    last_sem,
):
    mx = lax.axis_index("bx")
    my = lax.axis_index("by")
    pending = []

    def peer(dx, dy):
        return (lax.rem(mx + dx + nx, nx), lax.rem(my + dy + ny, ny))

    def send(src, dst, send_sem, recv_sem, dx, dy):
        copy = pltpu.make_async_remote_copy(
            src_ref=src, dst_ref=dst, send_sem=send_sem, recv_sem=recv_sem, device_id=peer(dx, dy), device_id_type=MESH
        )
        copy.start()
        pending.append(copy)
        return copy

    last_cols = (slice(None), slice(None), pl.ds(COLS - 128, 128))
    other_cols = (slice(None), slice(None), pl.ds(0, COLS - 128))
    last_rows = (slice(None), pl.ds(ROWS - 8, 8))
    other_rows = (slice(None), pl.ds(0, ROWS - 8))
    loads = [
        pltpu.make_async_copy(kmt, k_x.at[pl.ds(0, ROWS), pl.ds(0, COLS)], load_sem.at[0]),
        pltpu.make_async_copy(dest_in, dest, load_sem.at[1]),
        pltpu.make_async_copy(dz_in, dz, load_sem.at[2]),
        pltpu.make_async_copy(tracer, c0, load_sem.at[3]),
        pltpu.make_async_copy(u_east.at[last_cols], u0.at[last_cols], load_sem.at[4]),
        pltpu.make_async_copy(v_north.at[last_rows], v0.at[last_rows], load_sem.at[5]),
        pltpu.make_async_copy(u_east.at[other_cols], u0.at[other_cols], load_sem.at[6]),
        pltpu.make_async_copy(v_north.at[other_rows], v0.at[other_rows], load_sem.at[7]),
        pltpu.make_async_copy(wind, rhs, load_sem.at[8]),
    ]
    for copy in loads:
        copy.start()

    barrier = pltpu.get_barrier_semaphore()
    peers = [peer(dx, dy) for dx, dy in SIDES]
    peers += [peer(off, 0) for off in range(2, nx - 1)]
    peers += [peer(0, off) for off in range(2, ny - 1)]
    for target in peers:
        pl.semaphore_signal(barrier, inc=1, device_id=target, device_id_type=MESH)

    loads[0].wait()
    sub = lax.broadcasted_iota(jnp.int32, (8, COLS), 0)
    lane_row = lax.broadcasted_iota(jnp.int32, (8, COLS), 1)
    k_up = [pltpu.roll(k_x[strip(r), 0:COLS], 7, 0) for r in range(STRIPS)]
    for r in range(STRIPS):
        here = k_x[strip(r), 0:COLS]
        east = jnp.where(lane_row == COLS - 1, 0, pltpu.roll(here, COLS - 1, 1))
        north = jnp.where(sub == 7, k_up[r + 1] if r + 1 < STRIPS else 0, k_up[r])
        ke[strip(r), :] = jnp.minimum(here, east)
        kn[strip(r), :] = jnp.minimum(here, north)
    for copy in loads[1:6]:
        copy.wait()

    lane = lax.broadcasted_iota(jnp.int32, (ROWS, 128), 1)
    west = lane < 64
    group = ((lane + 4) & 127) >> 3
    slot = ((lane + 4) & 7) - 4

    def ends(field, k):
        return jnp.where(west, field[k, :, 0:128], field[k, :, COLS - 128 : COLS])

    def turned(value, lanes):
        return pltpu.roll(value, lanes % 128, 1) if lanes % 128 else value

    packed = jnp.zeros((ROWS, 128), F32)
    for k in range(levels):
        up_send[0, k : k + 1, :] = c0[k, ROWS - 1 : ROWS, :]
        up_send[1, k : k + 1, :] = v0[k, ROWS - 1 : ROWS, :]
        dn_send[k : k + 1, :] = c0[k, 0:1, :]
        both = jnp.where(slot == -2, turned(u0[k, :, COLS - 128 : COLS], 8 * k - 1), turned(ends(c0, k), 8 * k))
        packed = jnp.where(group == k, both, packed)
    col_send[...] = packed
    pl.semaphore_wait(barrier, len(peers))
    from_s = send(up_send, up_recv, rs.at[0], rr.at[0], 0, 1)
    from_n = send(dn_send, dn_recv, rs.at[1], rr.at[1], 0, -1)
    from_w = send(col_send, col_recv.at[0], rs.at[2], rr.at[2], 1, 0)
    from_e = send(col_send, col_recv.at[1], rs.at[3], rr.at[3], -1, 0)

    def rim_refs(row, col, corner):
        return [row.at[0], row.at[1], col.at[0], col.at[1]] + [corner.at[i] for i in range(4)]

    k_rims = rim_refs(krim_row, krim_col, krim_corner)
    k_sends = [send(rim(kmt, s), k_rims[s], ks.at[s], kr.at[s], *SIDES[s]) for s in range(8)]

    def advance(get, k, put):
        def north_flux(r, c, up, nxt):
            return an[k, strip(r), :] * c + bn[k, strip(r), :] * jnp.where(sub == 7, nxt, up)

        below = jnp.zeros((8, COLS), F32)
        c, up = get(0), pltpu.roll(get(0), 7, 0)
        for r in range(STRIPS):
            if r + 1 < STRIPS:
                c_next = get(r + 1)
                up_next = pltpu.roll(c_next, 7, 0)
            flux = north_flux(r, c, up, up_next)
            down = pltpu.roll(flux, 1, 0)
            flux_e = ae[k, strip(r), :] * c + be[k, strip(r), :] * pltpu.roll(c, COLS - 1, 1)
            spread = flux_e - pltpu.roll(flux_e, 1, 1)
            spread = spread + (flux - jnp.where(sub == 0, below, down))
            put(r, c - spread)
            below, c, up = down, c_next, up_next

    def first_step(k, carry):
        for r in range(STRIPS):
            half_u, half_v = 0.5 * u0[k, strip(r), :], 0.5 * v0[k, strip(r), :]
            wet_e, wet_n = ke[strip(r), :] > k, kn[strip(r), :] > k
            ae[k, strip(r), :] = jnp.where(wet_e, half_u + KAPPA, 0.0)
            be[k, strip(r), :] = jnp.where(wet_e, half_u - KAPPA, 0.0)
            an[k, strip(r), :] = jnp.where(wet_n, half_v + KAPPA, 0.0)
            bn[k, strip(r), :] = jnp.where(wet_n, half_v - KAPPA, 0.0)

        def put(r, value):
            c1[k, strip(r), :] = value

        advance(lambda r: c0[k, strip(r), :], k, put)
        return carry

    for copy in loads[6:]:
        copy.wait()
    lax.fori_loop(0, levels, first_step, 0)

    for copy in k_sends:
        copy.wait_recv()
    extend(k_x, k_rims)
    level16 = lax.broadcasted_iota(jnp.int32, (levels, COLS), 0)
    wet_n = jnp.minimum(k_x[ROWS - 1 : ROWS, 0:COLS], k_x[ROWS : ROWS + 1, 0:COLS]) > level16
    wet_s = jnp.minimum(k_x[0:1, 0:COLS], k_x[XR - 1 : XR, 0:COLS]) > level16
    wet_e = jnp.minimum(k_x[0:ROWS, COLS - 1 : COLS], k_x[0:ROWS, COLS : COLS + 1]) > group
    wet_w = jnp.minimum(k_x[0:ROWS, 0:1], k_x[0:ROWS, XC - 1 : XC]) > group

    def face(velocity, here, there, wet):
        half = 0.5 * velocity
        return jnp.where(wet, (half + KAPPA) * here + (half - KAPPA) * there, 0.0)

    def rim_rows(north_row, south_row, own_north, own_south):
        row_flux[0] = face(up_send[1], own_north, north_row, wet_n)
        row_flux[1] = face(up_recv[1], south_row, own_south, wet_s)

    def rim_cols(own, westward, eastward):
        out = face(turned(col_send[...], 1), own, turned(eastward, -1), wet_e)
        into = face(turned(col_recv[0], 2), turned(westward, 1), own, wet_w)
        return jnp.where(slot == -1, -out, jnp.where(slot == 0, into, 0.0))

    for copy in (from_s, from_n, from_w, from_e):
        copy.wait_recv()
    rim_rows(dn_recv[...], up_recv[0], up_send[0], dn_send[...])
    flux_cols = rim_cols(col_send[...], col_recv[0], col_recv[1])

    def correct(field, k, flux):
        change = turned(flux, -8 * k)
        field[k, :, 0:128] = field[k, :, 0:128] + jnp.where(lane == 0, change, 0.0)
        field[k, :, COLS - 128 : COLS] = field[k, :, COLS - 128 : COLS] + jnp.where(lane == 127, change, 0.0)
        field[k, 0:1, :] = field[k, 0:1, :] + row_flux[1, k : k + 1, :]
        field[k, ROWS - 1 : ROWS, :] = field[k, ROWS - 1 : ROWS, :] - row_flux[0, k : k + 1, :]

    packed = jnp.zeros((ROWS, 128), F32)
    for k in range(levels):
        correct(c1, k, flux_cols)
        rows1[0, k : k + 1, :] = c1[k, ROWS - 1 : ROWS, :]
        rows1[1, k : k + 1, :] = c1[k, 0:1, :]
        packed = jnp.where(group == k, turned(ends(c1, k), 8 * k), packed)
    cols1[...] = packed
    from_s = send(rows1.at[0], rows1_recv.at[0], rs.at[4], rr.at[4], 0, 1)
    from_n = send(rows1.at[1], rows1_recv.at[1], rs.at[5], rr.at[5], 0, -1)
    from_w = send(cols1, cols1_recv.at[0], rs.at[6], rr.at[6], 1, 0)
    from_e = send(cols1, cols1_recv.at[1], rs.at[7], rr.at[7], -1, 0)

    subx = lax.broadcasted_iota(jnp.int32, (8, XC), 0)
    for r in range(STRIPS + 1):
        here = k_x[strip(r), :]
        total = jnp.zeros((8, XC), F32)
        for k in range(levels):
            total = total + jnp.where(here > k, dz[k], 0.0)
        depth[strip(r), :] = total

    def ocean_of(r):
        return jnp.where(k_x[strip(r), :] > 0, 1.0, 0.0).astype(F32)

    rows_o = spread_rows(ocean_of, STRIPS + 1)
    rows_d = spread_rows(lambda r: depth[strip(r), :], STRIPS + 1)
    for r in range(STRIPS + 1):
        d = depth[strip(r), :]
        o = ocean_of(r)
        total = d * spread_cols(rows_o[r]) + spread_cols(rows_d[r]) - 8.0 * d
        whole = SIGMA + 0.25 * o * total
        diag[strip(r), :] = whole
        inv[strip(r), :] = o / whole

    blocks = COLS // BS

    def scatter(get, parts, outbox, inbox, ssem, rsem):
        copies = []
        for off in sorted(range(nx), key=lambda o: -min(o, nx - o)):
            target = lax.rem(mx + off, nx)
            hits = [dest[0, m] == target for m in range(blocks)]
            here = outbox.at[off] if off else inbox(0)
            for i in range(parts):
                chosen = None
                for m in range(blocks):
                    piece = get(m, i)
                    chosen = jnp.where(hits[m], piece, jnp.zeros_like(piece) if chosen is None else chosen)
                here[i] = chosen
            if off:
                copies.append(send(outbox.at[off], inbox(off), ssem.at[off], rsem.at[off], off, 0))
        return copies

    def block(m):
        return pl.ds(m * BS, BS)

    still_copies = scatter(
        lambda m, i: (depth, inv)[i][0:ROWS, block(m)], 2, still_out, lambda off: still.at[off], ds, dr
    )

    def second_step(k, carry):
        def put(r, value):
            c2[k, strip(r), :] = value
            wet = k_x[strip(r), 0:COLS] > k
            rhs[strip(r), :] = rhs[strip(r), :] + jnp.where(wet, dz[k] * value, 0.0)

        advance(lambda r: c1[k, strip(r), :], k, put)
        return carry

    lax.fori_loop(0, levels, second_step, 0)

    for copy in (from_s, from_n, from_w, from_e):
        copy.wait_recv()
    rim_rows(rows1_recv[1], rows1_recv[0], rows1[0], rows1[1])
    flux_cols = rim_cols(cols1[...], cols1_recv[0], cols1_recv[1])
    dz_rows = jnp.zeros((levels, 128), F32)
    dz_cols = jnp.zeros((ROWS, 128), F32)
    for k in range(levels):
        dz_rows = jnp.where(level16[:, 0:128] == k, dz[k], dz_rows)
        dz_cols = jnp.where(group == k, dz[k], dz_cols)
    dz_rows = jnp.concatenate([dz_rows] * (COLS // 128), axis=1)
    weighted = dz_cols * flux_cols
    change_w = jnp.sum(jnp.where(slot == 0, weighted, 0.0), axis=1, keepdims=True)
    change_e = jnp.sum(jnp.where(slot == -1, weighted, 0.0), axis=1, keepdims=True)
    rhs[:, 0:128] = rhs[:, 0:128] + jnp.where(lane == 0, change_w, 0.0)
    rhs[:, COLS - 128 : COLS] = rhs[:, COLS - 128 : COLS] + jnp.where(lane == 127, change_e, 0.0)
    rhs[0:1, :] = rhs[0:1, :] + jnp.sum(dz_rows * row_flux[1], axis=0, keepdims=True)
    rhs[ROWS - 1 : ROWS, :] = rhs[ROWS - 1 : ROWS, :] - jnp.sum(dz_rows * row_flux[0], axis=0, keepdims=True)

    for r in range(STRIPS):
        start = jnp.where(k_x[strip(r), 0:COLS] > 0, rhs[strip(r), :], 0.0)
        basis[0, strip(r), 0:COLS] = start * inv[strip(r), 0:COLS]
    z_rims = rim_refs(zrim_row, zrim_col, zrim_corner)
    z_sends = [send(rim(basis.at[0], s), z_rims[s], zs.at[s], zr.at[s], *SIDES[s]) for s in range(8)]
    first_copies = scatter(
        lambda m, i: basis[0, 0:ROWS, block(m)], 1, first_out, lambda off: slots.at[off, pl.ds(0, 1)], fs, fr
    )
    for k in range(levels):
        correct(c2, k, flux_cols)
    write = pltpu.make_async_copy(c2, tracer_out, out_sem)
    write.start()
    for copy in z_sends:
        copy.wait_recv()
    extend(basis.at[0], z_rims)

    moments = [jnp.zeros((8, 128), F32) for _ in range(8)]

    def inner_product(i, j):
        total = jnp.zeros((8, 128), F32)
        for r in range(STRIPS):
            product = diag[strip(r), 0:COLS] * basis[i, strip(r), 0:COLS] * basis[j, strip(r), 0:COLS]
            for m in range(COLS // 128):
                total = total + product[:, 128 * m : 128 * (m + 1)]
        return total

    moments[0] = inner_product(0, 0)
    lanex = lax.broadcasted_iota(jnp.int32, (8, XC), 1)
    first_lane = (lanex & (BS - 1)) == 0
    lane8 = lanex[:, 0:BS]
    edge_cols = [jnp.zeros((8, BS), F32) for _ in range(blocks)]
    for step in range(ITERS):
        rows_x, inner_x = spread_rows(lambda r: basis[step, strip(r), :], STRIPS + 1, True)
        rows_dx, inner_dx = spread_rows(lambda r: depth[strip(r), :] * basis[step, strip(r), :], STRIPS + 1, True)
        for r in range(STRIPS + 1):
            d, x = depth[strip(r), :], basis[step, strip(r), :]
            image = d * spread_cols(rows_x[r]) + spread_cols(rows_dx[r]) - 8.0 * (d * x)
            scale = (0.25 / HALF) * inv[strip(r), :]
            following = scale * image - (CENTRE / HALF) * x
            if step:
                following = following + following - basis[step - 1, strip(r), :]
            basis[step + 1, strip(r), :] = following
            if r < STRIPS:
                near_x = jnp.where(first_lane, pltpu.roll(inner_x[r], 1, 1), pltpu.roll(inner_x[r], XC - 1, 1))
                near_dx = jnp.where(first_lane, pltpu.roll(inner_dx[r], 1, 1), pltpu.roll(inner_dx[r], XC - 1, 1))
                edge = scale * (d * near_x + near_dx)
                for m in range(blocks):
                    moved = pltpu.roll(edge[:, m * BS : (m + 1) * BS], 16 * r + 2 * step + 1, 1)
                    edge_cols[m] = jnp.where((lane8 >> 1) == 8 * r + step, moved, edge_cols[m])
            else:
                beyond_x, beyond_dx = spread_cols(x), spread_cols(d * x)
                for row, out, at in ((ROWS - 1, 0, 0), (0, 7, 1)):
                    scale = (0.25 / HALF) * inv[row : row + 1, :]
                    edge = scale * (depth[row : row + 1, :] * beyond_x[out : out + 1] + beyond_dx[out : out + 1])
                    edge_rows[2 * step + at : 2 * step + at + 1, :] = edge[:, 0:COLS]
        moments[2 * step + 1] = inner_product(step, step + 1)
        if step < ITERS - 1:
            moments[2 * step + 2] = inner_product(step + 1, step + 1)

    row8 = lax.broadcasted_iota(jnp.int32, (8, 128), 0)
    mine = jnp.zeros((8, 128), F32)
    for m in range(8):
        mine = jnp.where(row8 == m, jnp.sum(moments[m], axis=0, keepdims=True), mine)
    part[...] = mine
    x_sends = [send(part, sums_x.at[off], xs.at[off], xr.at[off], off, 0) for off in range(1, nx)]
    edge_copies = scatter(
        lambda m, i: edge_cols[m] if i else edge_rows[:, block(m)], 2, edges_out, lambda off: edges.at[off], es, er
    )
    total = mine
    for off in range(1, nx):
        x_sends[off - 1].wait_recv()
        total = total + sums_x[off]
    part2[...] = total
    y_sends = [send(part2, sums_y.at[off], ys.at[off], yr.at[off], 0, off) for off in range(1, ny)]

    for copy in still_copies + first_copies + edge_copies:
        copy.wait_recv()

    def repeat(n, carry):
        sub8 = lax.broadcasted_iota(jnp.int32, (8, BS), 0)
        zero8 = jnp.zeros((8, BS), F32)
        sides = (lane8 == 0) | (lane8 == BS - 1)

        def spread(values):
            up = [pltpu.roll(v, 7, 0) for v in values]
            down = [pltpu.roll(v, 1, 0) for v in values]
            out = []
            for r in range(STRIPS):
                north = jnp.where(sub8 == 7, up[r + 1] if r + 1 < STRIPS else 0.0, up[r])
                south = jnp.where(sub8 == 0, down[r - 1] if r else 0.0, down[r])
                v = values[r] + values[r] + (north + south)
                east = jnp.where(lane8 == BS - 1, 0.0, pltpu.roll(v, BS - 1, 1))
                out.append(v + v + (east + jnp.where(lane8 == 0, 0.0, pltpu.roll(v, 1, 1))))
            return out

        x = [slots[n, 0, strip(r), :] for r in range(STRIPS)]
        before = [zero8] * STRIPS
        for step in range(ITERS):
            dx = [still[n, 0, strip(r), :] * x[r] for r in range(STRIPS)]
            wide_x, wide_dx = spread(x), spread(dx)
            after = []
            for r in range(STRIPS):
                image = still[n, 0, strip(r), :] * wide_x[r] + wide_dx[r] - 8.0 * dx[r]
                following = (0.25 / HALF) * still[n, 1, strip(r), :] * image - (CENTRE / HALF) * x[r]
                around = pltpu.roll(edges[n, 1], BS - (16 * r + 2 * step + 1), 1)
                following = following + jnp.where(sides, around, 0.0)
                if r == STRIPS - 1:
                    following = following + jnp.where(sub8 == 7, edges[n, 0, 2 * step : 2 * step + 1, :], 0.0)
                if r == 0:
                    following = following + jnp.where(sub8 == 0, edges[n, 0, 2 * step + 1 : 2 * step + 2, :], 0.0)
                if step:
                    following = following + following - before[r]
                slots[n, step + 1, strip(r), :] = following
                after.append(following)
            before, x = x, after
        for r in range(STRIPS):
            scaled = still[n, 1, strip(r), :]
            full[n, strip(r), :] = jnp.where(scaled > 0.0, 1.0 / jnp.where(scaled > 0.0, scaled, 1.0), 0.0)
        return carry

    lax.fori_loop(0, nx, repeat, 0)

    for off in range(1, ny):
        y_sends[off - 1].wait_recv()
        total = total + sums_y[off]
    total = jnp.sum(total, axis=1, keepdims=True)
    g = [total[m : m + 1, 0:1] for m in range(8)]

    nu = [g[0], g[1]]
    for m in range(2, 8):
        nu.append(g[m] + g[m] - nu[m % 2])
    gram = {}
    for i in range(ITERS):
        for j in range(ITERS + 1):
            gram[i, j] = 0.5 * (nu[i + j] + nu[abs(i - j)]) if i and j else nu[i + j]

    def dot(a, b):
        terms = []
        for i, first_c in enumerate(a):
            inside = None
            for j, second_c in enumerate(b):
                term = gram[min(i, j), max(i, j)] * second_c
                inside = term if inside is None else inside + term
            terms.append(first_c * inside)
        return functools.reduce(lambda p, q: p + q, terms)

    one = jnp.ones((1, 1), F32)
    zero = jnp.zeros((1, 1), F32)
    z, direction, x = [one], [one], [zero] * ITERS
    norm = dot(z, z)
    for step in range(ITERS):
        image = [(1.0 - CENTRE) * v for v in direction] + [zero]
        for i, v in enumerate(direction):
            if i == 0:
                image[1] = image[1] - HALF * v
            else:
                image[i + 1] = image[i + 1] - (0.5 * HALF) * v
                image[i - 1] = image[i - 1] - (0.5 * HALF) * v
        alpha = norm / dot(direction, image)
        for i, v in enumerate(direction):
            x[i] = x[i] + alpha * v
        z = [v - alpha * w for v, w in zip(z + [zero], image)]
        if step < ITERS - 1:
            following = dot(z, z)
            ratio = following / norm
            direction = [v + ratio * w for v, w in zip(z, direction + [zero])]
            norm = following

    results = []
    for n in range(nx):
        for r in range(STRIPS):
            y = [slots[n, i, strip(r), :] for i in range(ITERS + 1)]
            stage[n, 0, strip(r), :] = sum(x[i] * y[i] for i in range(ITERS))
            stage[n, 1, strip(r), :] = full[n, strip(r), :] * sum(z[i] * y[i] for i in range(ITERS + 1))
        place = pl.ds(pl.multiple_of(lax.rem(mx - n + nx, nx) * BS, BS), BS)
        copy = pltpu.make_async_copy(stage.at[n], barotropic.at[:, :, place], last_sem.at[n])
        copy.start()
        results.append(copy)
    for copy in results:
        copy.wait()
    write.wait()
    for copy in pending:
        copy.wait_send()


def on_device(tracer, u_east, v_north, kmt, dest, dz, wind):
    nx, ny = lax.axis_size("bx"), lax.axis_size("by")
    levels = tracer.shape[0]
    slab = pltpu.VMEM((levels, ROWS, COLS), F32)
    ext = pltpu.VMEM((XR, XC), F32)
    flat = pltpu.VMEM((ROWS, COLS), F32)
    flat_i = pltpu.VMEM((ROWS, COLS), jnp.int32)
    rows = pltpu.VMEM((levels, COLS), F32)
    rows2 = pltpu.VMEM((2, levels, COLS), F32)
    cols = pltpu.VMEM((ROWS, 128), F32)
    cols2 = pltpu.VMEM((2, ROWS, 128), F32)

    def rims(dtype):
        return [
            pltpu.VMEM((2, 8, COLS), dtype),
            pltpu.VMEM((2, ROWS, 128), dtype),
            pltpu.VMEM((4, 8, 128), dtype),
        ]

    scratch = [slab] * 5 + [pltpu.VMEM((XR, XC), jnp.int32), flat_i, flat_i, flat] + [slab] * 4
    scratch += [ext, ext, ext, pltpu.VMEM((ITERS + 1, XR, XC), F32)]
    scratch += [pltpu.SMEM(dest.shape, jnp.int32), pltpu.SMEM(dz.shape, F32)]
    scratch += rims(F32) + rims(jnp.int32)
    scratch += [rows2, rows, cols, rows2, rows, cols2]
    scratch += [rows2, rows2, cols, cols2, rows2]
    scratch += [
        pltpu.VMEM((8, 128), F32),
        pltpu.VMEM((nx, 8, 128), F32),
        pltpu.VMEM((8, 128), F32),
        pltpu.VMEM((ny, 8, 128), F32),
        pltpu.VMEM((nx, 2, ROWS, BS), F32),
        pltpu.VMEM((nx, 2, ROWS, BS), F32),
        pltpu.VMEM((nx, 1, ROWS, BS), F32),
        pltpu.VMEM((nx, ITERS + 1, ROWS, BS), F32),
        pltpu.VMEM((8, COLS), F32),
        pltpu.VMEM((nx, 2, 8, BS), F32),
        pltpu.VMEM((nx, 2, 8, BS), F32),
        pltpu.VMEM((nx, ROWS, BS), F32),
        pltpu.VMEM((nx, 2, ROWS, BS), F32),
    ]
    counts = [9, None] + [8] * 6 + [nx, nx, ny, ny] + [nx] * 7
    scratch += [pltpu.SemaphoreType.DMA((n,)) if n else pltpu.SemaphoreType.DMA for n in counts]
    anywhere = pl.BlockSpec(memory_space=pl.ANY)
    hbm = pl.BlockSpec(memory_space=pltpu.HBM)
    return pl.pallas_call(
        functools.partial(kernel, nx, ny, levels),
        out_shape=(
            jax.ShapeDtypeStruct(tracer.shape, F32),
            jax.ShapeDtypeStruct((2, ROWS, nx * BS), F32),
        ),
        in_specs=[hbm] * 7,
        out_specs=(anywhere, anywhere),
        scratch_shapes=scratch,
        compiler_params=pltpu.CompilerParams(
            collective_id=0, has_side_effects=True, vmem_limit_bytes=32 * 1024 * 1024
        ),
    )(*[pltpu.with_memory_space_constraint(x, pltpu.HBM) for x in (tracer, u_east, v_north, kmt, dest, dz, wind)])


def solution(mesh):
    in_specs = (
        P(None, "by", "bx"),
        P(None, "by", "bx"),
        P(None, "by", "bx"),
        P("by", "bx"),
        P("by", "bx"),
        P(),
        P("by", "bx"),
    )
    out_specs = (P(None, "by", "bx"), P(None, "by", "bx"))
    return jax.shard_map(
        on_device, mesh=mesh, in_specs=in_specs, out_specs=out_specs, check_vma=False
    )
```

```python
import functools

import jax
import jax.numpy as jnp
from jax import lax
from jax.experimental import pallas as pl
from jax.experimental.pallas import tpu as pltpu
from jax.sharding import PartitionSpec as P

BS = 128
ITERS = 4
KAPPA = 0.12
SIGMA = 0.2
CENTRE = 1.0 / 3.0
HALF = 2.0 / 3.0
MESH = pl.DeviceIdType.MESH
ROWS = 64
COLS = 512
XR = ROWS + 8
XC = COLS + 128
STRIPS = ROWS // 8
F32 = jnp.float32
SIDES = ((0, 1), (0, -1), (1, 0), (-1, 0), (1, 1), (-1, 1), (1, -1), (-1, -1))


def strip(r):
    return pl.ds(8 * r, 8)


def rim(ref, side):
    dx, dy = SIDES[side]
    rows = {1: pl.ds(ROWS - 8, 8), -1: pl.ds(0, 8), 0: pl.ds(0, ROWS)}[dy]
    cols = {1: pl.ds(COLS - 128, 128), -1: pl.ds(0, 128), 0: pl.ds(0, COLS)}[dx]
    return ref.at[rows, cols]


def pack_ends(ext):
    lane = lax.broadcasted_iota(jnp.int32, (8, 128), 1)
    packed = jnp.zeros((8, 128), ext.dtype)
    for r in range(STRIPS):
        both = jnp.where(lane < 64, ext[strip(r), 0:128], ext[strip(r), COLS - 128 : COLS])
        both = pltpu.roll(both, 16 * r, 1) if r else both
        packed = jnp.where(((lane + 8) & 127) >> 4 == r, both, packed)
    return packed


def extend(ext, rims):
    from_s, from_n, from_w, from_e, from_sw, from_se, from_nw, from_ne = rims
    low = lax.broadcasted_iota(jnp.int32, (8, COLS), 0) < 4
    ext[ROWS:XR, 0:COLS] = jnp.where(low, from_n[...], from_s[...])
    lane = lax.broadcasted_iota(jnp.int32, (8, 128), 1)
    ends = jnp.where(((lane + 8) & 15) < 8, from_w[...], from_e[...])
    for r in range(STRIPS):
        ext[strip(r), COLS:XC] = pltpu.roll(ends, 128 - 16 * r, 1) if r else ends
    east8 = lane < 64
    low8 = lax.broadcasted_iota(jnp.int32, (8, 128), 0) < 4
    ext[ROWS:XR, COLS:XC] = jnp.where(
        low8,
        jnp.where(east8, from_ne[...], from_nw[...]),
        jnp.where(east8, from_se[...], from_sw[...]),
    )


def spread_rows(get, count, wrap=True):
    x = [get(r) for r in range(count)]
    sub = lax.broadcasted_iota(jnp.int32, x[0].shape, 0)
    up = [pltpu.roll(v, 7, 0) for v in x]
    down = [pltpu.roll(v, 1, 0) for v in x]
    out = []
    for r in range(count):
        north = jnp.where(sub == 7, up[(r + 1) % count] if wrap or r + 1 < count else 0.0, up[r])
        south = jnp.where(sub == 0, down[r - 1] if wrap or r else 0.0, down[r])
        out.append(x[r] + x[r] + (north + south))
    return out


def spread_cols(v):
    return v + v + (pltpu.roll(v, 1, 1) + pltpu.roll(v, XC - 1, 1))


def kernel(
    nx,
    ny,
    levels,
    tracer,
    u_east,
    v_north,
    kmt,
    dest_in,
    dz_in,
    wind,
    tracer_out,
    barotropic,
    c0,
    u0,
    v0,
    c1,
    c2,
    k_x,
    ke,
    kn,
    rhs,
    ae,
    be,
    an,
    bn,
    depth,
    inv,
    diag,
    basis,
    dest,
    dz,
    zrim_row,
    zrim_col,
    zrim_corner,
    krim_row,
    krim_col,
    krim_corner,
    up_send,
    dn_send,
    col_send,
    up_recv,
    dn_recv,
    col_recv,
    rows1,
    rows1_recv,
    cols1,
    cols1_recv,
    rows_own,
    cols_own,
    kends,
    zends,
    row_flux,
    part,
    sums_x,
    part2,
    sums_y,
    still_out,
    still,
    first_out,
    slots,
    ring_d,
    edge_d,
    edge_s,
    edge_rows,
    edges_out,
    edges,
    full,
    stage,
    load_sem,
    out_sem,
    ks,
    kr,
    rs,
    rr,
    zs,
    zr,
    xs,
    xr,
    ys,
    yr,
    ds,
    dr,
    fs,
    fr,
    es,
    er,
    last_sem,
):
    mx = lax.axis_index("bx")
    my = lax.axis_index("by")
    pending, pending_rims = [], []

    def peer(dx, dy):
        return (lax.rem(mx + dx + nx, nx), lax.rem(my + dy + ny, ny))

    def send(src, dst, send_sem, recv_sem, dx, dy):
        copy = pltpu.make_async_remote_copy(
            src_ref=src, dst_ref=dst, send_sem=send_sem, recv_sem=recv_sem, device_id=peer(dx, dy), device_id_type=MESH
        )
        copy.start()
        pending.append(copy)
        return copy

    def send_rim(src, dst, send_sem, recv_sem, dx, dy):
        copy = pltpu.make_async_remote_copy(
            src_ref=src, dst_ref=dst, send_sem=send_sem, recv_sem=recv_sem, device_id=peer(dx, dy), device_id_type=MESH
        )
        goes, comes = {1: (has_n, has_s), -1: (has_s, has_n), 0: (None, None)}[dy]

        def guarded(action, guard):
            action() if guard is None else pl.when(guard)(action)

        guarded(copy.start, goes)
        pending_rims.append(lambda: guarded(copy.wait_send, goes))
        return lambda: guarded(copy.wait_recv, comes)

    has_n, has_s = my < ny - 1, my > 0
    barrier = pltpu.get_barrier_semaphore()

    def greet(dx, dy):
        pl.semaphore_signal(barrier, inc=1, device_id=peer(dx, dy), device_id_type=MESH)

    for off in sorted(range(1, ny), key=lambda o: -min(o, ny - o)):
        greet(0, off)
    for off in sorted(range(1, nx), key=lambda o: -min(o, nx - o)):
        greet(off, 0)
    for dx, dy in SIDES[4:]:
        pl.when(has_n if dy == 1 else has_s)(functools.partial(greet, dx, dy))
    n_peers = nx - 1 + ny - 1 + jnp.where(has_n, 2, 0) + jnp.where(has_s, 2, 0)

    last_cols = (slice(None), slice(None), pl.ds(COLS - 128, 128))
    other_cols = (slice(None), slice(None), pl.ds(0, COLS - 128))
    last_rows = (slice(None), pl.ds(ROWS - 8, 8))
    other_rows = (slice(None), pl.ds(0, ROWS - 8))
    loads = [
        pltpu.make_async_copy(kmt, k_x.at[pl.ds(0, ROWS), pl.ds(0, COLS)], load_sem.at[0]),
        pltpu.make_async_copy(dest_in, dest, load_sem.at[1]),
        pltpu.make_async_copy(dz_in, dz, load_sem.at[2]),
        pltpu.make_async_copy(tracer, c0, load_sem.at[3]),
        pltpu.make_async_copy(u_east.at[last_cols], u0.at[last_cols], load_sem.at[4]),
        pltpu.make_async_copy(v_north.at[last_rows], v0.at[last_rows], load_sem.at[5]),
        pltpu.make_async_copy(u_east.at[other_cols], u0.at[other_cols], load_sem.at[6]),
        pltpu.make_async_copy(v_north.at[other_rows], v0.at[other_rows], load_sem.at[7]),
        pltpu.make_async_copy(wind, rhs, load_sem.at[8]),
    ]
    for copy in loads:
        copy.start()

    def no_rim(at, corners):
        zrim_row[at] = jnp.zeros((8, COLS), F32)
        krim_row[at] = jnp.zeros((8, COLS), jnp.int32)
        for i in corners:
            zrim_corner[i] = jnp.zeros((8, 128), F32)
            krim_corner[i] = jnp.zeros((8, 128), jnp.int32)

    pl.when(jnp.logical_not(has_s))(lambda: no_rim(0, (0, 1)))
    pl.when(jnp.logical_not(has_n))(lambda: no_rim(1, (2, 3)))

    loads[0].wait()
    sub = lax.broadcasted_iota(jnp.int32, (8, COLS), 0)
    lane_row = lax.broadcasted_iota(jnp.int32, (8, COLS), 1)
    k_up = [pltpu.roll(k_x[strip(r), 0:COLS], 7, 0) for r in range(STRIPS)]
    for r in range(STRIPS):
        here = k_x[strip(r), 0:COLS]
        east = jnp.where(lane_row == COLS - 1, 0, pltpu.roll(here, COLS - 1, 1))
        north = jnp.where(sub == 7, k_up[r + 1] if r + 1 < STRIPS else 0, k_up[r])
        ke[strip(r), :] = jnp.minimum(here, east)
        kn[strip(r), :] = jnp.minimum(here, north)
    for copy in loads[1:6]:
        copy.wait()

    lane = lax.broadcasted_iota(jnp.int32, (ROWS, 128), 1)
    west = lane < 64
    group = ((lane + 4) & 127) >> 3
    slot = ((lane + 4) & 7) - 4

    def ends(field, k):
        return jnp.where(west, field[k, :, 0:128], field[k, :, COLS - 128 : COLS])

    def turned(value, lanes):
        return pltpu.roll(value, lanes % 128, 1) if lanes % 128 else value

    packed = jnp.zeros((ROWS, 128), F32)
    for k in range(levels):
        up_send[0, k : k + 1, :] = c0[k, ROWS - 1 : ROWS, :]
        up_send[1, k : k + 1, :] = v0[k, ROWS - 1 : ROWS, :]
        dn_send[k : k + 1, :] = c0[k, 0:1, :]
        both = jnp.where(slot == -2, turned(u0[k, :, COLS - 128 : COLS], 8 * k - 1), turned(ends(c0, k), 8 * k))
        packed = jnp.where(group == k, both, packed)
    col_send[...] = packed
    pl.semaphore_wait(barrier, n_peers)
    from_s = send_rim(up_send, up_recv, rs.at[0], rr.at[0], 0, 1)
    from_n = send_rim(dn_send, dn_recv, rs.at[1], rr.at[1], 0, -1)
    from_w = send_rim(col_send, col_recv.at[0], rs.at[2], rr.at[2], 1, 0)
    from_e = send_rim(col_send, col_recv.at[1], rs.at[3], rr.at[3], -1, 0)

    def rim_refs(row, col, corner):
        return [row.at[0], row.at[1], col.at[0], col.at[1]] + [corner.at[i] for i in range(4)]

    k_rims = rim_refs(krim_row, krim_col, krim_corner)
    kends[...] = pack_ends(k_x)
    k_sends = [
        send_rim(kends if SIDES[s][1] == 0 else rim(kmt, s), k_rims[s], ks.at[s], kr.at[s], *SIDES[s]) for s in range(8)
    ]

    def advance(get, k, put):
        def north_flux(r, c, up, nxt):
            return an[k, strip(r), :] * c + bn[k, strip(r), :] * jnp.where(sub == 7, nxt, up)

        below = jnp.zeros((8, COLS), F32)
        c, up = get(0), pltpu.roll(get(0), 7, 0)
        for r in range(STRIPS):
            if r + 1 < STRIPS:
                c_next = get(r + 1)
                up_next = pltpu.roll(c_next, 7, 0)
            flux = north_flux(r, c, up, up_next)
            down = pltpu.roll(flux, 1, 0)
            flux_e = ae[k, strip(r), :] * c + be[k, strip(r), :] * pltpu.roll(c, COLS - 1, 1)
            spread = flux_e - pltpu.roll(flux_e, 1, 1)
            spread = spread + (flux - jnp.where(sub == 0, below, down))
            put(r, c - spread)
            below, c, up = down, c_next, up_next

    def first_step(k, carry):
        for r in range(STRIPS):
            half_u, half_v = 0.5 * u0[k, strip(r), :], 0.5 * v0[k, strip(r), :]
            wet_e, wet_n = ke[strip(r), :] > k, kn[strip(r), :] > k
            ae[k, strip(r), :] = jnp.where(wet_e, half_u + KAPPA, 0.0)
            be[k, strip(r), :] = jnp.where(wet_e, half_u - KAPPA, 0.0)
            an[k, strip(r), :] = jnp.where(wet_n, half_v + KAPPA, 0.0)
            bn[k, strip(r), :] = jnp.where(wet_n, half_v - KAPPA, 0.0)

        def put(r, value):
            c1[k, strip(r), :] = value

        advance(lambda r: c0[k, strip(r), :], k, put)
        return carry

    for copy in loads[6:]:
        copy.wait()
    lax.fori_loop(0, levels, first_step, 0)
    packed = jnp.zeros((ROWS, 128), F32)
    for k in range(levels):
        rows_own[0, k : k + 1, :] = c1[k, ROWS - 1 : ROWS, :]
        rows_own[1, k : k + 1, :] = c1[k, 0:1, :]
        packed = jnp.where(group == k, turned(ends(c1, k), 8 * k), packed)
    cols_own[...] = packed

    for arrival in k_sends:
        arrival()
    extend(k_x, k_rims)
    level16 = lax.broadcasted_iota(jnp.int32, (levels, COLS), 0)
    wet_n = jnp.minimum(k_x[ROWS - 1 : ROWS, 0:COLS], k_x[ROWS : ROWS + 1, 0:COLS]) > level16
    wet_s = jnp.minimum(k_x[0:1, 0:COLS], k_x[XR - 1 : XR, 0:COLS]) > level16
    wet_e = jnp.minimum(k_x[0:ROWS, COLS - 1 : COLS], k_x[0:ROWS, COLS : COLS + 1]) > group
    wet_w = jnp.minimum(k_x[0:ROWS, 0:1], k_x[0:ROWS, XC - 1 : XC]) > group

    def face(velocity, here, there, wet):
        half = 0.5 * velocity
        return jnp.where(wet, (half + KAPPA) * here + (half - KAPPA) * there, 0.0)

    def rim_rows(north_row, south_row, own_north, own_south):
        row_flux[0] = face(up_send[1], own_north, north_row, wet_n)
        row_flux[1] = face(up_recv[1], south_row, own_south, wet_s)

    def rim_cols(own, westward, eastward):
        out = face(turned(col_send[...], 1), own, turned(eastward, -1), wet_e)
        into = face(turned(col_recv[0], 2), turned(westward, 1), own, wet_w)
        return jnp.where(slot == -1, -out, jnp.where(slot == 0, into, 0.0))

    for arrival in (from_s, from_n, from_w, from_e):
        arrival()
    rim_rows(dn_recv[...], up_recv[0], up_send[0], dn_send[...])
    flux_cols = rim_cols(col_send[...], col_recv[0], col_recv[1])

    def correct(field, k, flux):
        change = turned(flux, -8 * k)
        field[k, :, 0:128] = field[k, :, 0:128] + jnp.where(lane == 0, change, 0.0)
        field[k, :, COLS - 128 : COLS] = field[k, :, COLS - 128 : COLS] + jnp.where(lane == 127, change, 0.0)
        field[k, 0:1, :] = field[k, 0:1, :] + row_flux[1, k : k + 1, :]
        field[k, ROWS - 1 : ROWS, :] = field[k, ROWS - 1 : ROWS, :] - row_flux[0, k : k + 1, :]

    lane16 = lax.broadcasted_iota(jnp.int32, (levels, 128), 1)
    level8 = 8 * level16[:, 0:128]
    on_west, on_east = lane16 == level8, lane16 == ((level8 + 127) & 127)
    for at, row, sign in ((0, ROWS - 1, -1.0), (1, 0, 1.0)):
        line = jnp.broadcast_to(flux_cols[row : row + 1, :], (levels, 128))
        from_west = jnp.sum(jnp.where(on_west, line, 0.0), axis=1, keepdims=True)
        from_east = jnp.sum(jnp.where(on_east, line, 0.0), axis=1, keepdims=True)
        change = sign * row_flux[at]
        value = rows_own[at] + change
        rows1[at, :, 0:128] = value[:, 0:128] + jnp.where(lane16 == 0, from_west, 0.0)
        rows1[at, :, 128 : COLS - 128] = value[:, 128 : COLS - 128]
        rows1[at, :, COLS - 128 : COLS] = value[:, COLS - 128 : COLS] + jnp.where(lane16 == 127, from_east, 0.0)
        corner = jnp.where(on_west, change[:, 0:1], 0.0) + jnp.where(on_east, change[:, COLS - 1 : COLS], 0.0)
        cols_own[row : row + 1, :] = cols_own[row : row + 1, :] + jnp.sum(corner, axis=0, keepdims=True)
    cols1[...] = cols_own[...] + flux_cols
    from_s = send_rim(rows1.at[0], rows1_recv.at[0], rs.at[4], rr.at[4], 0, 1)
    from_n = send_rim(rows1.at[1], rows1_recv.at[1], rs.at[5], rr.at[5], 0, -1)
    from_w = send_rim(cols1, cols1_recv.at[0], rs.at[6], rr.at[6], 1, 0)
    from_e = send_rim(cols1, cols1_recv.at[1], rs.at[7], rr.at[7], -1, 0)
    for k in range(levels):
        correct(c1, k, flux_cols)

    subx = lax.broadcasted_iota(jnp.int32, (8, XC), 0)
    for r in range(STRIPS + 1):
        here = k_x[strip(r), :]
        total = jnp.zeros((8, XC), F32)
        for k in range(levels):
            total = total + jnp.where(here > k, dz[k], 0.0)
        depth[strip(r), :] = total

    def ocean_of(r):
        return jnp.where(k_x[strip(r), :] > 0, 1.0, 0.0).astype(F32)

    rows_o = spread_rows(ocean_of, STRIPS + 1)
    rows_d = spread_rows(lambda r: depth[strip(r), :], STRIPS + 1)
    for r in range(STRIPS + 1):
        d = depth[strip(r), :]
        o = ocean_of(r)
        total = d * spread_cols(rows_o[r]) + spread_cols(rows_d[r]) - 8.0 * d
        whole = SIGMA + 0.25 * o * total
        diag[strip(r), :] = whole
        inv[strip(r), :] = o / whole

    blocks = COLS // BS

    def scatter(get, parts, outbox, inbox, ssem, rsem):
        copies = []
        for off in sorted(range(nx), key=lambda o: -min(o, nx - o)):
            target = lax.rem(mx + off, nx)
            hits = [dest[0, m] == target for m in range(blocks)]
            here = outbox.at[off] if off else inbox(0)
            for i in range(parts):
                chosen = None
                for m in range(blocks):
                    piece = get(m, i)
                    chosen = jnp.where(hits[m], piece, jnp.zeros_like(piece) if chosen is None else chosen)
                here[i] = chosen
            if off:
                copies.append(send(outbox.at[off], inbox(off), ssem.at[off], rsem.at[off], off, 0))
        return copies

    def block(m):
        return pl.ds(m * BS, BS)

    still_copies = scatter(
        lambda m, i: (depth, inv)[i][0:ROWS, block(m)], 2, still_out, lambda off: still.at[off], ds, dr
    )

    def second_step(k, carry):
        def put(r, value):
            c2[k, strip(r), :] = value
            wet = k_x[strip(r), 0:COLS] > k
            rhs[strip(r), :] = rhs[strip(r), :] + jnp.where(wet, dz[k] * value, 0.0)

        advance(lambda r: c1[k, strip(r), :], k, put)
        return carry

    lax.fori_loop(0, levels, second_step, 0)

    for arrival in (from_s, from_n, from_w, from_e):
        arrival()
    rim_rows(rows1_recv[1], rows1_recv[0], rows1[0], rows1[1])
    flux_cols = rim_cols(cols1[...], cols1_recv[0], cols1_recv[1])
    dz_rows = jnp.zeros((levels, 128), F32)
    dz_cols = jnp.zeros((ROWS, 128), F32)
    for k in range(levels):
        dz_rows = jnp.where(level16[:, 0:128] == k, dz[k], dz_rows)
        dz_cols = jnp.where(group == k, dz[k], dz_cols)
    dz_rows = jnp.concatenate([dz_rows] * (COLS // 128), axis=1)
    weighted = dz_cols * flux_cols
    change_w = jnp.sum(jnp.where(slot == 0, weighted, 0.0), axis=1, keepdims=True)
    change_e = jnp.sum(jnp.where(slot == -1, weighted, 0.0), axis=1, keepdims=True)
    rhs[:, 0:128] = rhs[:, 0:128] + jnp.where(lane == 0, change_w, 0.0)
    rhs[:, COLS - 128 : COLS] = rhs[:, COLS - 128 : COLS] + jnp.where(lane == 127, change_e, 0.0)
    rhs[0:1, :] = rhs[0:1, :] + jnp.sum(dz_rows * row_flux[1], axis=0, keepdims=True)
    rhs[ROWS - 1 : ROWS, :] = rhs[ROWS - 1 : ROWS, :] - jnp.sum(dz_rows * row_flux[0], axis=0, keepdims=True)

    for r in range(STRIPS):
        start = jnp.where(k_x[strip(r), 0:COLS] > 0, rhs[strip(r), :], 0.0)
        basis[0, strip(r), 0:COLS] = start * inv[strip(r), 0:COLS]
    z_rims = rim_refs(zrim_row, zrim_col, zrim_corner)
    zends[...] = pack_ends(basis.at[0])
    z_sends = [
        send_rim(zends if SIDES[s][1] == 0 else rim(basis.at[0], s), z_rims[s], zs.at[s], zr.at[s], *SIDES[s])
        for s in range(8)
    ]
    first_copies = scatter(
        lambda m, i: basis[0, 0:ROWS, block(m)], 1, first_out, lambda off: slots.at[off, pl.ds(0, 1)], fs, fr
    )
    for k in range(levels):
        correct(c2, k, flux_cols)
    write = pltpu.make_async_copy(c2, tracer_out, out_sem)
    write.start()

    lane8 = lax.broadcasted_iota(jnp.int32, (8, BS), 1)

    def pack(both):
        packed = jnp.zeros((8, BS), F32)
        for m in range(blocks):
            packed = jnp.where(((lane8 + 8) & 127) >> 4 == m, turned(both[m], 16 * m), packed)
        return packed

    def tiles(ref, r):
        return [ref[strip(r), block(m)] for m in range(blocks + 1)]

    def pack_ring(tile):
        return pack([jnp.where(lane8 < 64, tile[m + 1], tile[m - 1]) for m in range(blocks)])

    def pack_edges(tile):
        return pack([jnp.where(lane8 == 0, turned(tile[m], 1), turned(tile[m], -1)) for m in range(blocks)])

    for r in range(STRIPS):
        ring_d[strip(r), :] = pack_ring(tiles(depth, r))
        edge_d[strip(r), :] = pack_edges(tiles(depth, r))
        edge_s[strip(r), :] = (0.25 / HALF) * pack_edges(tiles(inv, r))
    for arrival in z_sends:
        arrival()
    extend(basis.at[0], z_rims)

    moments = [jnp.zeros((8, 128), F32) for _ in range(8)]

    def inner_product(i, j):
        total = jnp.zeros((8, 128), F32)
        for r in range(STRIPS):
            product = diag[strip(r), 0:COLS] * basis[i, strip(r), 0:COLS] * basis[j, strip(r), 0:COLS]
            for m in range(COLS // 128):
                total = total + product[:, 128 * m : 128 * (m + 1)]
        return total

    moments[0] = inner_product(0, 0)
    for step in range(ITERS):
        rows_x = spread_rows(lambda r: basis[step, strip(r), :], STRIPS + 1)
        rows_dx = spread_rows(lambda r: depth[strip(r), :] * basis[step, strip(r), :], STRIPS + 1)
        for r in range(STRIPS + 1):
            d, x = depth[strip(r), :], basis[step, strip(r), :]
            image = d * spread_cols(rows_x[r]) + spread_cols(rows_dx[r]) - 8.0 * (d * x)
            scale = (0.25 / HALF) * inv[strip(r), :]
            following = scale * image - (CENTRE / HALF) * x
            if step:
                following = following + following - basis[step - 1, strip(r), :]
            basis[step + 1, strip(r), :] = following
        moments[2 * step + 1] = inner_product(step, step + 1)
        if step < ITERS - 1:
            moments[2 * step + 2] = inner_product(step + 1, step + 1)

    row8 = lax.broadcasted_iota(jnp.int32, (8, 128), 0)
    mine = jnp.zeros((8, 128), F32)
    for m in range(8):
        mine = jnp.where(row8 == m, jnp.sum(moments[m], axis=0, keepdims=True), mine)
    part[...] = mine
    x_sends = [send(part, sums_x.at[off], xs.at[off], xr.at[off], off, 0) for off in range(1, nx)]
    edge_cols = [jnp.zeros((8, BS), F32) for _ in range(blocks)]
    for step in range(ITERS):
        ring_x = [pack_ring(tiles(basis.at[step], r)) for r in range(STRIPS)]
        ring_dx = [ring_d[strip(r), :] * ring_x[r] for r in range(STRIPS)]
        inner_x = spread_rows(lambda r: ring_x[r], STRIPS, False)
        inner_dx = spread_rows(lambda r: ring_dx[r], STRIPS, False)
        for r in range(STRIPS):
            edge = edge_s[strip(r), :] * (edge_d[strip(r), :] * inner_x[r] + inner_dx[r])
            for m in range(blocks):
                moved = turned(edge, 16 * r + 2 * step + 1 - 16 * m)
                edge_cols[m] = jnp.where((lane8 >> 1) == 8 * r + step, moved, edge_cols[m])
        x = basis[step, strip(STRIPS), :]
        beyond_x, beyond_dx = spread_cols(x), spread_cols(depth[strip(STRIPS), :] * x)
        for row, out, at in ((ROWS - 1, 0, 0), (0, 7, 1)):
            scale = (0.25 / HALF) * inv[row : row + 1, :]
            edge = scale * (depth[row : row + 1, :] * beyond_x[out : out + 1] + beyond_dx[out : out + 1])
            edge_rows[2 * step + at : 2 * step + at + 1, :] = edge[:, 0:COLS]
    for m in range(blocks):
        edge_cols[m] = jnp.where((lane8 & 1) == 1, turned(edge_cols[m], 1), turned(edge_cols[m], -1))
    edge_copies = scatter(
        lambda m, i: edge_cols[m] if i else edge_rows[:, block(m)], 2, edges_out, lambda off: edges.at[off], es, er
    )
    total = mine
    for off in range(1, nx):
        x_sends[off - 1].wait_recv()
        total = total + sums_x[off]
    part2[...] = total
    y_sends = [send(part2, sums_y.at[off], ys.at[off], yr.at[off], 0, off) for off in range(1, ny)]

    for copy in still_copies + first_copies + edge_copies:
        copy.wait_recv()

    def repeat(n, carry):
        sub8 = lax.broadcasted_iota(jnp.int32, (8, BS), 0)
        zero8 = jnp.zeros((8, BS), F32)
        sides = (lane8 == 0) | (lane8 == BS - 1)

        def spread(values):
            up = [pltpu.roll(v, 7, 0) for v in values]
            down = [pltpu.roll(v, 1, 0) for v in values]
            out = []
            for r in range(STRIPS):
                north = jnp.where(sub8 == 7, up[r + 1] if r + 1 < STRIPS else 0.0, up[r])
                south = jnp.where(sub8 == 0, down[r - 1] if r else 0.0, down[r])
                v = values[r] + values[r] + (north + south)
                east = jnp.where(lane8 == BS - 1, 0.0, pltpu.roll(v, BS - 1, 1))
                out.append(v + v + (east + jnp.where(lane8 == 0, 0.0, pltpu.roll(v, 1, 1))))
            return out

        x = [slots[n, 0, strip(r), :] for r in range(STRIPS)]
        before = [zero8] * STRIPS
        for step in range(ITERS):
            dx = [still[n, 0, strip(r), :] * x[r] for r in range(STRIPS)]
            wide_x, wide_dx = spread(x), spread(dx)
            after = []
            for r in range(STRIPS):
                image = still[n, 0, strip(r), :] * wide_x[r] + wide_dx[r] - 8.0 * dx[r]
                following = (0.25 / HALF) * still[n, 1, strip(r), :] * image - (CENTRE / HALF) * x[r]
                around = pltpu.roll(edges[n, 1], BS - (16 * r + 2 * step + 1), 1)
                following = following + jnp.where(sides, around, 0.0)
                if r == STRIPS - 1:
                    following = following + jnp.where(sub8 == 7, edges[n, 0, 2 * step : 2 * step + 1, :], 0.0)
                if r == 0:
                    following = following + jnp.where(sub8 == 0, edges[n, 0, 2 * step + 1 : 2 * step + 2, :], 0.0)
                if step:
                    following = following + following - before[r]
                slots[n, step + 1, strip(r), :] = following
                after.append(following)
            before, x = x, after
        for r in range(STRIPS):
            scaled = still[n, 1, strip(r), :]
            full[n, strip(r), :] = jnp.where(scaled > 0.0, 1.0 / jnp.where(scaled > 0.0, scaled, 1.0), 0.0)
        return carry

    lax.fori_loop(0, nx, repeat, 0)

    for off in range(1, ny):
        y_sends[off - 1].wait_recv()
        total = total + sums_y[off]
    total = jnp.sum(total, axis=1, keepdims=True)
    g = [total[m : m + 1, 0:1] for m in range(8)]

    nu = [g[0], g[1]]
    for m in range(2, 8):
        nu.append(g[m] + g[m] - nu[m % 2])
    gram = {}
    for i in range(ITERS):
        for j in range(ITERS + 1):
            gram[i, j] = 0.5 * (nu[i + j] + nu[abs(i - j)]) if i and j else nu[i + j]

    def dot(a, b):
        terms = []
        for i, first_c in enumerate(a):
            inside = None
            for j, second_c in enumerate(b):
                term = gram[min(i, j), max(i, j)] * second_c
                inside = term if inside is None else inside + term
            terms.append(first_c * inside)
        return functools.reduce(lambda p, q: p + q, terms)

    one = jnp.ones((1, 1), F32)
    zero = jnp.zeros((1, 1), F32)
    z, direction, x = [one], [one], [zero] * ITERS
    norm = dot(z, z)
    for step in range(ITERS):
        image = [(1.0 - CENTRE) * v for v in direction] + [zero]
        for i, v in enumerate(direction):
            if i == 0:
                image[1] = image[1] - HALF * v
            else:
                image[i + 1] = image[i + 1] - (0.5 * HALF) * v
                image[i - 1] = image[i - 1] - (0.5 * HALF) * v
        alpha = norm / dot(direction, image)
        for i, v in enumerate(direction):
            x[i] = x[i] + alpha * v
        z = [v - alpha * w for v, w in zip(z + [zero], image)]
        if step < ITERS - 1:
            following = dot(z, z)
            ratio = following / norm
            direction = [v + ratio * w for v, w in zip(z, direction + [zero])]
            norm = following

    results = []
    for n in range(nx):
        for r in range(STRIPS):
            y = [slots[n, i, strip(r), :] for i in range(ITERS + 1)]
            stage[n, 0, strip(r), :] = sum(x[i] * y[i] for i in range(ITERS))
            stage[n, 1, strip(r), :] = full[n, strip(r), :] * sum(z[i] * y[i] for i in range(ITERS + 1))
        place = pl.ds(pl.multiple_of(lax.rem(mx - n + nx, nx) * BS, BS), BS)
        copy = pltpu.make_async_copy(stage.at[n], barotropic.at[:, :, place], last_sem.at[n])
        copy.start()
        results.append(copy)
    for copy in results:
        copy.wait()
    write.wait()
    for copy in pending:
        copy.wait_send()
    for departure in pending_rims:
        departure()


def on_device(tracer, u_east, v_north, kmt, dest, dz, wind):
    nx, ny = lax.axis_size("bx"), lax.axis_size("by")
    levels = tracer.shape[0]
    slab = pltpu.VMEM((levels, ROWS, COLS), F32)
    ext = pltpu.VMEM((XR, XC), F32)
    flat = pltpu.VMEM((ROWS, COLS), F32)
    flat_i = pltpu.VMEM((ROWS, COLS), jnp.int32)
    rows = pltpu.VMEM((levels, COLS), F32)
    rows2 = pltpu.VMEM((2, levels, COLS), F32)
    cols = pltpu.VMEM((ROWS, 128), F32)
    cols2 = pltpu.VMEM((2, ROWS, 128), F32)

    def rims(dtype):
        return [
            pltpu.VMEM((2, 8, COLS), dtype),
            pltpu.VMEM((2, 8, 128), dtype),
            pltpu.VMEM((4, 8, 128), dtype),
        ]

    scratch = [slab] * 5 + [pltpu.VMEM((XR, XC), jnp.int32), flat_i, flat_i, flat] + [slab] * 4
    scratch += [ext, ext, ext, pltpu.VMEM((ITERS + 1, XR, XC), F32)]
    scratch += [pltpu.SMEM(dest.shape, jnp.int32), pltpu.SMEM(dz.shape, F32)]
    scratch += rims(F32) + rims(jnp.int32)
    scratch += [rows2, rows, cols, rows2, rows, cols2]
    scratch += [rows2, rows2, cols, cols2, rows2, cols]
    scratch += [pltpu.VMEM((8, 128), jnp.int32), pltpu.VMEM((8, 128), F32), rows2]
    scratch += [
        pltpu.VMEM((8, 128), F32),
        pltpu.VMEM((nx, 8, 128), F32),
        pltpu.VMEM((8, 128), F32),
        pltpu.VMEM((ny, 8, 128), F32),
        pltpu.VMEM((nx, 2, ROWS, BS), F32),
        pltpu.VMEM((nx, 2, ROWS, BS), F32),
        pltpu.VMEM((nx, 1, ROWS, BS), F32),
        pltpu.VMEM((nx, ITERS + 1, ROWS, BS), F32),
        cols,
        cols,
        cols,
        pltpu.VMEM((8, COLS), F32),
        pltpu.VMEM((nx, 2, 8, BS), F32),
        pltpu.VMEM((nx, 2, 8, BS), F32),
        pltpu.VMEM((nx, ROWS, BS), F32),
        pltpu.VMEM((nx, 2, ROWS, BS), F32),
    ]
    counts = [9, None] + [8] * 6 + [nx, nx, ny, ny] + [nx] * 7
    scratch += [pltpu.SemaphoreType.DMA((n,)) if n else pltpu.SemaphoreType.DMA for n in counts]
    anywhere = pl.BlockSpec(memory_space=pl.ANY)
    hbm = pl.BlockSpec(memory_space=pltpu.HBM)
    return pl.pallas_call(
        functools.partial(kernel, nx, ny, levels),
        out_shape=(
            jax.ShapeDtypeStruct(tracer.shape, F32),
            jax.ShapeDtypeStruct((2, ROWS, nx * BS), F32),
        ),
        in_specs=[hbm] * 7,
        out_specs=(anywhere, anywhere),
        scratch_shapes=scratch,
        compiler_params=pltpu.CompilerParams(
            collective_id=0, has_side_effects=True, vmem_limit_bytes=32 * 1024 * 1024
        ),
    )(*[pltpu.with_memory_space_constraint(x, pltpu.HBM) for x in (tracer, u_east, v_north, kmt, dest, dz, wind)])


def solution(mesh):
    in_specs = (
        P(None, "by", "bx"),
        P(None, "by", "bx"),
        P(None, "by", "bx"),
        P("by", "bx"),
        P("by", "bx"),
        P(),
        P("by", "bx"),
    )
    out_specs = (P(None, "by", "bx"), P(None, "by", "bx"))
    return jax.shard_map(
        on_device, mesh=mesh, in_specs=in_specs, out_specs=out_specs, check_vma=False
    )
```

```python
import functools

import jax
import jax.numpy as jnp
from jax import lax
from jax.experimental import pallas as pl
from jax.experimental.pallas import tpu as pltpu
from jax.sharding import PartitionSpec as P

BS = 128
ITERS = 4
KAPPA = 0.12
SIGMA = 0.2
CENTRE = 1.0 / 3.0
HALF = 2.0 / 3.0
MESH = pl.DeviceIdType.MESH
ROWS = 64
COLS = 512
XR = ROWS + 8
XC = COLS + 128
STRIPS = ROWS // 8
F32 = jnp.float32
SIDES = ((0, 1), (0, -1), (1, 0), (-1, 0), (1, 1), (-1, 1), (1, -1), (-1, -1))


def strip(r):
    return pl.ds(8 * r, 8)


def rim(ref, side):
    dx, dy = SIDES[side]
    rows = {1: pl.ds(ROWS - 8, 8), -1: pl.ds(0, 8), 0: pl.ds(0, ROWS)}[dy]
    cols = {1: pl.ds(COLS - 128, 128), -1: pl.ds(0, 128), 0: pl.ds(0, COLS)}[dx]
    return ref.at[rows, cols]


def pack_ends(ext):
    lane = lax.broadcasted_iota(jnp.int32, (8, 128), 1)
    packed = jnp.zeros((8, 128), ext.dtype)
    for r in range(STRIPS):
        both = jnp.where(lane < 64, ext[strip(r), 0:128], ext[strip(r), COLS - 128 : COLS])
        both = pltpu.roll(both, 16 * r, 1) if r else both
        packed = jnp.where(((lane + 8) & 127) >> 4 == r, both, packed)
    return packed


def extend(ext, rims):
    from_s, from_n, from_w, from_e, from_sw, from_se, from_nw, from_ne = rims
    low = lax.broadcasted_iota(jnp.int32, (8, COLS), 0) < 4
    ext[ROWS:XR, 0:COLS] = jnp.where(low, from_n[...], from_s[...])
    lane = lax.broadcasted_iota(jnp.int32, (8, 128), 1)
    ends = jnp.where(((lane + 8) & 15) < 8, from_w[...], from_e[...])
    for r in range(STRIPS):
        ext[strip(r), COLS:XC] = pltpu.roll(ends, 128 - 16 * r, 1) if r else ends
    east8 = lane < 64
    low8 = lax.broadcasted_iota(jnp.int32, (8, 128), 0) < 4
    ext[ROWS:XR, COLS:XC] = jnp.where(
        low8,
        jnp.where(east8, from_ne[...], from_nw[...]),
        jnp.where(east8, from_se[...], from_sw[...]),
    )


def spread_rows(get, count, wrap=True):
    x = [get(r) for r in range(count)]
    sub = lax.broadcasted_iota(jnp.int32, x[0].shape, 0)
    up = [pltpu.roll(v, 7, 0) for v in x]
    down = [pltpu.roll(v, 1, 0) for v in x]
    out = []
    for r in range(count):
        north = jnp.where(sub == 7, up[(r + 1) % count] if wrap or r + 1 < count else 0.0, up[r])
        south = jnp.where(sub == 0, down[r - 1] if wrap or r else 0.0, down[r])
        out.append(x[r] + x[r] + (north + south))
    return out


def spread_cols(v):
    return v + v + (pltpu.roll(v, 1, 1) + pltpu.roll(v, XC - 1, 1))


def kernel(
    nx,
    ny,
    levels,
    tracer,
    u_east,
    v_north,
    kmt,
    dest_in,
    dz_in,
    wind,
    tracer_out,
    barotropic,
    c0,
    u0,
    v0,
    c1,
    c2,
    k_x,
    ke,
    kn,
    rhs,
    ae,
    be,
    an,
    bn,
    depth,
    inv,
    diag,
    basis,
    dest,
    dz,
    zrim_row,
    zrim_col,
    zrim_corner,
    krim_row,
    krim_col,
    krim_corner,
    up_send,
    dn_send,
    col_send,
    up_recv,
    dn_recv,
    col_recv,
    rows1,
    rows1_recv,
    cols1,
    cols1_recv,
    rows_own,
    cols_own,
    kends,
    zends,
    row_flux,
    part,
    sums_x,
    part2,
    sums_y,
    still_out,
    still,
    first_out,
    slots,
    ring_d,
    edge_d,
    edge_s,
    edge_rows,
    edges_out,
    edges,
    edge_rows0,
    edges0_out,
    edges0,
    full,
    stage,
    load_sem,
    out_sem,
    ks,
    kr,
    rs,
    rr,
    zs,
    zr,
    xs,
    xr,
    ys,
    yr,
    ds,
    dr,
    fs,
    fr,
    es,
    er,
    gs,
    gr,
    last_sem,
):
    mx = lax.axis_index("bx")
    my = lax.axis_index("by")
    pending, pending_rims = [], []

    def peer(dx, dy):
        return (lax.rem(mx + dx + nx, nx), lax.rem(my + dy + ny, ny))

    def send(src, dst, send_sem, recv_sem, dx, dy):
        copy = pltpu.make_async_remote_copy(
            src_ref=src, dst_ref=dst, send_sem=send_sem, recv_sem=recv_sem, device_id=peer(dx, dy), device_id_type=MESH
        )
        copy.start()
        pending.append(copy)
        return copy

    def send_rim(src, dst, send_sem, recv_sem, dx, dy):
        copy = pltpu.make_async_remote_copy(
            src_ref=src, dst_ref=dst, send_sem=send_sem, recv_sem=recv_sem, device_id=peer(dx, dy), device_id_type=MESH
        )
        goes, comes = {1: (has_n, has_s), -1: (has_s, has_n), 0: (None, None)}[dy]

        def guarded(action, guard):
            action() if guard is None else pl.when(guard)(action)

        guarded(copy.start, goes)
        pending_rims.append(lambda: guarded(copy.wait_send, goes))
        return lambda: guarded(copy.wait_recv, comes)

    has_n, has_s = my < ny - 1, my > 0
    barrier = pltpu.get_barrier_semaphore()

    def greet(dx, dy):
        pl.semaphore_signal(barrier, inc=1, device_id=peer(dx, dy), device_id_type=MESH)

    for off in sorted(range(1, ny), key=lambda o: -min(o, ny - o)):
        greet(0, off)
    for off in sorted(range(1, nx), key=lambda o: -min(o, nx - o)):
        greet(off, 0)
    for dx, dy in SIDES[4:]:
        pl.when(has_n if dy == 1 else has_s)(functools.partial(greet, dx, dy))
    n_peers = nx - 1 + ny - 1 + jnp.where(has_n, 2, 0) + jnp.where(has_s, 2, 0)

    last_cols = (slice(None), slice(None), pl.ds(COLS - 128, 128))
    other_cols = (slice(None), slice(None), pl.ds(0, COLS - 128))
    last_rows = (slice(None), pl.ds(ROWS - 8, 8))
    other_rows = (slice(None), pl.ds(0, ROWS - 8))
    loads = [
        pltpu.make_async_copy(kmt, k_x.at[pl.ds(0, ROWS), pl.ds(0, COLS)], load_sem.at[0]),
        pltpu.make_async_copy(dest_in, dest, load_sem.at[1]),
        pltpu.make_async_copy(dz_in, dz, load_sem.at[2]),
        pltpu.make_async_copy(tracer, c0, load_sem.at[3]),
        pltpu.make_async_copy(u_east.at[last_cols], u0.at[last_cols], load_sem.at[4]),
        pltpu.make_async_copy(v_north.at[last_rows], v0.at[last_rows], load_sem.at[5]),
        pltpu.make_async_copy(u_east.at[other_cols], u0.at[other_cols], load_sem.at[6]),
        pltpu.make_async_copy(v_north.at[other_rows], v0.at[other_rows], load_sem.at[7]),
        pltpu.make_async_copy(wind, rhs, load_sem.at[8]),
    ]
    for copy in loads:
        copy.start()

    def no_rim(at, corners):
        zrim_row[at] = jnp.zeros((8, COLS), F32)
        krim_row[at] = jnp.zeros((8, COLS), jnp.int32)
        for i in corners:
            zrim_corner[i] = jnp.zeros((8, 128), F32)
            krim_corner[i] = jnp.zeros((8, 128), jnp.int32)

    pl.when(jnp.logical_not(has_s))(lambda: no_rim(0, (0, 1)))
    pl.when(jnp.logical_not(has_n))(lambda: no_rim(1, (2, 3)))

    loads[0].wait()
    sub = lax.broadcasted_iota(jnp.int32, (8, COLS), 0)
    lane_row = lax.broadcasted_iota(jnp.int32, (8, COLS), 1)
    k_up = [pltpu.roll(k_x[strip(r), 0:COLS], 7, 0) for r in range(STRIPS)]
    for r in range(STRIPS):
        here = k_x[strip(r), 0:COLS]
        east = jnp.where(lane_row == COLS - 1, 0, pltpu.roll(here, COLS - 1, 1))
        north = jnp.where(sub == 7, k_up[r + 1] if r + 1 < STRIPS else 0, k_up[r])
        ke[strip(r), :] = jnp.minimum(here, east)
        kn[strip(r), :] = jnp.minimum(here, north)
    for copy in loads[1:6]:
        copy.wait()

    lane = lax.broadcasted_iota(jnp.int32, (ROWS, 128), 1)
    west = lane < 64
    group = ((lane + 4) & 127) >> 3
    slot = ((lane + 4) & 7) - 4

    def ends(field, k):
        return jnp.where(west, field[k, :, 0:128], field[k, :, COLS - 128 : COLS])

    def turned(value, lanes):
        return pltpu.roll(value, lanes % 128, 1) if lanes % 128 else value

    packed = jnp.zeros((ROWS, 128), F32)
    for k in range(levels):
        up_send[0, k : k + 1, :] = c0[k, ROWS - 1 : ROWS, :]
        up_send[1, k : k + 1, :] = v0[k, ROWS - 1 : ROWS, :]
        dn_send[k : k + 1, :] = c0[k, 0:1, :]
        both = jnp.where(slot == -2, turned(u0[k, :, COLS - 128 : COLS], 8 * k - 1), turned(ends(c0, k), 8 * k))
        packed = jnp.where(group == k, both, packed)
    col_send[...] = packed
    pl.semaphore_wait(barrier, n_peers)
    from_s = send_rim(up_send, up_recv, rs.at[0], rr.at[0], 0, 1)
    from_n = send_rim(dn_send, dn_recv, rs.at[1], rr.at[1], 0, -1)
    from_w = send_rim(col_send, col_recv.at[0], rs.at[2], rr.at[2], 1, 0)
    from_e = send_rim(col_send, col_recv.at[1], rs.at[3], rr.at[3], -1, 0)

    def rim_refs(row, col, corner):
        return [row.at[0], row.at[1], col.at[0], col.at[1]] + [corner.at[i] for i in range(4)]

    k_rims = rim_refs(krim_row, krim_col, krim_corner)
    kends[...] = pack_ends(k_x)
    k_sends = [
        send_rim(kends if SIDES[s][1] == 0 else rim(kmt, s), k_rims[s], ks.at[s], kr.at[s], *SIDES[s]) for s in range(8)
    ]

    def advance(get, k, put):
        def north_flux(r, c, up, nxt):
            return an[k, strip(r), :] * c + bn[k, strip(r), :] * jnp.where(sub == 7, nxt, up)

        below = jnp.zeros((8, COLS), F32)
        c, up = get(0), pltpu.roll(get(0), 7, 0)
        for r in range(STRIPS):
            if r + 1 < STRIPS:
                c_next = get(r + 1)
                up_next = pltpu.roll(c_next, 7, 0)
            flux = north_flux(r, c, up, up_next)
            down = pltpu.roll(flux, 1, 0)
            flux_e = ae[k, strip(r), :] * c + be[k, strip(r), :] * pltpu.roll(c, COLS - 1, 1)
            spread = flux_e - pltpu.roll(flux_e, 1, 1)
            spread = spread + (flux - jnp.where(sub == 0, below, down))
            put(r, c - spread)
            below, c, up = down, c_next, up_next

    def first_step(k, carry):
        for r in range(STRIPS):
            half_u, half_v = 0.5 * u0[k, strip(r), :], 0.5 * v0[k, strip(r), :]
            wet_e, wet_n = ke[strip(r), :] > k, kn[strip(r), :] > k
            ae[k, strip(r), :] = jnp.where(wet_e, half_u + KAPPA, 0.0)
            be[k, strip(r), :] = jnp.where(wet_e, half_u - KAPPA, 0.0)
            an[k, strip(r), :] = jnp.where(wet_n, half_v + KAPPA, 0.0)
            bn[k, strip(r), :] = jnp.where(wet_n, half_v - KAPPA, 0.0)

        def put(r, value):
            c1[k, strip(r), :] = value

        advance(lambda r: c0[k, strip(r), :], k, put)
        return carry

    for copy in loads[6:]:
        copy.wait()
    lax.fori_loop(0, levels, first_step, 0)
    packed = jnp.zeros((ROWS, 128), F32)
    for k in range(levels):
        rows_own[0, k : k + 1, :] = c1[k, ROWS - 1 : ROWS, :]
        rows_own[1, k : k + 1, :] = c1[k, 0:1, :]
        packed = jnp.where(group == k, turned(ends(c1, k), 8 * k), packed)
    cols_own[...] = packed

    for arrival in k_sends:
        arrival()
    extend(k_x, k_rims)
    level16 = lax.broadcasted_iota(jnp.int32, (levels, COLS), 0)
    wet_n = jnp.minimum(k_x[ROWS - 1 : ROWS, 0:COLS], k_x[ROWS : ROWS + 1, 0:COLS]) > level16
    wet_s = jnp.minimum(k_x[0:1, 0:COLS], k_x[XR - 1 : XR, 0:COLS]) > level16
    wet_e = jnp.minimum(k_x[0:ROWS, COLS - 1 : COLS], k_x[0:ROWS, COLS : COLS + 1]) > group
    wet_w = jnp.minimum(k_x[0:ROWS, 0:1], k_x[0:ROWS, XC - 1 : XC]) > group

    def face(velocity, here, there, wet):
        half = 0.5 * velocity
        return jnp.where(wet, (half + KAPPA) * here + (half - KAPPA) * there, 0.0)

    def rim_rows(north_row, south_row, own_north, own_south):
        row_flux[0] = face(up_send[1], own_north, north_row, wet_n)
        row_flux[1] = face(up_recv[1], south_row, own_south, wet_s)

    def rim_cols(own, westward, eastward):
        out = face(turned(col_send[...], 1), own, turned(eastward, -1), wet_e)
        into = face(turned(col_recv[0], 2), turned(westward, 1), own, wet_w)
        return jnp.where(slot == -1, -out, jnp.where(slot == 0, into, 0.0))

    for arrival in (from_s, from_n, from_w, from_e):
        arrival()
    rim_rows(dn_recv[...], up_recv[0], up_send[0], dn_send[...])
    flux_cols = rim_cols(col_send[...], col_recv[0], col_recv[1])

    def correct(field, k, flux):
        change = turned(flux, -8 * k)
        field[k, :, 0:128] = field[k, :, 0:128] + jnp.where(lane == 0, change, 0.0)
        field[k, :, COLS - 128 : COLS] = field[k, :, COLS - 128 : COLS] + jnp.where(lane == 127, change, 0.0)
        field[k, 0:1, :] = field[k, 0:1, :] + row_flux[1, k : k + 1, :]
        field[k, ROWS - 1 : ROWS, :] = field[k, ROWS - 1 : ROWS, :] - row_flux[0, k : k + 1, :]

    lane16 = lax.broadcasted_iota(jnp.int32, (levels, 128), 1)
    level8 = 8 * level16[:, 0:128]
    on_west, on_east = lane16 == level8, lane16 == ((level8 + 127) & 127)
    for at, row, sign in ((0, ROWS - 1, -1.0), (1, 0, 1.0)):
        line = jnp.broadcast_to(flux_cols[row : row + 1, :], (levels, 128))
        from_west = jnp.sum(jnp.where(on_west, line, 0.0), axis=1, keepdims=True)
        from_east = jnp.sum(jnp.where(on_east, line, 0.0), axis=1, keepdims=True)
        change = sign * row_flux[at]
        value = rows_own[at] + change
        rows1[at, :, 0:128] = value[:, 0:128] + jnp.where(lane16 == 0, from_west, 0.0)
        rows1[at, :, 128 : COLS - 128] = value[:, 128 : COLS - 128]
        rows1[at, :, COLS - 128 : COLS] = value[:, COLS - 128 : COLS] + jnp.where(lane16 == 127, from_east, 0.0)
        corner = jnp.where(on_west, change[:, 0:1], 0.0) + jnp.where(on_east, change[:, COLS - 1 : COLS], 0.0)
        cols_own[row : row + 1, :] = cols_own[row : row + 1, :] + jnp.sum(corner, axis=0, keepdims=True)
    cols1[...] = cols_own[...] + flux_cols
    from_s = send_rim(rows1.at[0], rows1_recv.at[0], rs.at[4], rr.at[4], 0, 1)
    from_n = send_rim(rows1.at[1], rows1_recv.at[1], rs.at[5], rr.at[5], 0, -1)
    from_w = send_rim(cols1, cols1_recv.at[0], rs.at[6], rr.at[6], 1, 0)
    from_e = send_rim(cols1, cols1_recv.at[1], rs.at[7], rr.at[7], -1, 0)
    for k in range(levels):
        correct(c1, k, flux_cols)

    subx = lax.broadcasted_iota(jnp.int32, (8, XC), 0)
    for r in range(STRIPS + 1):
        here = k_x[strip(r), :]
        total = jnp.zeros((8, XC), F32)
        for k in range(levels):
            total = total + jnp.where(here > k, dz[k], 0.0)
        depth[strip(r), :] = total

    def ocean_of(r):
        return jnp.where(k_x[strip(r), :] > 0, 1.0, 0.0).astype(F32)

    rows_o = spread_rows(ocean_of, STRIPS + 1)
    rows_d = spread_rows(lambda r: depth[strip(r), :], STRIPS + 1)
    for r in range(STRIPS + 1):
        d = depth[strip(r), :]
        o = ocean_of(r)
        total = d * spread_cols(rows_o[r]) + spread_cols(rows_d[r]) - 8.0 * d
        whole = SIGMA + 0.25 * o * total
        diag[strip(r), :] = whole
        inv[strip(r), :] = o / whole

    blocks = COLS // BS

    def scatter(get, parts, outbox, inbox, ssem, rsem):
        copies = []
        for off in sorted(range(nx), key=lambda o: -min(o, nx - o)):
            target = lax.rem(mx + off, nx)
            hits = [dest[0, m] == target for m in range(blocks)]
            here = outbox.at[off] if off else inbox(0)
            for i in range(parts):
                chosen = None
                for m in range(blocks):
                    piece = get(m, i)
                    chosen = jnp.where(hits[m], piece, jnp.zeros_like(piece) if chosen is None else chosen)
                here[i] = chosen
            if off:
                copies.append(send(outbox.at[off], inbox(off), ssem.at[off], rsem.at[off], off, 0))
        return copies

    def block(m):
        return pl.ds(m * BS, BS)

    still_copies = scatter(
        lambda m, i: depth[0:ROWS, block(m)], 1, still_out, lambda off: still.at[off, pl.ds(0, 1)], ds, dr
    )

    lane8 = lax.broadcasted_iota(jnp.int32, (8, BS), 1)

    def pack(both):
        packed = jnp.zeros((8, BS), F32)
        for m in range(blocks):
            packed = jnp.where(((lane8 + 8) & 127) >> 4 == m, turned(both[m], 16 * m), packed)
        return packed

    def tiles(ref, r):
        return [ref[strip(r), block(m)] for m in range(blocks + 1)]

    def pack_ring(tile):
        return pack([jnp.where(lane8 < 64, tile[m + 1], tile[m - 1]) for m in range(blocks)])

    def pack_edges(tile):
        return pack([jnp.where(lane8 == 0, turned(tile[m], 1), turned(tile[m], -1)) for m in range(blocks)])

    for r in range(STRIPS):
        ring_d[strip(r), :] = pack_ring(tiles(depth, r))
        edge_d[strip(r), :] = pack_edges(tiles(depth, r))
        edge_s[strip(r), :] = (0.25 / HALF) * pack_edges(tiles(inv, r))

    def edge_columns(step, ring_x, ring_dx, scale, cols_m):
        inner_x = spread_rows(lambda r: ring_x[r], STRIPS, False)
        inner_dx = spread_rows(lambda r: ring_dx[r], STRIPS, False)
        for r in range(STRIPS):
            edge = scale(r) * (edge_d[strip(r), :] * inner_x[r] + inner_dx[r])
            for m in range(blocks):
                moved = turned(edge, 16 * r + 2 * step + 1 - 16 * m)
                cols_m[m] = jnp.where((lane8 >> 1) == 8 * r + step, moved, cols_m[m])

    def edge_lines(step, x, dx, scale, out_rows):
        beyond_x, beyond_dx = spread_cols(x), spread_cols(dx)
        for row, out, at in ((ROWS - 1, 0, 0), (0, 7, 1)):
            edge = scale(row) * (depth[row : row + 1, :] * beyond_x[out : out + 1] + beyond_dx[out : out + 1])
            out_rows[2 * step + at : 2 * step + at + 1, :] = edge[:, 0:COLS]

    def swapped(value):
        return jnp.where((lane8 & 1) == 1, turned(value, 1), turned(value, -1))

    def one_if(wet):
        return jnp.where(wet, 1.0, 0.0).astype(F32)

    ring_0 = [ring_d[strip(r), :] for r in range(STRIPS)]
    edge_cols = [jnp.zeros((8, BS), F32) for _ in range(blocks)]
    edge_columns(
        0, [one_if(v > 0.0) for v in ring_0], ring_0, lambda r: 0.25 * one_if(edge_d[strip(r), :] > 0.0), edge_cols
    )
    edge_rows0[...] = jnp.zeros((8, COLS), F32)
    edge_lines(
        0,
        ocean_of(STRIPS),
        depth[strip(STRIPS), :],
        lambda row: 0.25 * one_if(depth[row : row + 1, :] > 0.0),
        edge_rows0,
    )
    edge_cols0 = [swapped(v) for v in edge_cols]
    edge0_copies = scatter(
        lambda m, i: edge_cols0[m] if i else edge_rows0[:, block(m)], 2, edges0_out, lambda off: edges0.at[off], gs, gr
    )

    def second_step(k, carry):
        def put(r, value):
            c2[k, strip(r), :] = value
            wet = k_x[strip(r), 0:COLS] > k
            rhs[strip(r), :] = rhs[strip(r), :] + jnp.where(wet, dz[k] * value, 0.0)

        advance(lambda r: c1[k, strip(r), :], k, put)
        return carry

    lax.fori_loop(0, levels, second_step, 0)

    for arrival in (from_s, from_n, from_w, from_e):
        arrival()
    rim_rows(rows1_recv[1], rows1_recv[0], rows1[0], rows1[1])
    flux_cols = rim_cols(cols1[...], cols1_recv[0], cols1_recv[1])
    dz_rows = jnp.zeros((levels, 128), F32)
    dz_cols = jnp.zeros((ROWS, 128), F32)
    for k in range(levels):
        dz_rows = jnp.where(level16[:, 0:128] == k, dz[k], dz_rows)
        dz_cols = jnp.where(group == k, dz[k], dz_cols)
    dz_rows = jnp.concatenate([dz_rows] * (COLS // 128), axis=1)
    weighted = dz_cols * flux_cols
    change_w = jnp.sum(jnp.where(slot == 0, weighted, 0.0), axis=1, keepdims=True)
    change_e = jnp.sum(jnp.where(slot == -1, weighted, 0.0), axis=1, keepdims=True)
    rhs[:, 0:128] = rhs[:, 0:128] + jnp.where(lane == 0, change_w, 0.0)
    rhs[:, COLS - 128 : COLS] = rhs[:, COLS - 128 : COLS] + jnp.where(lane == 127, change_e, 0.0)
    rhs[0:1, :] = rhs[0:1, :] + jnp.sum(dz_rows * row_flux[1], axis=0, keepdims=True)
    rhs[ROWS - 1 : ROWS, :] = rhs[ROWS - 1 : ROWS, :] - jnp.sum(dz_rows * row_flux[0], axis=0, keepdims=True)

    for r in range(STRIPS):
        start = jnp.where(k_x[strip(r), 0:COLS] > 0, rhs[strip(r), :], 0.0)
        basis[0, strip(r), 0:COLS] = start * inv[strip(r), 0:COLS]
    z_rims = rim_refs(zrim_row, zrim_col, zrim_corner)
    zends[...] = pack_ends(basis.at[0])
    z_sends = [
        send_rim(zends if SIDES[s][1] == 0 else rim(basis.at[0], s), z_rims[s], zs.at[s], zr.at[s], *SIDES[s])
        for s in range(8)
    ]
    first_copies = scatter(
        lambda m, i: basis[0, 0:ROWS, block(m)], 1, first_out, lambda off: slots.at[off, pl.ds(0, 1)], fs, fr
    )
    for k in range(levels):
        correct(c2, k, flux_cols)
    write = pltpu.make_async_copy(c2, tracer_out, out_sem)
    write.start()

    for copy in still_copies + edge0_copies:
        copy.wait_recv()
    sub8 = lax.broadcasted_iota(jnp.int32, (8, BS), 0)
    sides = (lane8 == 0) | (lane8 == BS - 1)

    def spread(values):
        out = []
        for v in spread_rows(lambda r: values[r], STRIPS, False):
            east = jnp.where(lane8 == BS - 1, 0.0, pltpu.roll(v, BS - 1, 1))
            out.append(v + v + (east + jnp.where(lane8 == 0, 0.0, pltpu.roll(v, 1, 1))))
        return out

    def with_edges(value, r, step, packet, n):
        value = value + jnp.where(sides, pltpu.roll(packet[n, 1], BS - (16 * r + 2 * step + 1), 1), 0.0)
        if r == STRIPS - 1:
            value = value + jnp.where(sub8 == 7, packet[n, 0, 2 * step : 2 * step + 1, :], 0.0)
        if r == 0:
            value = value + jnp.where(sub8 == 0, packet[n, 0, 2 * step + 1 : 2 * step + 2, :], 0.0)
        return value

    def block_diagonal(n, carry):
        d = [still[n, 0, strip(r), :] for r in range(STRIPS)]
        o = [one_if(v > 0.0) for v in d]
        wide_o, wide_d = spread(o), spread(d)
        for r in range(STRIPS):
            total = d[r] * wide_o[r] + wide_d[r] - 8.0 * d[r]
            whole = with_edges(SIGMA + 0.25 * o[r] * total, r, 0, edges0, n)
            full[n, strip(r), :] = whole
            still[n, 1, strip(r), :] = o[r] / whole
        return carry

    lax.fori_loop(0, nx, block_diagonal, 0)

    for arrival in z_sends:
        arrival()
    extend(basis.at[0], z_rims)

    moments = [jnp.zeros((8, 128), F32) for _ in range(8)]

    def inner_product(i, j):
        total = jnp.zeros((8, 128), F32)
        for r in range(STRIPS):
            product = diag[strip(r), 0:COLS] * basis[i, strip(r), 0:COLS] * basis[j, strip(r), 0:COLS]
            for m in range(COLS // 128):
                total = total + product[:, 128 * m : 128 * (m + 1)]
        return total

    moments[0] = inner_product(0, 0)
    for step in range(ITERS):
        rows_x = spread_rows(lambda r: basis[step, strip(r), :], STRIPS + 1)
        rows_dx = spread_rows(lambda r: depth[strip(r), :] * basis[step, strip(r), :], STRIPS + 1)
        for r in range(STRIPS + 1):
            d, x = depth[strip(r), :], basis[step, strip(r), :]
            image = d * spread_cols(rows_x[r]) + spread_cols(rows_dx[r]) - 8.0 * (d * x)
            scale = (0.25 / HALF) * inv[strip(r), :]
            following = scale * image - (CENTRE / HALF) * x
            if step:
                following = following + following - basis[step - 1, strip(r), :]
            basis[step + 1, strip(r), :] = following
        moments[2 * step + 1] = inner_product(step, step + 1)
        if step < ITERS - 1:
            moments[2 * step + 2] = inner_product(step + 1, step + 1)

    row8 = lax.broadcasted_iota(jnp.int32, (8, 128), 0)
    mine = jnp.zeros((8, 128), F32)
    for m in range(8):
        mine = jnp.where(row8 == m, jnp.sum(moments[m], axis=0, keepdims=True), mine)
    part[...] = mine
    x_sends = [send(part, sums_x.at[off], xs.at[off], xr.at[off], off, 0) for off in range(1, nx)]
    edge_cols = [jnp.zeros((8, BS), F32) for _ in range(blocks)]
    for step in range(ITERS):
        ring_x = [pack_ring(tiles(basis.at[step], r)) for r in range(STRIPS)]
        ring_dx = [ring_d[strip(r), :] * ring_x[r] for r in range(STRIPS)]
        edge_columns(step, ring_x, ring_dx, lambda r: edge_s[strip(r), :], edge_cols)
        x = basis[step, strip(STRIPS), :]
        edge_lines(
            step, x, depth[strip(STRIPS), :] * x, lambda row: (0.25 / HALF) * inv[row : row + 1, :], edge_rows
        )
    edge_cols = [swapped(v) for v in edge_cols]
    edge_copies = scatter(
        lambda m, i: edge_cols[m] if i else edge_rows[:, block(m)], 2, edges_out, lambda off: edges.at[off], es, er
    )
    total = mine
    for off in range(1, nx):
        x_sends[off - 1].wait_recv()
        total = total + sums_x[off]
    part2[...] = total
    y_sends = [send(part2, sums_y.at[off], ys.at[off], yr.at[off], 0, off) for off in range(1, ny)]

    for copy in first_copies + edge_copies:
        copy.wait_recv()

    def repeat(n, carry):
        x = [slots[n, 0, strip(r), :] for r in range(STRIPS)]
        before = x
        for step in range(ITERS):
            dx = [still[n, 0, strip(r), :] * x[r] for r in range(STRIPS)]
            wide_x, wide_dx = spread(x), spread(dx)
            after = []
            for r in range(STRIPS):
                image = still[n, 0, strip(r), :] * wide_x[r] + wide_dx[r] - 8.0 * dx[r]
                following = (0.25 / HALF) * still[n, 1, strip(r), :] * image - (CENTRE / HALF) * x[r]
                following = with_edges(following, r, step, edges, n)
                if step:
                    following = following + following - before[r]
                slots[n, step + 1, strip(r), :] = following
                after.append(following)
            before, x = x, after
        return carry

    lax.fori_loop(0, nx, repeat, 0)

    for off in range(1, ny):
        y_sends[off - 1].wait_recv()
        total = total + sums_y[off]
    total = jnp.sum(total, axis=1, keepdims=True)
    g = [total[m : m + 1, 0:1] for m in range(8)]

    nu = [g[0], g[1]]
    for m in range(2, 8):
        nu.append(g[m] + g[m] - nu[m % 2])
    gram = {}
    for i in range(ITERS):
        for j in range(ITERS + 1):
            gram[i, j] = 0.5 * (nu[i + j] + nu[abs(i - j)]) if i and j else nu[i + j]

    def dot(a, b):
        terms = []
        for i, first_c in enumerate(a):
            inside = None
            for j, second_c in enumerate(b):
                term = gram[min(i, j), max(i, j)] * second_c
                inside = term if inside is None else inside + term
            terms.append(first_c * inside)
        return functools.reduce(lambda p, q: p + q, terms)

    one = jnp.ones((1, 1), F32)
    zero = jnp.zeros((1, 1), F32)
    z, direction, x = [one], [one], [zero] * ITERS
    norm = dot(z, z)
    for step in range(ITERS):
        image = [(1.0 - CENTRE) * v for v in direction] + [zero]
        for i, v in enumerate(direction):
            if i == 0:
                image[1] = image[1] - HALF * v
            else:
                image[i + 1] = image[i + 1] - (0.5 * HALF) * v
                image[i - 1] = image[i - 1] - (0.5 * HALF) * v
        alpha = norm / dot(direction, image)
        for i, v in enumerate(direction):
            x[i] = x[i] + alpha * v
        z = [v - alpha * w for v, w in zip(z + [zero], image)]
        if step < ITERS - 1:
            following = dot(z, z)
            ratio = following / norm
            direction = [v + ratio * w for v, w in zip(z, direction + [zero])]
            norm = following

    results = []
    for n in range(nx):
        for r in range(STRIPS):
            y = [slots[n, i, strip(r), :] for i in range(ITERS + 1)]
            stage[n, 0, strip(r), :] = sum(x[i] * y[i] for i in range(ITERS))
            stage[n, 1, strip(r), :] = full[n, strip(r), :] * sum(z[i] * y[i] for i in range(ITERS + 1))
        place = pl.ds(pl.multiple_of(lax.rem(mx - n + nx, nx) * BS, BS), BS)
        copy = pltpu.make_async_copy(stage.at[n], barotropic.at[:, :, place], last_sem.at[n])
        copy.start()
        results.append(copy)
    for copy in results:
        copy.wait()
    write.wait()
    for copy in pending:
        copy.wait_send()
    for departure in pending_rims:
        departure()


def on_device(tracer, u_east, v_north, kmt, dest, dz, wind):
    nx, ny = lax.axis_size("bx"), lax.axis_size("by")
    levels = tracer.shape[0]
    slab = pltpu.VMEM((levels, ROWS, COLS), F32)
    ext = pltpu.VMEM((XR, XC), F32)
    flat = pltpu.VMEM((ROWS, COLS), F32)
    flat_i = pltpu.VMEM((ROWS, COLS), jnp.int32)
    rows = pltpu.VMEM((levels, COLS), F32)
    rows2 = pltpu.VMEM((2, levels, COLS), F32)
    cols = pltpu.VMEM((ROWS, 128), F32)
    cols2 = pltpu.VMEM((2, ROWS, 128), F32)

    def rims(dtype):
        return [
            pltpu.VMEM((2, 8, COLS), dtype),
            pltpu.VMEM((2, 8, 128), dtype),
            pltpu.VMEM((4, 8, 128), dtype),
        ]

    scratch = [slab] * 5 + [pltpu.VMEM((XR, XC), jnp.int32), flat_i, flat_i, flat] + [slab] * 4
    scratch += [ext, ext, ext, pltpu.VMEM((ITERS + 1, XR, XC), F32)]
    scratch += [pltpu.SMEM(dest.shape, jnp.int32), pltpu.SMEM(dz.shape, F32)]
    scratch += rims(F32) + rims(jnp.int32)
    scratch += [rows2, rows, cols, rows2, rows, cols2]
    scratch += [rows2, rows2, cols, cols2, rows2, cols]
    scratch += [pltpu.VMEM((8, 128), jnp.int32), pltpu.VMEM((8, 128), F32), rows2]
    scratch += [
        pltpu.VMEM((8, 128), F32),
        pltpu.VMEM((nx, 8, 128), F32),
        pltpu.VMEM((8, 128), F32),
        pltpu.VMEM((ny, 8, 128), F32),
        pltpu.VMEM((nx, 1, ROWS, BS), F32),
        pltpu.VMEM((nx, 2, ROWS, BS), F32),
        pltpu.VMEM((nx, 1, ROWS, BS), F32),
        pltpu.VMEM((nx, ITERS + 1, ROWS, BS), F32),
        cols,
        cols,
        cols,
        pltpu.VMEM((8, COLS), F32),
        pltpu.VMEM((nx, 2, 8, BS), F32),
        pltpu.VMEM((nx, 2, 8, BS), F32),
        pltpu.VMEM((8, COLS), F32),
        pltpu.VMEM((nx, 2, 8, BS), F32),
        pltpu.VMEM((nx, 2, 8, BS), F32),
        pltpu.VMEM((nx, ROWS, BS), F32),
        pltpu.VMEM((nx, 2, ROWS, BS), F32),
    ]
    counts = [9, None] + [8] * 6 + [nx, nx, ny, ny] + [nx] * 9
    scratch += [pltpu.SemaphoreType.DMA((n,)) if n else pltpu.SemaphoreType.DMA for n in counts]
    anywhere = pl.BlockSpec(memory_space=pl.ANY)
    hbm = pl.BlockSpec(memory_space=pltpu.HBM)
    return pl.pallas_call(
        functools.partial(kernel, nx, ny, levels),
        out_shape=(
            jax.ShapeDtypeStruct(tracer.shape, F32),
            jax.ShapeDtypeStruct((2, ROWS, nx * BS), F32),
        ),
        in_specs=[hbm] * 7,
        out_specs=(anywhere, anywhere),
        scratch_shapes=scratch,
        compiler_params=pltpu.CompilerParams(
            collective_id=0, has_side_effects=True, vmem_limit_bytes=32 * 1024 * 1024
        ),
    )(*[pltpu.with_memory_space_constraint(x, pltpu.HBM) for x in (tracer, u_east, v_north, kmt, dest, dz, wind)])


def solution(mesh):
    in_specs = (
        P(None, "by", "bx"),
        P(None, "by", "bx"),
        P(None, "by", "bx"),
        P("by", "bx"),
        P("by", "bx"),
        P(),
        P("by", "bx"),
    )
    out_specs = (P(None, "by", "bx"), P(None, "by", "bx"))
    return jax.shard_map(
        on_device, mesh=mesh, in_specs=in_specs, out_specs=out_specs, check_vma=False
    )
```

```python
import functools

import jax
import jax.numpy as jnp
from jax import lax
from jax.experimental import pallas as pl
from jax.experimental.pallas import tpu as pltpu
from jax.sharding import PartitionSpec as P

BS = 128
ITERS = 4
KAPPA = 0.12
SIGMA = 0.2
CENTRE = 1.0 / 3.0
HALF = 2.0 / 3.0
MESH = pl.DeviceIdType.MESH
ROWS = 64
COLS = 512
XR = ROWS + 8
XC = COLS + 128
STRIPS = ROWS // 8
F32 = jnp.float32
SIDES = ((0, 1), (0, -1), (1, 0), (-1, 0), (1, 1), (-1, 1), (1, -1), (-1, -1))


def strip(r):
    return pl.ds(8 * r, 8)


def rim(ref, side):
    dx, dy = SIDES[side]
    rows = {1: pl.ds(ROWS - 8, 8), -1: pl.ds(0, 8), 0: pl.ds(0, ROWS)}[dy]
    cols = {1: pl.ds(COLS - 128, 128), -1: pl.ds(0, 128), 0: pl.ds(0, COLS)}[dx]
    return ref.at[rows, cols]


def pack_ends(ext):
    lane = lax.broadcasted_iota(jnp.int32, (8, 128), 1)
    packed = jnp.zeros((8, 128), ext.dtype)
    for r in range(STRIPS):
        both = jnp.where(lane < 64, ext[strip(r), 0:128], ext[strip(r), COLS - 128 : COLS])
        both = pltpu.roll(both, 16 * r, 1) if r else both
        packed = jnp.where(((lane + 8) & 127) >> 4 == r, both, packed)
    return packed


def extend(ext, rims):
    from_s, from_n, from_w, from_e, from_sw, from_se, from_nw, from_ne = rims
    low = lax.broadcasted_iota(jnp.int32, (8, COLS), 0) < 4
    ext[ROWS:XR, 0:COLS] = jnp.where(low, from_n[...], from_s[...])
    lane = lax.broadcasted_iota(jnp.int32, (8, 128), 1)
    ends = jnp.where(((lane + 8) & 15) < 8, from_w[...], from_e[...])
    for r in range(STRIPS):
        ext[strip(r), COLS:XC] = pltpu.roll(ends, 128 - 16 * r, 1) if r else ends
    east8 = lane < 64
    low8 = lax.broadcasted_iota(jnp.int32, (8, 128), 0) < 4
    ext[ROWS:XR, COLS:XC] = jnp.where(
        low8,
        jnp.where(east8, from_ne[...], from_nw[...]),
        jnp.where(east8, from_se[...], from_sw[...]),
    )


def spread_rows(get, count, wrap=True):
    x = [get(r) for r in range(count)]
    sub = lax.broadcasted_iota(jnp.int32, x[0].shape, 0)
    up = [pltpu.roll(v, 7, 0) for v in x]
    down = [pltpu.roll(v, 1, 0) for v in x]
    out = []
    for r in range(count):
        north = jnp.where(sub == 7, up[(r + 1) % count] if wrap or r + 1 < count else 0.0, up[r])
        south = jnp.where(sub == 0, down[r - 1] if wrap or r else 0.0, down[r])
        out.append(x[r] + x[r] + (north + south))
    return out


def spread_cols(v):
    return v + v + (pltpu.roll(v, 1, 1) + pltpu.roll(v, XC - 1, 1))


def kernel(
    nx,
    ny,
    levels,
    tracer,
    u_east,
    v_north,
    kmt,
    dest_in,
    dz_in,
    wind,
    tracer_out,
    barotropic,
    c0,
    u0,
    v0,
    c1,
    c2,
    k_x,
    ke,
    kn,
    rhs,
    ae,
    be,
    an,
    bn,
    depth,
    inv,
    diag,
    basis,
    dest,
    dz,
    zrim_row,
    zrim_col,
    zrim_corner,
    krim_row,
    krim_col,
    krim_corner,
    up_send,
    dn_send,
    col_send,
    up_recv,
    dn_recv,
    col_recv,
    rows1,
    rows1_recv,
    cols1,
    cols1_recv,
    rows_own,
    cols_own,
    corner_send,
    corner_recv,
    side_recv,
    kends,
    zends,
    row_flux,
    part,
    sums_x,
    part2,
    sums_y,
    still_out,
    still,
    first_out,
    slots,
    ring_d,
    edge_d,
    edge_s,
    edge_rows,
    edges_out,
    edges,
    edge_rows0,
    edges0_out,
    edges0,
    full,
    stage,
    load_sem,
    out_sem,
    ks,
    kr,
    rs,
    rr,
    zs,
    zr,
    xs,
    xr,
    ys,
    yr,
    ds,
    dr,
    fs,
    fr,
    es,
    er,
    gs,
    gr,
    hs,
    hr,
    last_sem,
):
    mx = lax.axis_index("bx")
    my = lax.axis_index("by")
    pending, pending_rims = [], []

    def peer(dx, dy):
        return (lax.rem(mx + dx + nx, nx), lax.rem(my + dy + ny, ny))

    def send(src, dst, send_sem, recv_sem, dx, dy):
        copy = pltpu.make_async_remote_copy(
            src_ref=src, dst_ref=dst, send_sem=send_sem, recv_sem=recv_sem, device_id=peer(dx, dy), device_id_type=MESH
        )
        copy.start()
        pending.append(copy)
        return copy

    def send_rim(src, dst, send_sem, recv_sem, dx, dy):
        copy = pltpu.make_async_remote_copy(
            src_ref=src, dst_ref=dst, send_sem=send_sem, recv_sem=recv_sem, device_id=peer(dx, dy), device_id_type=MESH
        )
        goes, comes = {1: (has_n, has_s), -1: (has_s, has_n), 0: (None, None)}[dy]

        def guarded(action, guard):
            action() if guard is None else pl.when(guard)(action)

        guarded(copy.start, goes)
        pending_rims.append(lambda: guarded(copy.wait_send, goes))
        return lambda: guarded(copy.wait_recv, comes)

    has_n, has_s = my < ny - 1, my > 0
    barrier = pltpu.get_barrier_semaphore()

    def greet(dx, dy):
        pl.semaphore_signal(barrier, inc=1, device_id=peer(dx, dy), device_id_type=MESH)

    for off in sorted(range(1, ny), key=lambda o: -min(o, ny - o)):
        greet(0, off)
    for off in sorted(range(1, nx), key=lambda o: -min(o, nx - o)):
        greet(off, 0)
    for dx, dy in SIDES[4:]:
        pl.when(has_n if dy == 1 else has_s)(functools.partial(greet, dx, dy))
    n_peers = nx - 1 + ny - 1 + jnp.where(has_n, 2, 0) + jnp.where(has_s, 2, 0)

    last_cols = (slice(None), slice(None), pl.ds(COLS - 128, 128))
    other_cols = (slice(None), slice(None), pl.ds(0, COLS - 128))
    last_rows = (slice(None), pl.ds(ROWS - 8, 8))
    other_rows = (slice(None), pl.ds(0, ROWS - 8))
    loads = [
        pltpu.make_async_copy(kmt, k_x.at[pl.ds(0, ROWS), pl.ds(0, COLS)], load_sem.at[0]),
        pltpu.make_async_copy(dest_in, dest, load_sem.at[1]),
        pltpu.make_async_copy(dz_in, dz, load_sem.at[2]),
        pltpu.make_async_copy(tracer, c0, load_sem.at[3]),
        pltpu.make_async_copy(u_east.at[last_cols], u0.at[last_cols], load_sem.at[4]),
        pltpu.make_async_copy(v_north.at[last_rows], v0.at[last_rows], load_sem.at[5]),
        pltpu.make_async_copy(u_east.at[other_cols], u0.at[other_cols], load_sem.at[6]),
        pltpu.make_async_copy(v_north.at[other_rows], v0.at[other_rows], load_sem.at[7]),
        pltpu.make_async_copy(wind, rhs, load_sem.at[8]),
    ]
    for copy in loads:
        copy.start()

    def no_rim(at, corners):
        zrim_row[at] = jnp.zeros((8, COLS), F32)
        krim_row[at] = jnp.zeros((8, COLS), jnp.int32)
        for i in corners:
            zrim_corner[i] = jnp.zeros((8, 128), F32)
            krim_corner[i] = jnp.zeros((8, 128), jnp.int32)

    pl.when(jnp.logical_not(has_s))(lambda: no_rim(0, (0, 1)))
    pl.when(jnp.logical_not(has_n))(lambda: no_rim(1, (2, 3)))

    loads[0].wait()
    sub = lax.broadcasted_iota(jnp.int32, (8, COLS), 0)
    lane_row = lax.broadcasted_iota(jnp.int32, (8, COLS), 1)
    k_up = [pltpu.roll(k_x[strip(r), 0:COLS], 7, 0) for r in range(STRIPS)]
    for r in range(STRIPS):
        here = k_x[strip(r), 0:COLS]
        east = jnp.where(lane_row == COLS - 1, 0, pltpu.roll(here, COLS - 1, 1))
        north = jnp.where(sub == 7, k_up[r + 1] if r + 1 < STRIPS else 0, k_up[r])
        ke[strip(r), :] = jnp.minimum(here, east)
        kn[strip(r), :] = jnp.minimum(here, north)
    for copy in loads[1:6]:
        copy.wait()

    lane = lax.broadcasted_iota(jnp.int32, (ROWS, 128), 1)
    west = lane < 64
    group = ((lane + 4) & 127) >> 3
    slot = ((lane + 4) & 7) - 4

    def ends(field, k):
        return jnp.where(west, field[k, :, 0:128], field[k, :, COLS - 128 : COLS])

    def turned(value, lanes):
        return pltpu.roll(value, lanes % 128, 1) if lanes % 128 else value

    packed = jnp.zeros((ROWS, 128), F32)
    for k in range(levels):
        up_send[0, k : k + 1, :] = c0[k, ROWS - 1 : ROWS, :]
        up_send[1, k : k + 1, :] = v0[k, ROWS - 1 : ROWS, :]
        dn_send[k : k + 1, :] = c0[k, 0:1, :]
        corner_send[0, 2, k : k + 1, :] = u0[k, ROWS - 1 : ROWS, COLS - 128 : COLS]
        corner_send[2, 1, k : k + 1, :] = u0[k, 0:1, COLS - 128 : COLS]
        both = jnp.where(slot == -2, turned(u0[k, :, COLS - 128 : COLS], 8 * k - 1), turned(ends(c0, k), 8 * k))
        packed = jnp.where(group == k, both, packed)
    col_send[...] = packed
    first, last = pl.ds(0, 128), pl.ds(COLS - 128, 128)
    for i, end in enumerate((last, first)):
        corner_send[i, 0] = up_send[0, :, end]
        corner_send[i, 1] = up_send[1, :, end]
        corner_send[2 + i, 0] = dn_send[:, end]
    for i, j in ((1, 2), (2, 2), (3, 1), (3, 2)):
        corner_send[i, j] = jnp.zeros((levels, 128), F32)
    pl.semaphore_wait(barrier, n_peers)
    from_s = send_rim(up_send, up_recv, rs.at[0], rr.at[0], 0, 1)
    from_n = send_rim(dn_send, dn_recv, rs.at[1], rr.at[1], 0, -1)
    from_w = send_rim(col_send, col_recv.at[0], rs.at[2], rr.at[2], 1, 0)
    from_e = send_rim(col_send, col_recv.at[1], rs.at[3], rr.at[3], -1, 0)

    def rim_refs(row, col, corner):
        return [row.at[0], row.at[1], col.at[0], col.at[1]] + [corner.at[i] for i in range(4)]

    k_rims = rim_refs(krim_row, krim_col, krim_corner)
    kends[...] = pack_ends(k_x)
    k_sends = [
        send_rim(kends if SIDES[s][1] == 0 else rim(kmt, s), k_rims[s], ks.at[s], kr.at[s], *SIDES[s]) for s in range(8)
    ]

    corner_sends = [
        send_rim(corner_send.at[i], corner_recv.at[i], hs.at[i], hr.at[i], *SIDES[4 + i]) for i in range(4)
    ]
    for i, (a, b) in enumerate(((0, 2), (2, 1), (0, 1), (1, 1))):
        corner_sends.append(
            send_rim(corner_send.at[a, b], side_recv.at[i], hs.at[4 + i], hr.at[4 + i], *SIDES[i])
        )

    def advance(get, k, put):
        def north_flux(r, c, up, nxt):
            return an[k, strip(r), :] * c + bn[k, strip(r), :] * jnp.where(sub == 7, nxt, up)

        below = jnp.zeros((8, COLS), F32)
        c, up = get(0), pltpu.roll(get(0), 7, 0)
        for r in range(STRIPS):
            if r + 1 < STRIPS:
                c_next = get(r + 1)
                up_next = pltpu.roll(c_next, 7, 0)
            flux = north_flux(r, c, up, up_next)
            down = pltpu.roll(flux, 1, 0)
            flux_e = ae[k, strip(r), :] * c + be[k, strip(r), :] * pltpu.roll(c, COLS - 1, 1)
            spread = flux_e - pltpu.roll(flux_e, 1, 1)
            spread = spread + (flux - jnp.where(sub == 0, below, down))
            put(r, c - spread)
            below, c, up = down, c_next, up_next

    def first_step(k, carry):
        for r in range(STRIPS):
            half_u, half_v = 0.5 * u0[k, strip(r), :], 0.5 * v0[k, strip(r), :]
            wet_e, wet_n = ke[strip(r), :] > k, kn[strip(r), :] > k
            ae[k, strip(r), :] = jnp.where(wet_e, half_u + KAPPA, 0.0)
            be[k, strip(r), :] = jnp.where(wet_e, half_u - KAPPA, 0.0)
            an[k, strip(r), :] = jnp.where(wet_n, half_v + KAPPA, 0.0)
            bn[k, strip(r), :] = jnp.where(wet_n, half_v - KAPPA, 0.0)

        def put(r, value):
            c1[k, strip(r), :] = value

        advance(lambda r: c0[k, strip(r), :], k, put)
        return carry

    for copy in loads[6:]:
        copy.wait()
    lax.fori_loop(0, levels, first_step, 0)
    packed = jnp.zeros((ROWS, 128), F32)
    for k in range(levels):
        rows_own[0, k : k + 1, :] = c1[k, ROWS - 1 : ROWS, :]
        rows_own[1, k : k + 1, :] = c1[k, 0:1, :]
        packed = jnp.where(group == k, turned(ends(c1, k), 8 * k), packed)
    cols_own[...] = packed
    second = [
        send_rim(rows_own.at[0], rows1_recv.at[0], rs.at[4], rr.at[4], 0, 1),
        send_rim(rows_own.at[1], rows1_recv.at[1], rs.at[5], rr.at[5], 0, -1),
        send_rim(cols_own, cols1_recv.at[0], rs.at[6], rr.at[6], 1, 0),
        send_rim(cols_own, cols1_recv.at[1], rs.at[7], rr.at[7], -1, 0),
    ]

    for arrival in k_sends:
        arrival()
    extend(k_x, k_rims)
    level16 = lax.broadcasted_iota(jnp.int32, (levels, COLS), 0)
    wet_n = jnp.minimum(k_x[ROWS - 1 : ROWS, 0:COLS], k_x[ROWS : ROWS + 1, 0:COLS]) > level16
    wet_s = jnp.minimum(k_x[0:1, 0:COLS], k_x[XR - 1 : XR, 0:COLS]) > level16
    wet_e = jnp.minimum(k_x[0:ROWS, COLS - 1 : COLS], k_x[0:ROWS, COLS : COLS + 1]) > group
    wet_w = jnp.minimum(k_x[0:ROWS, 0:1], k_x[0:ROWS, XC - 1 : XC]) > group

    def face(velocity, here, there, wet):
        half = 0.5 * velocity
        return jnp.where(wet, (half + KAPPA) * here + (half - KAPPA) * there, 0.0)

    def rim_rows(north_row, south_row, own_north, own_south):
        row_flux[0] = face(up_send[1], own_north, north_row, wet_n)
        row_flux[1] = face(up_recv[1], south_row, own_south, wet_s)

    def rim_cols(own, westward, eastward):
        out = face(turned(col_send[...], 1), own, turned(eastward, -1), wet_e)
        into = face(turned(col_recv[0], 2), turned(westward, 1), own, wet_w)
        return jnp.where(slot == -1, -out, jnp.where(slot == 0, into, 0.0))

    for arrival in (from_s, from_n, from_w, from_e):
        arrival()
    rim_rows(dn_recv[...], up_recv[0], up_send[0], dn_send[...])
    flux_cols = rim_cols(col_send[...], col_recv[0], col_recv[1])

    def correct(field, k, flux):
        change = turned(flux, -8 * k)
        field[k, :, 0:128] = field[k, :, 0:128] + jnp.where(lane == 0, change, 0.0)
        field[k, :, COLS - 128 : COLS] = field[k, :, COLS - 128 : COLS] + jnp.where(lane == 127, change, 0.0)
        field[k, 0:1, :] = field[k, 0:1, :] + row_flux[1, k : k + 1, :]
        field[k, ROWS - 1 : ROWS, :] = field[k, ROWS - 1 : ROWS, :] - row_flux[0, k : k + 1, :]

    lane16 = lax.broadcasted_iota(jnp.int32, (levels, 128), 1)
    level8 = 8 * level16[:, 0:128]
    cols1[...] = cols_own[...] + flux_cols
    on_west, on_east = lane16 == level8, lane16 == ((level8 + 127) & 127)
    for at, row, sign in ((0, ROWS - 1, -1.0), (1, 0, 1.0)):
        line = jnp.broadcast_to(flux_cols[row : row + 1, :], (levels, 128))
        from_west = jnp.sum(jnp.where(on_west, line, 0.0), axis=1, keepdims=True)
        from_east = jnp.sum(jnp.where(on_east, line, 0.0), axis=1, keepdims=True)
        change = sign * row_flux[at]
        value = rows_own[at] + change
        rows1[at, :, 0:128] = value[:, 0:128] + jnp.where(lane16 == 0, from_west, 0.0)
        rows1[at, :, 128 : COLS - 128] = value[:, 128 : COLS - 128]
        rows1[at, :, COLS - 128 : COLS] = value[:, COLS - 128 : COLS] + jnp.where(lane16 == 127, from_east, 0.0)
        corner = jnp.where(on_west, change[:, 0:1], 0.0) + jnp.where(on_east, change[:, COLS - 1 : COLS], 0.0)
        cols1[row : row + 1, :] = cols1[row : row + 1, :] + jnp.sum(corner, axis=0, keepdims=True)
    for k in range(levels):
        correct(c1, k, flux_cols)

    subx = lax.broadcasted_iota(jnp.int32, (8, XC), 0)
    for r in range(STRIPS + 1):
        here = k_x[strip(r), :]
        total = jnp.zeros((8, XC), F32)
        for k in range(levels):
            total = total + jnp.where(here > k, dz[k], 0.0)
        depth[strip(r), :] = total

    def ocean_of(r):
        return jnp.where(k_x[strip(r), :] > 0, 1.0, 0.0).astype(F32)

    rows_o = spread_rows(ocean_of, STRIPS + 1)
    rows_d = spread_rows(lambda r: depth[strip(r), :], STRIPS + 1)
    for r in range(STRIPS + 1):
        d = depth[strip(r), :]
        o = ocean_of(r)
        total = d * spread_cols(rows_o[r]) + spread_cols(rows_d[r]) - 8.0 * d
        whole = SIGMA + 0.25 * o * total
        diag[strip(r), :] = whole
        inv[strip(r), :] = o / whole

    blocks = COLS // BS

    def scatter(get, parts, outbox, inbox, ssem, rsem):
        copies = []
        for off in sorted(range(nx), key=lambda o: -min(o, nx - o)):
            target = lax.rem(mx + off, nx)
            hits = [dest[0, m] == target for m in range(blocks)]
            here = outbox.at[off] if off else inbox(0)
            for i in range(parts):
                chosen = None
                for m in range(blocks):
                    piece = get(m, i)
                    chosen = jnp.where(hits[m], piece, jnp.zeros_like(piece) if chosen is None else chosen)
                here[i] = chosen
            if off:
                copies.append(send(outbox.at[off], inbox(off), ssem.at[off], rsem.at[off], off, 0))
        return copies

    def block(m):
        return pl.ds(m * BS, BS)

    still_copies = scatter(
        lambda m, i: depth[0:ROWS, block(m)], 1, still_out, lambda off: still.at[off, pl.ds(0, 1)], ds, dr
    )

    lane8 = lax.broadcasted_iota(jnp.int32, (8, BS), 1)

    def pack(both):
        packed = jnp.zeros((8, BS), F32)
        for m in range(blocks):
            packed = jnp.where(((lane8 + 8) & 127) >> 4 == m, turned(both[m], 16 * m), packed)
        return packed

    def tiles(ref, r):
        return [ref[strip(r), block(m)] for m in range(blocks + 1)]

    def pack_ring(tile):
        return pack([jnp.where(lane8 < 64, tile[m + 1], tile[m - 1]) for m in range(blocks)])

    def pack_edges(tile):
        return pack([jnp.where(lane8 == 0, turned(tile[m], 1), turned(tile[m], -1)) for m in range(blocks)])

    for r in range(STRIPS):
        ring_d[strip(r), :] = pack_ring(tiles(depth, r))
        edge_d[strip(r), :] = pack_edges(tiles(depth, r))
        edge_s[strip(r), :] = (0.25 / HALF) * pack_edges(tiles(inv, r))

    def edge_columns(step, ring_x, ring_dx, scale, cols_m):
        inner_x = spread_rows(lambda r: ring_x[r], STRIPS, False)
        inner_dx = spread_rows(lambda r: ring_dx[r], STRIPS, False)
        for r in range(STRIPS):
            edge = scale(r) * (edge_d[strip(r), :] * inner_x[r] + inner_dx[r])
            for m in range(blocks):
                moved = turned(edge, 16 * r + 2 * step + 1 - 16 * m)
                cols_m[m] = jnp.where((lane8 >> 1) == 8 * r + step, moved, cols_m[m])

    def edge_lines(step, x, dx, scale, out_rows):
        beyond_x, beyond_dx = spread_cols(x), spread_cols(dx)
        for row, out, at in ((ROWS - 1, 0, 0), (0, 7, 1)):
            edge = scale(row) * (depth[row : row + 1, :] * beyond_x[out : out + 1] + beyond_dx[out : out + 1])
            out_rows[2 * step + at : 2 * step + at + 1, :] = edge[:, 0:COLS]

    def swapped(value):
        return jnp.where((lane8 & 1) == 1, turned(value, 1), turned(value, -1))

    def one_if(wet):
        return jnp.where(wet, 1.0, 0.0).astype(F32)

    ring_0 = [ring_d[strip(r), :] for r in range(STRIPS)]
    edge_cols = [jnp.zeros((8, BS), F32) for _ in range(blocks)]
    edge_columns(
        0, [one_if(v > 0.0) for v in ring_0], ring_0, lambda r: 0.25 * one_if(edge_d[strip(r), :] > 0.0), edge_cols
    )
    edge_rows0[...] = jnp.zeros((8, COLS), F32)
    edge_lines(
        0,
        ocean_of(STRIPS),
        depth[strip(STRIPS), :],
        lambda row: 0.25 * one_if(depth[row : row + 1, :] > 0.0),
        edge_rows0,
    )
    edge_cols0 = [swapped(v) for v in edge_cols]
    edge0_copies = scatter(
        lambda m, i: edge_cols0[m] if i else edge_rows0[:, block(m)], 2, edges0_out, lambda off: edges0.at[off], gs, gr
    )

    def second_step(k, carry):
        def put(r, value):
            c2[k, strip(r), :] = value
            wet = k_x[strip(r), 0:COLS] > k
            rhs[strip(r), :] = rhs[strip(r), :] + jnp.where(wet, dz[k] * value, 0.0)

        advance(lambda r: c1[k, strip(r), :], k, put)
        return carry

    lax.fori_loop(0, levels, second_step, 0)

    for arrival in second + corner_sends:
        arrival()
    c_s, c_n = up_recv[0], dn_recv[...]
    (c_sw, v_sw, u_sw), (c_se, v_se) = [corner_recv[0, i] for i in range(3)], [corner_recv[1, i] for i in range(2)]
    (c_nw, u_nw), c_ne = [corner_recv[2, i] for i in range(2)], corner_recv[3, 0]
    u_s, u_n, v_w, v_e = [side_recv[i] for i in range(4)]
    south, north, far_w, far_e = XR - 1, ROWS, XC - 1, COLS

    def both_wet(a, b):
        here, there = [k_x[i : i + 1, j : j + 1] for i, j in (a, b)]
        return jnp.minimum(here, there) > level16[:, 0:128]

    def as_rows(line, mask):
        return jnp.sum(jnp.where(mask, jnp.broadcast_to(line, (levels, 128)), 0.0), axis=1, keepdims=True)

    def as_cols(column, mask):
        return jnp.sum(jnp.where(mask, column, 0.0), axis=0, keepdims=True)

    flux_sw = face(turned(u_sw, 1), turned(c_sw, 1), c_s[:, 0:128], both_wet((south, far_w), (south, 0)))
    flux_se = face(u_s, c_s[:, COLS - 128 : COLS], turned(c_se, -1), both_wet((south, COLS - 1), (south, far_e)))
    flux_nw = face(turned(u_nw, 1), turned(c_nw, 1), c_n[:, 0:128], both_wet((north, far_w), (north, 0)))
    flux_ne = face(u_n, c_n[:, COLS - 128 : COLS], turned(c_ne, -1), both_wet((north, COLS - 1), (north, far_e)))

    def with_corners(row, flux_w, flux_e):
        middle = row[:, 128 : COLS - 128]
        west_end = row[:, 0:128] + jnp.where(lane16 == 0, flux_w, 0.0)
        east_end = row[:, COLS - 128 : COLS] - jnp.where(lane16 == 127, flux_e, 0.0)
        return jnp.concatenate([west_end, middle, east_end], axis=1)

    row_s = with_corners(rows1_recv[0] - row_flux[1], flux_sw, flux_se)
    row_n = with_corners(rows1_recv[1] + row_flux[0], flux_nw, flux_ne)

    w_first, w_last = [as_rows(col_recv[0, r : r + 1, :], on_east) for r in (0, ROWS - 1)]
    e_first, e_last = [as_rows(col_recv[1, r : r + 1, :], on_west) for r in (0, ROWS - 1)]
    rise_sw = face(v_sw, c_sw, w_first, both_wet((south, far_w), (0, far_w)))[:, 127:128]
    rise_nw = face(v_w, w_last, c_nw, both_wet((ROWS - 1, far_w), (north, far_w)))[:, 127:128]
    rise_se = face(v_se, c_se, e_first, both_wet((south, far_e), (0, far_e)))[:, 0:1]
    rise_ne = face(v_e, e_last, c_ne, both_wet((ROWS - 1, far_e), (north, far_e)))[:, 0:1]
    row64 = lax.broadcasted_iota(jnp.int32, (ROWS, 128), 0)

    def beyond(arrived, shift, below, above, mask):
        value = arrived - turned(flux_cols, shift)
        value = value + jnp.where(row64 == 0, as_cols(below, mask), 0.0)
        return value - jnp.where(row64 == ROWS - 1, as_cols(above, mask), 0.0)

    col_w = beyond(cols1_recv[0], -1, rise_sw, rise_nw, on_east)
    col_e = beyond(cols1_recv[1], 1, rise_se, rise_ne, on_west)

    rim_rows(row_n, row_s, rows1[0], rows1[1])
    flux_cols = rim_cols(cols1[...], col_w, col_e)
    dz_rows = jnp.zeros((levels, 128), F32)
    dz_cols = jnp.zeros((ROWS, 128), F32)
    for k in range(levels):
        dz_rows = jnp.where(level16[:, 0:128] == k, dz[k], dz_rows)
        dz_cols = jnp.where(group == k, dz[k], dz_cols)
    dz_rows = jnp.concatenate([dz_rows] * (COLS // 128), axis=1)
    weighted = dz_cols * flux_cols
    change_w = jnp.sum(jnp.where(slot == 0, weighted, 0.0), axis=1, keepdims=True)
    change_e = jnp.sum(jnp.where(slot == -1, weighted, 0.0), axis=1, keepdims=True)
    rhs[:, 0:128] = rhs[:, 0:128] + jnp.where(lane == 0, change_w, 0.0)
    rhs[:, COLS - 128 : COLS] = rhs[:, COLS - 128 : COLS] + jnp.where(lane == 127, change_e, 0.0)
    rhs[0:1, :] = rhs[0:1, :] + jnp.sum(dz_rows * row_flux[1], axis=0, keepdims=True)
    rhs[ROWS - 1 : ROWS, :] = rhs[ROWS - 1 : ROWS, :] - jnp.sum(dz_rows * row_flux[0], axis=0, keepdims=True)

    for r in range(STRIPS):
        start = jnp.where(k_x[strip(r), 0:COLS] > 0, rhs[strip(r), :], 0.0)
        basis[0, strip(r), 0:COLS] = start * inv[strip(r), 0:COLS]
    z_rims = rim_refs(zrim_row, zrim_col, zrim_corner)
    zends[...] = pack_ends(basis.at[0])
    z_sends = [
        send_rim(zends if SIDES[s][1] == 0 else rim(basis.at[0], s), z_rims[s], zs.at[s], zr.at[s], *SIDES[s])
        for s in range(8)
    ]
    first_copies = scatter(
        lambda m, i: basis[0, 0:ROWS, block(m)], 1, first_out, lambda off: slots.at[off, pl.ds(0, 1)], fs, fr
    )
    for k in range(levels):
        correct(c2, k, flux_cols)
    write = pltpu.make_async_copy(c2, tracer_out, out_sem)
    write.start()

    for copy in still_copies + edge0_copies:
        copy.wait_recv()
    sub8 = lax.broadcasted_iota(jnp.int32, (8, BS), 0)
    sides = (lane8 == 0) | (lane8 == BS - 1)

    def spread(values):
        out = []
        for v in spread_rows(lambda r: values[r], STRIPS, False):
            east = jnp.where(lane8 == BS - 1, 0.0, pltpu.roll(v, BS - 1, 1))
            out.append(v + v + (east + jnp.where(lane8 == 0, 0.0, pltpu.roll(v, 1, 1))))
        return out

    def with_edges(value, r, step, packet, n):
        value = value + jnp.where(sides, pltpu.roll(packet[n, 1], BS - (16 * r + 2 * step + 1), 1), 0.0)
        if r == STRIPS - 1:
            value = value + jnp.where(sub8 == 7, packet[n, 0, 2 * step : 2 * step + 1, :], 0.0)
        if r == 0:
            value = value + jnp.where(sub8 == 0, packet[n, 0, 2 * step + 1 : 2 * step + 2, :], 0.0)
        return value

    def block_diagonal(n, carry):
        d = [still[n, 0, strip(r), :] for r in range(STRIPS)]
        o = [one_if(v > 0.0) for v in d]
        wide_o, wide_d = spread(o), spread(d)
        for r in range(STRIPS):
            total = d[r] * wide_o[r] + wide_d[r] - 8.0 * d[r]
            whole = with_edges(SIGMA + 0.25 * o[r] * total, r, 0, edges0, n)
            full[n, strip(r), :] = whole
            still[n, 1, strip(r), :] = o[r] / whole
        return carry

    lax.fori_loop(0, nx, block_diagonal, 0)

    for arrival in z_sends:
        arrival()
    extend(basis.at[0], z_rims)

    moments = [jnp.zeros((8, 128), F32) for _ in range(8)]

    def inner_product(i, j):
        total = jnp.zeros((8, 128), F32)
        for r in range(STRIPS):
            product = diag[strip(r), 0:COLS] * basis[i, strip(r), 0:COLS] * basis[j, strip(r), 0:COLS]
            for m in range(COLS // 128):
                total = total + product[:, 128 * m : 128 * (m + 1)]
        return total

    moments[0] = inner_product(0, 0)
    for step in range(ITERS):
        rows_x = spread_rows(lambda r: basis[step, strip(r), :], STRIPS + 1)
        rows_dx = spread_rows(lambda r: depth[strip(r), :] * basis[step, strip(r), :], STRIPS + 1)
        for r in range(STRIPS + 1):
            d, x = depth[strip(r), :], basis[step, strip(r), :]
            image = d * spread_cols(rows_x[r]) + spread_cols(rows_dx[r]) - 8.0 * (d * x)
            scale = (0.25 / HALF) * inv[strip(r), :]
            following = scale * image - (CENTRE / HALF) * x
            if step:
                following = following + following - basis[step - 1, strip(r), :]
            basis[step + 1, strip(r), :] = following
        moments[2 * step + 1] = inner_product(step, step + 1)
        if step < ITERS - 1:
            moments[2 * step + 2] = inner_product(step + 1, step + 1)

    row8 = lax.broadcasted_iota(jnp.int32, (8, 128), 0)
    mine = jnp.zeros((8, 128), F32)
    for m in range(8):
        mine = jnp.where(row8 == m, jnp.sum(moments[m], axis=0, keepdims=True), mine)
    part[...] = mine
    x_sends = [send(part, sums_x.at[off], xs.at[off], xr.at[off], off, 0) for off in range(1, nx)]
    edge_cols = [jnp.zeros((8, BS), F32) for _ in range(blocks)]
    for step in range(ITERS):
        ring_x = [pack_ring(tiles(basis.at[step], r)) for r in range(STRIPS)]
        ring_dx = [ring_d[strip(r), :] * ring_x[r] for r in range(STRIPS)]
        edge_columns(step, ring_x, ring_dx, lambda r: edge_s[strip(r), :], edge_cols)
        x = basis[step, strip(STRIPS), :]
        edge_lines(
            step, x, depth[strip(STRIPS), :] * x, lambda row: (0.25 / HALF) * inv[row : row + 1, :], edge_rows
        )
    edge_cols = [swapped(v) for v in edge_cols]
    edge_copies = scatter(
        lambda m, i: edge_cols[m] if i else edge_rows[:, block(m)], 2, edges_out, lambda off: edges.at[off], es, er
    )
    total = mine
    for off in range(1, nx):
        x_sends[off - 1].wait_recv()
        total = total + sums_x[off]
    part2[...] = total
    y_sends = [send(part2, sums_y.at[off], ys.at[off], yr.at[off], 0, off) for off in range(1, ny)]

    for copy in first_copies + edge_copies:
        copy.wait_recv()

    def repeat(n, carry):
        x = [slots[n, 0, strip(r), :] for r in range(STRIPS)]
        before = x
        for step in range(ITERS):
            dx = [still[n, 0, strip(r), :] * x[r] for r in range(STRIPS)]
            wide_x, wide_dx = spread(x), spread(dx)
            after = []
            for r in range(STRIPS):
                image = still[n, 0, strip(r), :] * wide_x[r] + wide_dx[r] - 8.0 * dx[r]
                following = (0.25 / HALF) * still[n, 1, strip(r), :] * image - (CENTRE / HALF) * x[r]
                following = with_edges(following, r, step, edges, n)
                if step:
                    following = following + following - before[r]
                slots[n, step + 1, strip(r), :] = following
                after.append(following)
            before, x = x, after
        return carry

    lax.fori_loop(0, nx, repeat, 0)

    for off in range(1, ny):
        y_sends[off - 1].wait_recv()
        total = total + sums_y[off]
    total = jnp.sum(total, axis=1, keepdims=True)
    g = [total[m : m + 1, 0:1] for m in range(8)]

    nu = [g[0], g[1]]
    for m in range(2, 8):
        nu.append(g[m] + g[m] - nu[m % 2])
    gram = {}
    for i in range(ITERS):
        for j in range(ITERS + 1):
            gram[i, j] = 0.5 * (nu[i + j] + nu[abs(i - j)]) if i and j else nu[i + j]

    def dot(a, b):
        terms = []
        for i, first_c in enumerate(a):
            inside = None
            for j, second_c in enumerate(b):
                term = gram[min(i, j), max(i, j)] * second_c
                inside = term if inside is None else inside + term
            terms.append(first_c * inside)
        return functools.reduce(lambda p, q: p + q, terms)

    one = jnp.ones((1, 1), F32)
    zero = jnp.zeros((1, 1), F32)
    z, direction, x = [one], [one], [zero] * ITERS
    norm = dot(z, z)
    for step in range(ITERS):
        image = [(1.0 - CENTRE) * v for v in direction] + [zero]
        for i, v in enumerate(direction):
            if i == 0:
                image[1] = image[1] - HALF * v
            else:
                image[i + 1] = image[i + 1] - (0.5 * HALF) * v
                image[i - 1] = image[i - 1] - (0.5 * HALF) * v
        alpha = norm / dot(direction, image)
        for i, v in enumerate(direction):
            x[i] = x[i] + alpha * v
        z = [v - alpha * w for v, w in zip(z + [zero], image)]
        if step < ITERS - 1:
            following = dot(z, z)
            ratio = following / norm
            direction = [v + ratio * w for v, w in zip(z, direction + [zero])]
            norm = following

    results = []
    for n in range(nx):
        for r in range(STRIPS):
            y = [slots[n, i, strip(r), :] for i in range(ITERS + 1)]
            stage[n, 0, strip(r), :] = sum(x[i] * y[i] for i in range(ITERS))
            stage[n, 1, strip(r), :] = full[n, strip(r), :] * sum(z[i] * y[i] for i in range(ITERS + 1))
        place = pl.ds(pl.multiple_of(lax.rem(mx - n + nx, nx) * BS, BS), BS)
        copy = pltpu.make_async_copy(stage.at[n], barotropic.at[:, :, place], last_sem.at[n])
        copy.start()
        results.append(copy)
    for copy in results:
        copy.wait()
    write.wait()
    for copy in pending:
        copy.wait_send()
    for departure in pending_rims:
        departure()


def on_device(tracer, u_east, v_north, kmt, dest, dz, wind):
    nx, ny = lax.axis_size("bx"), lax.axis_size("by")
    levels = tracer.shape[0]
    slab = pltpu.VMEM((levels, ROWS, COLS), F32)
    ext = pltpu.VMEM((XR, XC), F32)
    flat = pltpu.VMEM((ROWS, COLS), F32)
    flat_i = pltpu.VMEM((ROWS, COLS), jnp.int32)
    rows = pltpu.VMEM((levels, COLS), F32)
    rows2 = pltpu.VMEM((2, levels, COLS), F32)
    cols = pltpu.VMEM((ROWS, 128), F32)
    cols2 = pltpu.VMEM((2, ROWS, 128), F32)

    def rims(dtype):
        return [
            pltpu.VMEM((2, 8, COLS), dtype),
            pltpu.VMEM((2, 8, 128), dtype),
            pltpu.VMEM((4, 8, 128), dtype),
        ]

    scratch = [slab] * 5 + [pltpu.VMEM((XR, XC), jnp.int32), flat_i, flat_i, flat] + [slab] * 4
    scratch += [ext, ext, ext, pltpu.VMEM((ITERS + 1, XR, XC), F32)]
    scratch += [pltpu.SMEM(dest.shape, jnp.int32), pltpu.SMEM(dz.shape, F32)]
    scratch += rims(F32) + rims(jnp.int32)
    scratch += [rows2, rows, cols, rows2, rows, cols2]
    scratch += [rows2, rows2, cols, cols2, rows2, cols]
    scratch += [pltpu.VMEM((4, 3, levels, 128), F32)] * 2 + [pltpu.VMEM((4, levels, 128), F32)]
    scratch += [pltpu.VMEM((8, 128), jnp.int32), pltpu.VMEM((8, 128), F32), rows2]
    scratch += [
        pltpu.VMEM((8, 128), F32),
        pltpu.VMEM((nx, 8, 128), F32),
        pltpu.VMEM((8, 128), F32),
        pltpu.VMEM((ny, 8, 128), F32),
        pltpu.VMEM((nx, 1, ROWS, BS), F32),
        pltpu.VMEM((nx, 2, ROWS, BS), F32),
        pltpu.VMEM((nx, 1, ROWS, BS), F32),
        pltpu.VMEM((nx, ITERS + 1, ROWS, BS), F32),
        cols,
        cols,
        cols,
        pltpu.VMEM((8, COLS), F32),
        pltpu.VMEM((nx, 2, 8, BS), F32),
        pltpu.VMEM((nx, 2, 8, BS), F32),
        pltpu.VMEM((8, COLS), F32),
        pltpu.VMEM((nx, 2, 8, BS), F32),
        pltpu.VMEM((nx, 2, 8, BS), F32),
        pltpu.VMEM((nx, ROWS, BS), F32),
        pltpu.VMEM((nx, 2, ROWS, BS), F32),
    ]
    counts = [9, None] + [8] * 6 + [nx, nx, ny, ny] + [nx] * 8 + [8, 8, nx]
    scratch += [pltpu.SemaphoreType.DMA((n,)) if n else pltpu.SemaphoreType.DMA for n in counts]
    anywhere = pl.BlockSpec(memory_space=pl.ANY)
    hbm = pl.BlockSpec(memory_space=pltpu.HBM)
    return pl.pallas_call(
        functools.partial(kernel, nx, ny, levels),
        out_shape=(
            jax.ShapeDtypeStruct(tracer.shape, F32),
            jax.ShapeDtypeStruct((2, ROWS, nx * BS), F32),
        ),
        in_specs=[hbm] * 7,
        out_specs=(anywhere, anywhere),
        scratch_shapes=scratch,
        compiler_params=pltpu.CompilerParams(
            collective_id=0, has_side_effects=True, vmem_limit_bytes=32 * 1024 * 1024
        ),
    )(*[pltpu.with_memory_space_constraint(x, pltpu.HBM) for x in (tracer, u_east, v_north, kmt, dest, dz, wind)])


def solution(mesh):
    in_specs = (
        P(None, "by", "bx"),
        P(None, "by", "bx"),
        P(None, "by", "bx"),
        P("by", "bx"),
        P("by", "bx"),
        P(),
        P("by", "bx"),
    )
    out_specs = (P(None, "by", "bx"), P(None, "by", "bx"))
    return jax.shard_map(
        on_device, mesh=mesh, in_specs=in_specs, out_specs=out_specs, check_vma=False
    )
```

```python
import functools

import jax
import jax.numpy as jnp
from jax import lax
from jax.experimental import pallas as pl
from jax.experimental.pallas import tpu as pltpu
from jax.sharding import PartitionSpec as P

BS = 128
ITERS = 4
KAPPA = 0.12
SIGMA = 0.2
CENTRE = 1.0 / 3.0
HALF = 2.0 / 3.0
MESH = pl.DeviceIdType.MESH
ROWS = 64
COLS = 512
XR = ROWS + 8
XC = COLS + 128
STRIPS = ROWS // 8
F32 = jnp.float32
SIDES = ((0, 1), (0, -1), (1, 0), (-1, 0), (1, 1), (-1, 1), (1, -1), (-1, -1))


def strip(r):
    return pl.ds(8 * r, 8)


def rim(ref, side):
    dx, dy = SIDES[side]
    rows = {1: pl.ds(ROWS - 8, 8), -1: pl.ds(0, 8), 0: pl.ds(0, ROWS)}[dy]
    cols = {1: pl.ds(COLS - 128, 128), -1: pl.ds(0, 128), 0: pl.ds(0, COLS)}[dx]
    return ref.at[rows, cols]


def pack_ends(ext):
    lane = lax.broadcasted_iota(jnp.int32, (8, 128), 1)
    packed = jnp.zeros((8, 128), ext.dtype)
    for r in range(STRIPS):
        both = jnp.where(lane < 64, ext[strip(r), 0:128], ext[strip(r), COLS - 128 : COLS])
        both = pltpu.roll(both, 16 * r, 1) if r else both
        packed = jnp.where(((lane + 8) & 127) >> 4 == r, both, packed)
    return packed


def extend(ext, rims):
    from_s, from_n, from_w, from_e, from_sw, from_se, from_nw, from_ne = rims
    low = lax.broadcasted_iota(jnp.int32, (8, COLS), 0) < 4
    ext[ROWS:XR, 0:COLS] = jnp.where(low, from_n[...], from_s[...])
    lane = lax.broadcasted_iota(jnp.int32, (8, 128), 1)
    ends = jnp.where(((lane + 8) & 15) < 8, from_w[...], from_e[...])
    for r in range(STRIPS):
        ext[strip(r), COLS:XC] = pltpu.roll(ends, 128 - 16 * r, 1) if r else ends
    east8 = lane < 64
    low8 = lax.broadcasted_iota(jnp.int32, (8, 128), 0) < 4
    ext[ROWS:XR, COLS:XC] = jnp.where(
        low8,
        jnp.where(east8, from_ne[...], from_nw[...]),
        jnp.where(east8, from_se[...], from_sw[...]),
    )


def spread_rows(get, count, wrap=True):
    x = [get(r) for r in range(count)]
    sub = lax.broadcasted_iota(jnp.int32, x[0].shape, 0)
    up = [pltpu.roll(v, 7, 0) for v in x]
    down = [pltpu.roll(v, 1, 0) for v in x]
    out = []
    for r in range(count):
        north = jnp.where(sub == 7, up[(r + 1) % count] if wrap or r + 1 < count else 0.0, up[r])
        south = jnp.where(sub == 0, down[r - 1] if wrap or r else 0.0, down[r])
        out.append(x[r] + x[r] + (north + south))
    return out


def spread_cols(v):
    return v + v + (pltpu.roll(v, 1, 1) + pltpu.roll(v, XC - 1, 1))


def kernel(
    nx,
    ny,
    levels,
    tracer,
    u_east,
    v_north,
    kmt,
    dest_in,
    dz_in,
    wind,
    tracer_out,
    barotropic,
    c0,
    u0,
    v0,
    c1,
    k_x,
    ke,
    kn,
    rhs,
    ae,
    be,
    an,
    bn,
    depth,
    depth_e,
    depth_w,
    inv,
    diag,
    basis,
    dest,
    dz,
    zrim_row,
    zrim_col,
    zrim_corner,
    krim_row,
    krim_col,
    krim_corner,
    up_send,
    dn_send,
    col_send,
    up_recv,
    dn_recv,
    col_recv,
    rows1,
    rows1_recv,
    cols1,
    cols1_recv,
    rows_own,
    cols_own,
    kends,
    zends,
    row_flux,
    part,
    sums_x,
    part2,
    sums_y,
    still_out,
    still,
    first_out,
    slots,
    ring_d,
    edge_d,
    edge_s,
    edge_rows,
    edges_out,
    edges,
    edge_rows0,
    edges0_out,
    edges0,
    full,
    load_sem,
    ks,
    kr,
    rs,
    rr,
    zs,
    zr,
    xs,
    xr,
    ys,
    yr,
    ds,
    dr,
    fs,
    fr,
    es,
    er,
    gs,
    gr,
):
    mx = lax.axis_index("bx")
    my = lax.axis_index("by")
    pending, pending_rims = [], []

    def peer(dx, dy):
        return (lax.rem(mx + dx + nx, nx), lax.rem(my + dy + ny, ny))

    def send(src, dst, send_sem, recv_sem, dx, dy):
        copy = pltpu.make_async_remote_copy(
            src_ref=src, dst_ref=dst, send_sem=send_sem, recv_sem=recv_sem, device_id=peer(dx, dy), device_id_type=MESH
        )
        copy.start()
        pending.append(copy)
        return copy

    def send_rim(src, dst, send_sem, recv_sem, dx, dy):
        copy = pltpu.make_async_remote_copy(
            src_ref=src, dst_ref=dst, send_sem=send_sem, recv_sem=recv_sem, device_id=peer(dx, dy), device_id_type=MESH
        )
        goes, comes = {1: (has_n, has_s), -1: (has_s, has_n), 0: (None, None)}[dy]

        def guarded(action, guard):
            action() if guard is None else pl.when(guard)(action)

        guarded(copy.start, goes)
        pending_rims.append(lambda: guarded(copy.wait_send, goes))
        return lambda: guarded(copy.wait_recv, comes)

    has_n, has_s = my < ny - 1, my > 0
    barrier = pltpu.get_barrier_semaphore()

    def greet(dx, dy):
        pl.semaphore_signal(barrier, inc=1, device_id=peer(dx, dy), device_id_type=MESH)

    for off in sorted(range(1, ny), key=lambda o: -min(o, ny - o)):
        greet(0, off)
    for off in sorted(range(1, nx), key=lambda o: -min(o, nx - o)):
        greet(off, 0)
    for dx, dy in SIDES[4:]:
        pl.when(has_n if dy == 1 else has_s)(functools.partial(greet, dx, dy))
    n_peers = nx - 1 + ny - 1 + jnp.where(has_n, 2, 0) + jnp.where(has_s, 2, 0)

    last_cols = (slice(None), slice(None), pl.ds(COLS - 128, 128))
    other_cols = (slice(None), slice(None), pl.ds(0, COLS - 128))
    last_rows = (slice(None), pl.ds(ROWS - 8, 8))
    other_rows = (slice(None), pl.ds(0, ROWS - 8))
    loads = [
        pltpu.make_async_copy(kmt, k_x.at[pl.ds(0, ROWS), pl.ds(0, COLS)], load_sem.at[0]),
        pltpu.make_async_copy(dest_in, dest, load_sem.at[1]),
        pltpu.make_async_copy(dz_in, dz, load_sem.at[2]),
        pltpu.make_async_copy(tracer, c0, load_sem.at[3]),
        pltpu.make_async_copy(u_east.at[last_cols], u0.at[last_cols], load_sem.at[4]),
        pltpu.make_async_copy(v_north.at[last_rows], v0.at[last_rows], load_sem.at[5]),
        pltpu.make_async_copy(u_east.at[other_cols], u0.at[other_cols], load_sem.at[6]),
        pltpu.make_async_copy(v_north.at[other_rows], v0.at[other_rows], load_sem.at[7]),
        pltpu.make_async_copy(wind, rhs, load_sem.at[8]),
    ]
    for copy in loads:
        copy.start()

    def no_rim(at, corners):
        zrim_row[at] = jnp.zeros((8, COLS), F32)
        krim_row[at] = jnp.zeros((8, COLS), jnp.int32)
        for i in corners:
            zrim_corner[i] = jnp.zeros((8, 128), F32)
            krim_corner[i] = jnp.zeros((8, 128), jnp.int32)

    pl.when(jnp.logical_not(has_s))(lambda: no_rim(0, (0, 1)))
    pl.when(jnp.logical_not(has_n))(lambda: no_rim(1, (2, 3)))

    loads[0].wait()
    sub = lax.broadcasted_iota(jnp.int32, (8, COLS), 0)
    lane_row = lax.broadcasted_iota(jnp.int32, (8, COLS), 1)
    k_up = [pltpu.roll(k_x[strip(r), 0:COLS], 7, 0) for r in range(STRIPS)]
    for r in range(STRIPS):
        here = k_x[strip(r), 0:COLS]
        east = jnp.where(lane_row == COLS - 1, 0, pltpu.roll(here, COLS - 1, 1))
        north = jnp.where(sub == 7, k_up[r + 1] if r + 1 < STRIPS else 0, k_up[r])
        ke[strip(r), :] = jnp.minimum(here, east)
        kn[strip(r), :] = jnp.minimum(here, north)
    for copy in loads[1:6]:
        copy.wait()

    lane = lax.broadcasted_iota(jnp.int32, (ROWS, 128), 1)
    west = lane < 64
    group = ((lane + 4) & 127) >> 3
    slot = ((lane + 4) & 7) - 4

    def ends(field, k):
        return jnp.where(west, field[k, :, 0:128], field[k, :, COLS - 128 : COLS])

    def turned(value, lanes):
        return pltpu.roll(value, lanes % 128, 1) if lanes % 128 else value

    packed = jnp.zeros((ROWS, 128), F32)
    for k in range(levels):
        up_send[0, k : k + 1, :] = c0[k, ROWS - 1 : ROWS, :]
        up_send[1, k : k + 1, :] = v0[k, ROWS - 1 : ROWS, :]
        dn_send[k : k + 1, :] = c0[k, 0:1, :]
        both = jnp.where(slot == -2, turned(u0[k, :, COLS - 128 : COLS], 8 * k - 1), turned(ends(c0, k), 8 * k))
        packed = jnp.where(group == k, both, packed)
    col_send[...] = packed
    pl.semaphore_wait(barrier, n_peers)
    from_s = send_rim(up_send, up_recv, rs.at[0], rr.at[0], 0, 1)
    from_n = send_rim(dn_send, dn_recv, rs.at[1], rr.at[1], 0, -1)
    from_w = send_rim(col_send, col_recv.at[0], rs.at[2], rr.at[2], 1, 0)
    from_e = send_rim(col_send, col_recv.at[1], rs.at[3], rr.at[3], -1, 0)

    def rim_refs(row, col, corner):
        return [row.at[0], row.at[1], col.at[0], col.at[1]] + [corner.at[i] for i in range(4)]

    k_rims = rim_refs(krim_row, krim_col, krim_corner)
    kends[...] = pack_ends(k_x)
    k_sends = [
        send_rim(kends if SIDES[s][1] == 0 else rim(kmt, s), k_rims[s], ks.at[s], kr.at[s], *SIDES[s]) for s in range(8)
    ]

    def advance(get, k, put):
        def north_flux(r, c, up, nxt):
            return an[k, strip(r), :] * c + bn[k, strip(r), :] * jnp.where(sub == 7, nxt, up)

        below = jnp.zeros((8, COLS), F32)
        c, up = get(0), pltpu.roll(get(0), 7, 0)
        for r in range(STRIPS):
            if r + 1 < STRIPS:
                c_next = get(r + 1)
                up_next = pltpu.roll(c_next, 7, 0)
            flux = north_flux(r, c, up, up_next)
            down = pltpu.roll(flux, 1, 0)
            flux_e = ae[k, strip(r), :] * c + be[k, strip(r), :] * pltpu.roll(c, COLS - 1, 1)
            spread = flux_e - pltpu.roll(flux_e, 1, 1)
            spread = spread + (flux - jnp.where(sub == 0, below, down))
            put(r, c - spread)
            below, c, up = down, c_next, up_next

    def first_step(k, carry):
        for r in range(STRIPS):
            half_u, half_v = 0.5 * u0[k, strip(r), :], 0.5 * v0[k, strip(r), :]
            wet_e, wet_n = ke[strip(r), :] > k, kn[strip(r), :] > k
            ae[k, strip(r), :] = jnp.where(wet_e, half_u + KAPPA, 0.0)
            be[k, strip(r), :] = jnp.where(wet_e, half_u - KAPPA, 0.0)
            an[k, strip(r), :] = jnp.where(wet_n, half_v + KAPPA, 0.0)
            bn[k, strip(r), :] = jnp.where(wet_n, half_v - KAPPA, 0.0)

        def put(r, value):
            c1[k, strip(r), :] = value

        advance(lambda r: c0[k, strip(r), :], k, put)
        return carry

    for copy in loads[6:]:
        copy.wait()
    lax.fori_loop(0, levels, first_step, 0)
    packed = jnp.zeros((ROWS, 128), F32)
    for k in range(levels):
        rows_own[0, k : k + 1, :] = c1[k, ROWS - 1 : ROWS, :]
        rows_own[1, k : k + 1, :] = c1[k, 0:1, :]
        packed = jnp.where(group == k, turned(ends(c1, k), 8 * k), packed)
    cols_own[...] = packed

    for arrival in k_sends:
        arrival()
    extend(k_x, k_rims)
    level16 = lax.broadcasted_iota(jnp.int32, (levels, COLS), 0)
    wet_n = jnp.minimum(k_x[ROWS - 1 : ROWS, 0:COLS], k_x[ROWS : ROWS + 1, 0:COLS]) > level16
    wet_s = jnp.minimum(k_x[0:1, 0:COLS], k_x[XR - 1 : XR, 0:COLS]) > level16
    wet_e = jnp.minimum(k_x[0:ROWS, COLS - 1 : COLS], k_x[0:ROWS, COLS : COLS + 1]) > group
    wet_w = jnp.minimum(k_x[0:ROWS, 0:1], k_x[0:ROWS, XC - 1 : XC]) > group

    def face(velocity, here, there, wet):
        half = 0.5 * velocity
        return jnp.where(wet, (half + KAPPA) * here + (half - KAPPA) * there, 0.0)

    def rim_rows(north_row, south_row, own_north, own_south):
        row_flux[0] = face(up_send[1], own_north, north_row, wet_n)
        row_flux[1] = face(up_recv[1], south_row, own_south, wet_s)

    def rim_cols(own, westward, eastward):
        out = face(turned(col_send[...], 1), own, turned(eastward, -1), wet_e)
        into = face(turned(col_recv[0], 2), turned(westward, 1), own, wet_w)
        return jnp.where(slot == -1, -out, jnp.where(slot == 0, into, 0.0))

    for arrival in (from_s, from_n, from_w, from_e):
        arrival()
    rim_rows(dn_recv[...], up_recv[0], up_send[0], dn_send[...])
    flux_cols = rim_cols(col_send[...], col_recv[0], col_recv[1])

    def correct(field, k, flux):
        change = turned(flux, -8 * k)
        field[k, :, 0:128] = field[k, :, 0:128] + jnp.where(lane == 0, change, 0.0)
        field[k, :, COLS - 128 : COLS] = field[k, :, COLS - 128 : COLS] + jnp.where(lane == 127, change, 0.0)
        field[k, 0:1, :] = field[k, 0:1, :] + row_flux[1, k : k + 1, :]
        field[k, ROWS - 1 : ROWS, :] = field[k, ROWS - 1 : ROWS, :] - row_flux[0, k : k + 1, :]

    lane16 = lax.broadcasted_iota(jnp.int32, (levels, 128), 1)
    level8 = 8 * level16[:, 0:128]
    on_west, on_east = lane16 == level8, lane16 == ((level8 + 127) & 127)
    for at, row, sign in ((0, ROWS - 1, -1.0), (1, 0, 1.0)):
        line = jnp.broadcast_to(flux_cols[row : row + 1, :], (levels, 128))
        from_west = jnp.sum(jnp.where(on_west, line, 0.0), axis=1, keepdims=True)
        from_east = jnp.sum(jnp.where(on_east, line, 0.0), axis=1, keepdims=True)
        change = sign * row_flux[at]
        value = rows_own[at] + change
        rows1[at, :, 0:128] = value[:, 0:128] + jnp.where(lane16 == 0, from_west, 0.0)
        rows1[at, :, 128 : COLS - 128] = value[:, 128 : COLS - 128]
        rows1[at, :, COLS - 128 : COLS] = value[:, COLS - 128 : COLS] + jnp.where(lane16 == 127, from_east, 0.0)
        corner = jnp.where(on_west, change[:, 0:1], 0.0) + jnp.where(on_east, change[:, COLS - 1 : COLS], 0.0)
        cols_own[row : row + 1, :] = cols_own[row : row + 1, :] + jnp.sum(corner, axis=0, keepdims=True)
    cols1[...] = cols_own[...] + flux_cols
    from_s = send_rim(rows1.at[0], rows1_recv.at[0], rs.at[4], rr.at[4], 0, 1)
    from_n = send_rim(rows1.at[1], rows1_recv.at[1], rs.at[5], rr.at[5], 0, -1)
    from_w = send_rim(cols1, cols1_recv.at[0], rs.at[6], rr.at[6], 1, 0)
    from_e = send_rim(cols1, cols1_recv.at[1], rs.at[7], rr.at[7], -1, 0)
    for k in range(levels):
        correct(c1, k, flux_cols)

    subx = lax.broadcasted_iota(jnp.int32, (8, XC), 0)
    for r in range(STRIPS + 1):
        here = k_x[strip(r), :]
        total = jnp.zeros((8, XC), F32)
        for k in range(levels):
            total = total + jnp.where(here > k, dz[k], 0.0)
        depth[strip(r), :] = total
        depth_e[strip(r), :] = pltpu.roll(total, XC - 1, 1)
        depth_w[strip(r), :] = pltpu.roll(total, 1, 1)

    def ocean_of(r):
        return jnp.where(k_x[strip(r), :] > 0, 1.0, 0.0).astype(F32)

    rows_o = spread_rows(ocean_of, STRIPS + 1)
    rows_d = spread_rows(lambda r: depth[strip(r), :], STRIPS + 1)
    for r in range(STRIPS + 1):
        d = depth[strip(r), :]
        o = ocean_of(r)
        total = d * spread_cols(rows_o[r]) + spread_cols(rows_d[r]) - 8.0 * d
        whole = SIGMA + 0.25 * o * total
        diag[strip(r), :] = whole
        inv[strip(r), :] = o / whole

    blocks = COLS // BS

    def scatter(get, parts, outbox, inbox, ssem, rsem):
        copies = []
        for off in sorted(range(nx), key=lambda o: -min(o, nx - o)):
            target = lax.rem(mx + off, nx)
            hits = [dest[0, m] == target for m in range(blocks)]
            here = outbox.at[off] if off else inbox(0)
            for i in range(parts):
                chosen = None
                for m in range(blocks):
                    piece = get(m, i)
                    chosen = jnp.where(hits[m], piece, jnp.zeros_like(piece) if chosen is None else chosen)
                here[i] = chosen
            if off:
                copies.append(send(outbox.at[off], inbox(off), ssem.at[off], rsem.at[off], off, 0))
        return copies

    def block(m):
        return pl.ds(m * BS, BS)

    still_copies = scatter(
        lambda m, i: depth[0:ROWS, block(m)], 1, still_out, lambda off: still.at[off, pl.ds(0, 1)], ds, dr
    )

    lane8 = lax.broadcasted_iota(jnp.int32, (8, BS), 1)

    def pack(both):
        packed = jnp.zeros((8, BS), F32)
        for m in range(blocks):
            packed = jnp.where(((lane8 + 8) & 127) >> 4 == m, turned(both[m], 16 * m), packed)
        return packed

    def tiles(ref, r):
        return [ref[strip(r), block(m)] for m in range(blocks + 1)]

    def pack_ring(tile):
        return pack([jnp.where(lane8 < 64, tile[m + 1], tile[m - 1]) for m in range(blocks)])

    def pack_edges(tile):
        return pack([jnp.where(lane8 == 0, turned(tile[m], 1), turned(tile[m], -1)) for m in range(blocks)])

    for r in range(STRIPS):
        ring_d[strip(r), :] = pack_ring(tiles(depth, r))
        edge_d[strip(r), :] = pack_edges(tiles(depth, r))
        edge_s[strip(r), :] = (0.25 / HALF) * pack_edges(tiles(inv, r))

    def edge_columns(step, ring_x, ring_dx, scale, cols_m):
        inner_x = spread_rows(lambda r: ring_x[r], STRIPS, False)
        inner_dx = spread_rows(lambda r: ring_dx[r], STRIPS, False)
        for r in range(STRIPS):
            edge = scale(r) * (edge_d[strip(r), :] * inner_x[r] + inner_dx[r])
            for m in range(blocks):
                moved = turned(edge, 16 * r + 2 * step + 1 - 16 * m)
                cols_m[m] = jnp.where((lane8 >> 1) == 8 * r + step, moved, cols_m[m])

    def edge_lines(step, x, dx, scale, out_rows):
        beyond_x, beyond_dx = spread_cols(x), spread_cols(dx)
        for row, out, at in ((ROWS - 1, 0, 0), (0, 7, 1)):
            edge = scale(row) * (depth[row : row + 1, :] * beyond_x[out : out + 1] + beyond_dx[out : out + 1])
            out_rows[2 * step + at : 2 * step + at + 1, :] = edge[:, 0:COLS]

    def swapped(value):
        return jnp.where((lane8 & 1) == 1, turned(value, 1), turned(value, -1))

    def one_if(wet):
        return jnp.where(wet, 1.0, 0.0).astype(F32)

    ring_0 = [ring_d[strip(r), :] for r in range(STRIPS)]
    edge_cols = [jnp.zeros((8, BS), F32) for _ in range(blocks)]
    edge_columns(
        0, [one_if(v > 0.0) for v in ring_0], ring_0, lambda r: 0.25 * one_if(edge_d[strip(r), :] > 0.0), edge_cols
    )
    edge_rows0[...] = jnp.zeros((8, COLS), F32)
    edge_lines(
        0,
        ocean_of(STRIPS),
        depth[strip(STRIPS), :],
        lambda row: 0.25 * one_if(depth[row : row + 1, :] > 0.0),
        edge_rows0,
    )
    edge_cols0 = [swapped(v) for v in edge_cols]
    edge0_copies = scatter(
        lambda m, i: edge_cols0[m] if i else edge_rows0[:, block(m)], 2, edges0_out, lambda off: edges0.at[off], gs, gr
    )

    def second_step(k, carry):
        def put(r, value):
            tracer_out[k, strip(r), :] = value
            wet = k_x[strip(r), 0:COLS] > k
            rhs[strip(r), :] = rhs[strip(r), :] + jnp.where(wet, dz[k] * value, 0.0)

        advance(lambda r: c1[k, strip(r), :], k, put)
        return carry

    lax.fori_loop(0, levels, second_step, 0)

    for arrival in (from_s, from_n, from_w, from_e):
        arrival()
    rim_rows(rows1_recv[1], rows1_recv[0], rows1[0], rows1[1])
    flux_cols = rim_cols(cols1[...], cols1_recv[0], cols1_recv[1])
    dz_rows = jnp.zeros((levels, 128), F32)
    dz_cols = jnp.zeros((ROWS, 128), F32)
    for k in range(levels):
        dz_rows = jnp.where(level16[:, 0:128] == k, dz[k], dz_rows)
        dz_cols = jnp.where(group == k, dz[k], dz_cols)
    dz_rows = jnp.concatenate([dz_rows] * (COLS // 128), axis=1)
    weighted = dz_cols * flux_cols
    change_w = jnp.sum(jnp.where(slot == 0, weighted, 0.0), axis=1, keepdims=True)
    change_e = jnp.sum(jnp.where(slot == -1, weighted, 0.0), axis=1, keepdims=True)
    rhs[:, 0:128] = rhs[:, 0:128] + jnp.where(lane == 0, change_w, 0.0)
    rhs[:, COLS - 128 : COLS] = rhs[:, COLS - 128 : COLS] + jnp.where(lane == 127, change_e, 0.0)
    rhs[0:1, :] = rhs[0:1, :] + jnp.sum(dz_rows * row_flux[1], axis=0, keepdims=True)
    rhs[ROWS - 1 : ROWS, :] = rhs[ROWS - 1 : ROWS, :] - jnp.sum(dz_rows * row_flux[0], axis=0, keepdims=True)

    for r in range(STRIPS):
        start = jnp.where(k_x[strip(r), 0:COLS] > 0, rhs[strip(r), :], 0.0)
        basis[0, strip(r), 0:COLS] = start * inv[strip(r), 0:COLS]
    z_rims = rim_refs(zrim_row, zrim_col, zrim_corner)
    zends[...] = pack_ends(basis.at[0])
    z_sends = [
        send_rim(zends if SIDES[s][1] == 0 else rim(basis.at[0], s), z_rims[s], zs.at[s], zr.at[s], *SIDES[s])
        for s in range(8)
    ]
    first_copies = scatter(
        lambda m, i: basis[0, 0:ROWS, block(m)], 1, first_out, lambda off: slots.at[off, pl.ds(0, 1)], fs, fr
    )
    for k in range(levels):
        correct(tracer_out, k, flux_cols)

    for copy in still_copies + edge0_copies:
        copy.wait_recv()
    sub8 = lax.broadcasted_iota(jnp.int32, (8, BS), 0)
    sides = (lane8 == 0) | (lane8 == BS - 1)

    def spread(values):
        out = []
        for v in spread_rows(lambda r: values[r], STRIPS, False):
            east = jnp.where(lane8 == BS - 1, 0.0, pltpu.roll(v, BS - 1, 1))
            out.append(v + v + (east + jnp.where(lane8 == 0, 0.0, pltpu.roll(v, 1, 1))))
        return out

    def with_edges(value, r, step, packet, n):
        value = value + jnp.where(sides, pltpu.roll(packet[n, 1], BS - (16 * r + 2 * step + 1), 1), 0.0)
        if r == STRIPS - 1:
            value = value + jnp.where(sub8 == 7, packet[n, 0, 2 * step : 2 * step + 1, :], 0.0)
        if r == 0:
            value = value + jnp.where(sub8 == 0, packet[n, 0, 2 * step + 1 : 2 * step + 2, :], 0.0)
        return value

    def block_diagonal(n, carry):
        d = [still[n, 0, strip(r), :] for r in range(STRIPS)]
        o = [one_if(v > 0.0) for v in d]
        wide_o, wide_d = spread(o), spread(d)
        for r in range(STRIPS):
            total = d[r] * wide_o[r] + wide_d[r] - 8.0 * d[r]
            whole = with_edges(SIGMA + 0.25 * o[r] * total, r, 0, edges0, n)
            full[n, strip(r), :] = whole
            still[n, 1, strip(r), :] = o[r] / whole
        return carry

    lax.fori_loop(0, nx, block_diagonal, 0)

    for arrival in z_sends:
        arrival()
    extend(basis.at[0], z_rims)

    moments = [jnp.zeros((8, 128), F32) for _ in range(8)]

    def inner_product(i, j):
        total = jnp.zeros((8, 128), F32)
        for r in range(STRIPS):
            product = diag[strip(r), 0:COLS] * basis[i, strip(r), 0:COLS] * basis[j, strip(r), 0:COLS]
            for m in range(COLS // 128):
                total = total + product[:, 128 * m : 128 * (m + 1)]
        return total

    moments[0] = inner_product(0, 0)
    for step in range(ITERS):
        rows_x = spread_rows(lambda r: basis[step, strip(r), :], STRIPS + 1)
        rows_dx = spread_rows(lambda r: depth[strip(r), :] * basis[step, strip(r), :], STRIPS + 1)
        for r in range(STRIPS + 1 if step < ITERS - 1 else STRIPS):
            d, x = depth[strip(r), :], basis[step, strip(r), :]
            image = 2.0 * (d * rows_x[r] + rows_dx[r]) - 8.0 * (d * x)
            image = image + pltpu.roll(depth_e[strip(r), :] * rows_x[r] + rows_dx[r], 1, 1)
            image = image + pltpu.roll(depth_w[strip(r), :] * rows_x[r] + rows_dx[r], XC - 1, 1)
            scale = (0.25 / HALF) * inv[strip(r), :]
            following = scale * image - (CENTRE / HALF) * x
            if step:
                following = following + following - basis[step - 1, strip(r), :]
            basis[step + 1, strip(r), :] = following
        moments[2 * step + 1] = inner_product(step, step + 1)
        if step < ITERS - 1:
            moments[2 * step + 2] = inner_product(step + 1, step + 1)

    row8 = lax.broadcasted_iota(jnp.int32, (8, 128), 0)
    mine = jnp.zeros((8, 128), F32)
    for m in range(8):
        mine = jnp.where(row8 == m, jnp.sum(moments[m], axis=0, keepdims=True), mine)
    part[...] = mine
    x_sends = [send(part, sums_x.at[off], xs.at[off], xr.at[off], off, 0) for off in range(1, nx)]
    edge_cols = [jnp.zeros((8, BS), F32) for _ in range(blocks)]
    for step in range(ITERS):
        ring_x = [pack_ring(tiles(basis.at[step], r)) for r in range(STRIPS)]
        ring_dx = [ring_d[strip(r), :] * ring_x[r] for r in range(STRIPS)]
        edge_columns(step, ring_x, ring_dx, lambda r: edge_s[strip(r), :], edge_cols)
        x = basis[step, strip(STRIPS), :]
        edge_lines(
            step, x, depth[strip(STRIPS), :] * x, lambda row: (0.25 / HALF) * inv[row : row + 1, :], edge_rows
        )
    edge_cols = [swapped(v) for v in edge_cols]
    edge_copies = scatter(
        lambda m, i: edge_cols[m] if i else edge_rows[:, block(m)], 2, edges_out, lambda off: edges.at[off], es, er
    )
    total = mine
    for off in range(1, nx):
        x_sends[off - 1].wait_recv()
        total = total + sums_x[off]
    part2[...] = total
    y_sends = [send(part2, sums_y.at[off], ys.at[off], yr.at[off], 0, off) for off in range(1, ny)]

    for copy in first_copies + edge_copies:
        copy.wait_recv()

    def repeat(n, carry):
        x = [slots[n, 0, strip(r), :] for r in range(STRIPS)]
        before = x
        for step in range(ITERS):
            dx = [still[n, 0, strip(r), :] * x[r] for r in range(STRIPS)]
            wide_x, wide_dx = spread(x), spread(dx)
            after = []
            for r in range(STRIPS):
                image = still[n, 0, strip(r), :] * wide_x[r] + wide_dx[r] - 8.0 * dx[r]
                following = (0.25 / HALF) * still[n, 1, strip(r), :] * image - (CENTRE / HALF) * x[r]
                following = with_edges(following, r, step, edges, n)
                if step:
                    following = following + following - before[r]
                slots[n, step + 1, strip(r), :] = following
                after.append(following)
            before, x = x, after
        return carry

    lax.fori_loop(0, nx, repeat, 0)

    for off in range(1, ny):
        y_sends[off - 1].wait_recv()
        total = total + sums_y[off]
    total = jnp.sum(total, axis=1, keepdims=True)
    g = [total[m : m + 1, 0:1] for m in range(8)]

    nu = [g[0], g[1]]
    for m in range(2, 8):
        nu.append(g[m] + g[m] - nu[m % 2])
    gram = {}
    for i in range(ITERS):
        for j in range(ITERS + 1):
            gram[i, j] = 0.5 * (nu[i + j] + nu[abs(i - j)]) if i and j else nu[i + j]

    def dot(a, b):
        terms = []
        for i, first_c in enumerate(a):
            inside = None
            for j, second_c in enumerate(b):
                term = gram[min(i, j), max(i, j)] * second_c
                inside = term if inside is None else inside + term
            terms.append(first_c * inside)
        return functools.reduce(lambda p, q: p + q, terms)

    one = jnp.ones((1, 1), F32)
    zero = jnp.zeros((1, 1), F32)
    z, direction, x = [one], [one], [zero] * ITERS
    norm = dot(z, z)
    for step in range(ITERS):
        image = [(1.0 - CENTRE) * v for v in direction] + [zero]
        for i, v in enumerate(direction):
            if i == 0:
                image[1] = image[1] - HALF * v
            else:
                image[i + 1] = image[i + 1] - (0.5 * HALF) * v
                image[i - 1] = image[i - 1] - (0.5 * HALF) * v
        alpha = norm / dot(direction, image)
        for i, v in enumerate(direction):
            x[i] = x[i] + alpha * v
        z = [v - alpha * w for v, w in zip(z + [zero], image)]
        if step < ITERS - 1:
            following = dot(z, z)
            ratio = following / norm
            direction = [v + ratio * w for v, w in zip(z, direction + [zero])]
            norm = following

    for n in range(nx):
        place = pl.ds(pl.multiple_of(lax.rem(mx - n + nx, nx) * BS, BS), BS)
        for r in range(STRIPS):
            y = [slots[n, i, strip(r), :] for i in range(ITERS + 1)]
            barotropic[0, strip(r), place] = sum(x[i] * y[i] for i in range(ITERS))
            barotropic[1, strip(r), place] = full[n, strip(r), :] * sum(z[i] * y[i] for i in range(ITERS + 1))
    for copy in pending:
        copy.wait_send()
    for departure in pending_rims:
        departure()


def on_device(tracer, u_east, v_north, kmt, dest, dz, wind):
    nx, ny = lax.axis_size("bx"), lax.axis_size("by")
    levels = tracer.shape[0]
    slab = pltpu.VMEM((levels, ROWS, COLS), F32)
    ext = pltpu.VMEM((XR, XC), F32)
    flat = pltpu.VMEM((ROWS, COLS), F32)
    flat_i = pltpu.VMEM((ROWS, COLS), jnp.int32)
    rows = pltpu.VMEM((levels, COLS), F32)
    rows2 = pltpu.VMEM((2, levels, COLS), F32)
    cols = pltpu.VMEM((ROWS, 128), F32)
    cols2 = pltpu.VMEM((2, ROWS, 128), F32)

    def rims(dtype):
        return [
            pltpu.VMEM((2, 8, COLS), dtype),
            pltpu.VMEM((2, 8, 128), dtype),
            pltpu.VMEM((4, 8, 128), dtype),
        ]

    scratch = [slab] * 4 + [pltpu.VMEM((XR, XC), jnp.int32), flat_i, flat_i, flat] + [slab] * 4
    scratch += [ext, ext, ext, ext, ext, pltpu.VMEM((ITERS + 1, XR, XC), F32)]
    scratch += [pltpu.SMEM(dest.shape, jnp.int32), pltpu.SMEM(dz.shape, F32)]
    scratch += rims(F32) + rims(jnp.int32)
    scratch += [rows2, rows, cols, rows2, rows, cols2]
    scratch += [rows2, rows2, cols, cols2, rows2, cols]
    scratch += [pltpu.VMEM((8, 128), jnp.int32), pltpu.VMEM((8, 128), F32), rows2]
    scratch += [
        pltpu.VMEM((8, 128), F32),
        pltpu.VMEM((nx, 8, 128), F32),
        pltpu.VMEM((8, 128), F32),
        pltpu.VMEM((ny, 8, 128), F32),
        pltpu.VMEM((nx, 1, ROWS, BS), F32),
        pltpu.VMEM((nx, 2, ROWS, BS), F32),
        pltpu.VMEM((nx, 1, ROWS, BS), F32),
        pltpu.VMEM((nx, ITERS + 1, ROWS, BS), F32),
        cols,
        cols,
        cols,
        pltpu.VMEM((8, COLS), F32),
        pltpu.VMEM((nx, 2, 8, BS), F32),
        pltpu.VMEM((nx, 2, 8, BS), F32),
        pltpu.VMEM((8, COLS), F32),
        pltpu.VMEM((nx, 2, 8, BS), F32),
        pltpu.VMEM((nx, 2, 8, BS), F32),
        pltpu.VMEM((nx, ROWS, BS), F32),
    ]
    counts = [9] + [8] * 6 + [nx, nx, ny, ny] + [nx] * 8
    scratch += [pltpu.SemaphoreType.DMA((n,)) for n in counts]
    in_vmem = pl.BlockSpec(memory_space=pltpu.VMEM)
    hbm = pl.BlockSpec(memory_space=pltpu.HBM)
    return pl.pallas_call(
        functools.partial(kernel, nx, ny, levels),
        out_shape=(
            jax.ShapeDtypeStruct(tracer.shape, F32),
            jax.ShapeDtypeStruct((2, ROWS, nx * BS), F32),
        ),
        in_specs=[hbm] * 7,
        out_specs=(in_vmem, in_vmem),
        scratch_shapes=scratch,
        compiler_params=pltpu.CompilerParams(
            collective_id=0, has_side_effects=True, vmem_limit_bytes=32 * 1024 * 1024
        ),
    )(*[pltpu.with_memory_space_constraint(x, pltpu.HBM) for x in (tracer, u_east, v_north, kmt, dest, dz, wind)])


def solution(mesh):
    in_specs = (
        P(None, "by", "bx"),
        P(None, "by", "bx"),
        P(None, "by", "bx"),
        P("by", "bx"),
        P("by", "bx"),
        P(),
        P("by", "bx"),
    )
    out_specs = (P(None, "by", "bx"), P(None, "by", "bx"))
    return jax.shard_map(
        on_device, mesh=mesh, in_specs=in_specs, out_specs=out_specs, check_vma=False
    )
```

```python
import functools

import jax
import jax.numpy as jnp
from jax import lax
from jax.experimental import pallas as pl
from jax.experimental.pallas import tpu as pltpu
from jax.sharding import PartitionSpec as P

BS = 128
ITERS = 4
KAPPA = 0.12
SIGMA = 0.2
CENTRE = 1.0 / 3.0
HALF = 2.0 / 3.0
MESH = pl.DeviceIdType.MESH
ROWS = 64
COLS = 512
XR = ROWS + 8
XC = COLS + 128
STRIPS = ROWS // 8
F32 = jnp.float32
SIDES = ((0, 1), (0, -1), (1, 0), (-1, 0), (1, 1), (-1, 1), (1, -1), (-1, -1))


def strip(r):
    return pl.ds(8 * r, 8)


def rim(ref, side):
    dx, dy = SIDES[side]
    rows = {1: pl.ds(ROWS - 8, 8), -1: pl.ds(0, 8), 0: pl.ds(0, ROWS)}[dy]
    cols = {1: pl.ds(COLS - 128, 128), -1: pl.ds(0, 128), 0: pl.ds(0, COLS)}[dx]
    return ref.at[rows, cols]


def pack_ends(ext):
    lane = lax.broadcasted_iota(jnp.int32, (8, 128), 1)
    packed = jnp.zeros((8, 128), ext.dtype)
    for r in range(STRIPS):
        both = jnp.where(lane < 64, ext[strip(r), 0:128], ext[strip(r), COLS - 128 : COLS])
        both = pltpu.roll(both, 16 * r, 1) if r else both
        packed = jnp.where(((lane + 8) & 127) >> 4 == r, both, packed)
    return packed


def extend(ext, rims):
    from_s, from_n, from_w, from_e, from_sw, from_se, from_nw, from_ne = rims
    low = lax.broadcasted_iota(jnp.int32, (8, COLS), 0) < 4
    ext[ROWS:XR, 0:COLS] = jnp.where(low, from_n[...], from_s[...])
    lane = lax.broadcasted_iota(jnp.int32, (8, 128), 1)
    ends = jnp.where(((lane + 8) & 15) < 8, from_w[...], from_e[...])
    for r in range(STRIPS):
        ext[strip(r), COLS:XC] = pltpu.roll(ends, 128 - 16 * r, 1) if r else ends
    east8 = lane < 64
    low8 = lax.broadcasted_iota(jnp.int32, (8, 128), 0) < 4
    ext[ROWS:XR, COLS:XC] = jnp.where(
        low8,
        jnp.where(east8, from_ne[...], from_nw[...]),
        jnp.where(east8, from_se[...], from_sw[...]),
    )


def spread_rows(get, count, wrap=True):
    x = [get(r) for r in range(count)]
    sub = lax.broadcasted_iota(jnp.int32, x[0].shape, 0)
    up = [pltpu.roll(v, 7, 0) for v in x]
    down = [pltpu.roll(v, 1, 0) for v in x]
    out = []
    for r in range(count):
        north = jnp.where(sub == 7, up[(r + 1) % count] if wrap or r + 1 < count else 0.0, up[r])
        south = jnp.where(sub == 0, down[r - 1] if wrap or r else 0.0, down[r])
        out.append(x[r] + x[r] + (north + south))
    return out


def spread_cols(v):
    return v + v + (pltpu.roll(v, 1, 1) + pltpu.roll(v, XC - 1, 1))


def kernel(
    nx,
    ny,
    levels,
    tracer,
    u_east,
    v_north,
    kmt,
    dest_in,
    dz_in,
    wind,
    tracer_out,
    barotropic,
    c0,
    u0,
    v0,
    c1,
    k_x,
    ke,
    kn,
    rhs,
    ae,
    be,
    an,
    bn,
    depth,
    depth_e,
    depth_w,
    inv,
    diag,
    basis,
    dest,
    dz,
    zrim_row,
    zrim_col,
    zrim_corner,
    krim_row,
    krim_col,
    krim_corner,
    up_send,
    dn_send,
    col_send,
    up_recv,
    dn_recv,
    col_recv,
    rows1,
    rows1_recv,
    cols1,
    cols1_recv,
    rows_own,
    cols_own,
    kends,
    zends,
    row_flux,
    part,
    sums_x,
    part2,
    sums_y,
    still_out,
    still,
    first_out,
    slots,
    ring_d,
    edge_d,
    edge_s,
    edge_rows,
    edges_out,
    edges,
    edge_rows0,
    edges0_out,
    edges0,
    full,
    load_sem,
    ks,
    kr,
    rs,
    rr,
    zs,
    zr,
    xs,
    xr,
    ys,
    yr,
    ds,
    dr,
    fs,
    fr,
    es,
    er,
    gs,
    gr,
):
    mx = lax.axis_index("bx")
    my = lax.axis_index("by")
    pending, pending_rims = [], []

    def peer(dx, dy):
        return (lax.rem(mx + dx + nx, nx), lax.rem(my + dy + ny, ny))

    def send(src, dst, send_sem, recv_sem, dx, dy):
        copy = pltpu.make_async_remote_copy(
            src_ref=src, dst_ref=dst, send_sem=send_sem, recv_sem=recv_sem, device_id=peer(dx, dy), device_id_type=MESH
        )
        copy.start()
        pending.append(copy)
        return copy

    def send_rim(src, dst, send_sem, recv_sem, dx, dy):
        copy = pltpu.make_async_remote_copy(
            src_ref=src, dst_ref=dst, send_sem=send_sem, recv_sem=recv_sem, device_id=peer(dx, dy), device_id_type=MESH
        )
        goes, comes = {1: (has_n, has_s), -1: (has_s, has_n), 0: (None, None)}[dy]

        def guarded(action, guard):
            action() if guard is None else pl.when(guard)(action)

        guarded(copy.start, goes)
        pending_rims.append(lambda: guarded(copy.wait_send, goes))
        return lambda: guarded(copy.wait_recv, comes)

    has_n, has_s = my < ny - 1, my > 0
    barrier = pltpu.get_barrier_semaphore()

    def greet(dx, dy):
        pl.semaphore_signal(barrier, inc=1, device_id=peer(dx, dy), device_id_type=MESH)

    for off in sorted(range(1, ny), key=lambda o: -min(o, ny - o)):
        greet(0, off)
    for off in sorted(range(1, nx), key=lambda o: -min(o, nx - o)):
        greet(off, 0)
    for dx, dy in SIDES[4:]:
        pl.when(has_n if dy == 1 else has_s)(functools.partial(greet, dx, dy))
    n_peers = nx - 1 + ny - 1 + jnp.where(has_n, 2, 0) + jnp.where(has_s, 2, 0)

    last_cols = (slice(None), slice(None), pl.ds(COLS - 128, 128))
    other_cols = (slice(None), slice(None), pl.ds(0, COLS - 128))
    last_rows = (slice(None), pl.ds(ROWS - 8, 8))
    other_rows = (slice(None), pl.ds(0, ROWS - 8))
    loads = [
        pltpu.make_async_copy(kmt, k_x.at[pl.ds(0, ROWS), pl.ds(0, COLS)], load_sem.at[0]),
        pltpu.make_async_copy(dest_in, dest, load_sem.at[1]),
        pltpu.make_async_copy(dz_in, dz, load_sem.at[2]),
        pltpu.make_async_copy(tracer, c0, load_sem.at[3]),
        pltpu.make_async_copy(u_east.at[last_cols], u0.at[last_cols], load_sem.at[4]),
        pltpu.make_async_copy(v_north.at[last_rows], v0.at[last_rows], load_sem.at[5]),
        pltpu.make_async_copy(u_east.at[other_cols], u0.at[other_cols], load_sem.at[6]),
        pltpu.make_async_copy(v_north.at[other_rows], v0.at[other_rows], load_sem.at[7]),
        pltpu.make_async_copy(wind, rhs, load_sem.at[8]),
    ]
    for copy in loads:
        copy.start()

    def no_rim(at, corners):
        zrim_row[at] = jnp.zeros((8, COLS), F32)
        krim_row[at] = jnp.zeros((8, COLS), jnp.int32)
        for i in corners:
            zrim_corner[i] = jnp.zeros((8, 128), F32)
            krim_corner[i] = jnp.zeros((8, 128), jnp.int32)

    pl.when(jnp.logical_not(has_s))(lambda: no_rim(0, (0, 1)))
    pl.when(jnp.logical_not(has_n))(lambda: no_rim(1, (2, 3)))

    loads[0].wait()
    sub = lax.broadcasted_iota(jnp.int32, (8, COLS), 0)
    lane_row = lax.broadcasted_iota(jnp.int32, (8, COLS), 1)
    k_up = [pltpu.roll(k_x[strip(r), 0:COLS], 7, 0) for r in range(STRIPS)]
    for r in range(STRIPS):
        here = k_x[strip(r), 0:COLS]
        east = jnp.where(lane_row == COLS - 1, 0, pltpu.roll(here, COLS - 1, 1))
        north = jnp.where(sub == 7, k_up[r + 1] if r + 1 < STRIPS else 0, k_up[r])
        ke[strip(r), :] = jnp.minimum(here, east)
        kn[strip(r), :] = jnp.minimum(here, north)
    for copy in loads[1:6]:
        copy.wait()

    lane = lax.broadcasted_iota(jnp.int32, (ROWS, 128), 1)
    west = lane < 64
    group = ((lane + 4) & 127) >> 3
    slot = ((lane + 4) & 7) - 4

    def ends(field, k):
        return jnp.where(west, field[k, :, 0:128], field[k, :, COLS - 128 : COLS])

    def turned(value, lanes):
        return pltpu.roll(value, lanes % 128, 1) if lanes % 128 else value

    packed = jnp.zeros((ROWS, 128), F32)
    for k in range(levels):
        up_send[0, k : k + 1, :] = c0[k, ROWS - 1 : ROWS, :]
        up_send[1, k : k + 1, :] = v0[k, ROWS - 1 : ROWS, :]
        dn_send[k : k + 1, :] = c0[k, 0:1, :]
        both = jnp.where(slot == -2, turned(u0[k, :, COLS - 128 : COLS], 8 * k - 1), turned(ends(c0, k), 8 * k))
        packed = jnp.where(group == k, both, packed)
    col_send[...] = packed
    pl.semaphore_wait(barrier, n_peers)
    from_s = send_rim(up_send, up_recv, rs.at[0], rr.at[0], 0, 1)
    from_n = send_rim(dn_send, dn_recv, rs.at[1], rr.at[1], 0, -1)
    from_w = send_rim(col_send, col_recv.at[0], rs.at[2], rr.at[2], 1, 0)
    from_e = send_rim(col_send, col_recv.at[1], rs.at[3], rr.at[3], -1, 0)

    def rim_refs(row, col, corner):
        return [row.at[0], row.at[1], col.at[0], col.at[1]] + [corner.at[i] for i in range(4)]

    k_rims = rim_refs(krim_row, krim_col, krim_corner)
    kends[...] = pack_ends(k_x)
    k_sends = [
        send_rim(kends if SIDES[s][1] == 0 else rim(kmt, s), k_rims[s], ks.at[s], kr.at[s], *SIDES[s]) for s in range(8)
    ]

    def advance(get, k, put):
        def north_flux(r, c, up, nxt):
            return an[k, strip(r), :] * c + bn[k, strip(r), :] * jnp.where(sub == 7, nxt, up)

        below = jnp.zeros((8, COLS), F32)
        c, up = get(0), pltpu.roll(get(0), 7, 0)
        for r in range(STRIPS):
            if r + 1 < STRIPS:
                c_next = get(r + 1)
                up_next = pltpu.roll(c_next, 7, 0)
            flux = north_flux(r, c, up, up_next)
            down = pltpu.roll(flux, 1, 0)
            flux_e = ae[k, strip(r), :] * c + be[k, strip(r), :] * pltpu.roll(c, COLS - 1, 1)
            spread = flux_e - pltpu.roll(flux_e, 1, 1)
            spread = spread + (flux - jnp.where(sub == 0, below, down))
            put(r, c - spread)
            below, c, up = down, c_next, up_next

    def first_step(k, carry):
        for r in range(STRIPS):
            half_u, half_v = 0.5 * u0[k, strip(r), :], 0.5 * v0[k, strip(r), :]
            wet_e, wet_n = ke[strip(r), :] > k, kn[strip(r), :] > k
            ae[k, strip(r), :] = jnp.where(wet_e, half_u + KAPPA, 0.0)
            be[k, strip(r), :] = jnp.where(wet_e, half_u - KAPPA, 0.0)
            an[k, strip(r), :] = jnp.where(wet_n, half_v + KAPPA, 0.0)
            bn[k, strip(r), :] = jnp.where(wet_n, half_v - KAPPA, 0.0)

        def put(r, value):
            c1[k, strip(r), :] = value

        advance(lambda r: c0[k, strip(r), :], k, put)
        return carry

    for copy in loads[6:]:
        copy.wait()
    lax.fori_loop(0, levels, first_step, 0)
    packed = jnp.zeros((ROWS, 128), F32)
    for k in range(levels):
        rows_own[0, k : k + 1, :] = c1[k, ROWS - 1 : ROWS, :]
        rows_own[1, k : k + 1, :] = c1[k, 0:1, :]
        packed = jnp.where(group == k, turned(ends(c1, k), 8 * k), packed)
    cols_own[...] = packed

    for arrival in k_sends:
        arrival()
    extend(k_x, k_rims)
    level16 = lax.broadcasted_iota(jnp.int32, (levels, COLS), 0)
    wet_n = jnp.minimum(k_x[ROWS - 1 : ROWS, 0:COLS], k_x[ROWS : ROWS + 1, 0:COLS]) > level16
    wet_s = jnp.minimum(k_x[0:1, 0:COLS], k_x[XR - 1 : XR, 0:COLS]) > level16
    wet_e = jnp.minimum(k_x[0:ROWS, COLS - 1 : COLS], k_x[0:ROWS, COLS : COLS + 1]) > group
    wet_w = jnp.minimum(k_x[0:ROWS, 0:1], k_x[0:ROWS, XC - 1 : XC]) > group

    def face(velocity, here, there, wet):
        half = 0.5 * velocity
        return jnp.where(wet, (half + KAPPA) * here + (half - KAPPA) * there, 0.0)

    def rim_rows(north_row, south_row, own_north, own_south):
        row_flux[0] = face(up_send[1], own_north, north_row, wet_n)
        row_flux[1] = face(up_recv[1], south_row, own_south, wet_s)

    def rim_cols(own, westward, eastward):
        out = face(turned(col_send[...], 1), own, turned(eastward, -1), wet_e)
        into = face(turned(col_recv[0], 2), turned(westward, 1), own, wet_w)
        return jnp.where(slot == -1, -out, jnp.where(slot == 0, into, 0.0))

    for arrival in (from_s, from_n, from_w, from_e):
        arrival()
    rim_rows(dn_recv[...], up_recv[0], up_send[0], dn_send[...])
    flux_cols = rim_cols(col_send[...], col_recv[0], col_recv[1])

    def correct(field, k, flux):
        change = turned(flux, -8 * k)
        field[k, :, 0:128] = field[k, :, 0:128] + jnp.where(lane == 0, change, 0.0)
        field[k, :, COLS - 128 : COLS] = field[k, :, COLS - 128 : COLS] + jnp.where(lane == 127, change, 0.0)
        field[k, 0:1, :] = field[k, 0:1, :] + row_flux[1, k : k + 1, :]
        field[k, ROWS - 1 : ROWS, :] = field[k, ROWS - 1 : ROWS, :] - row_flux[0, k : k + 1, :]

    lane16 = lax.broadcasted_iota(jnp.int32, (levels, 128), 1)
    level8 = 8 * level16[:, 0:128]
    on_west, on_east = lane16 == level8, lane16 == ((level8 + 127) & 127)
    for at, row, sign in ((0, ROWS - 1, -1.0), (1, 0, 1.0)):
        line = jnp.broadcast_to(flux_cols[row : row + 1, :], (levels, 128))
        from_west = jnp.sum(jnp.where(on_west, line, 0.0), axis=1, keepdims=True)
        from_east = jnp.sum(jnp.where(on_east, line, 0.0), axis=1, keepdims=True)
        change = sign * row_flux[at]
        value = rows_own[at] + change
        rows1[at, :, 0:128] = value[:, 0:128] + jnp.where(lane16 == 0, from_west, 0.0)
        rows1[at, :, 128 : COLS - 128] = value[:, 128 : COLS - 128]
        rows1[at, :, COLS - 128 : COLS] = value[:, COLS - 128 : COLS] + jnp.where(lane16 == 127, from_east, 0.0)
        corner = jnp.where(on_west, change[:, 0:1], 0.0) + jnp.where(on_east, change[:, COLS - 1 : COLS], 0.0)
        cols_own[row : row + 1, :] = cols_own[row : row + 1, :] + jnp.sum(corner, axis=0, keepdims=True)
    cols1[...] = cols_own[...] + flux_cols
    from_s = send_rim(rows1.at[0], rows1_recv.at[0], rs.at[4], rr.at[4], 0, 1)
    from_n = send_rim(rows1.at[1], rows1_recv.at[1], rs.at[5], rr.at[5], 0, -1)
    from_w = send_rim(cols1, cols1_recv.at[0], rs.at[6], rr.at[6], 1, 0)
    from_e = send_rim(cols1, cols1_recv.at[1], rs.at[7], rr.at[7], -1, 0)
    for k in range(levels):
        correct(c1, k, flux_cols)

    subx = lax.broadcasted_iota(jnp.int32, (8, XC), 0)
    for r in range(STRIPS + 1):
        here = k_x[strip(r), :]
        total = jnp.zeros((8, XC), F32)
        for k in range(levels):
            total = total + jnp.where(here > k, dz[k], 0.0)
        depth[strip(r), :] = total
        depth_e[strip(r), :] = pltpu.roll(total, XC - 1, 1)
        depth_w[strip(r), :] = pltpu.roll(total, 1, 1)

    def ocean_of(r):
        return jnp.where(k_x[strip(r), :] > 0, 1.0, 0.0).astype(F32)

    rows_o = spread_rows(ocean_of, STRIPS + 1)
    rows_d = spread_rows(lambda r: depth[strip(r), :], STRIPS + 1)
    for r in range(STRIPS + 1):
        d = depth[strip(r), :]
        o = ocean_of(r)
        total = d * spread_cols(rows_o[r]) + spread_cols(rows_d[r]) - 8.0 * d
        whole = SIGMA + 0.25 * o * total
        diag[strip(r), :] = whole
        inv[strip(r), :] = o / whole

    blocks = COLS // BS

    def scatter(get, parts, outbox, inbox, ssem, rsem):
        copies = []
        for off in sorted(range(nx), key=lambda o: -min(o, nx - o)):
            target = lax.rem(mx + off, nx)
            hits = [dest[0, m] == target for m in range(blocks)]
            here = outbox.at[off] if off else inbox(0)
            for i in range(parts):
                chosen = None
                for m in range(blocks):
                    piece = get(m, i)
                    chosen = jnp.where(hits[m], piece, jnp.zeros_like(piece) if chosen is None else chosen)
                here[i] = chosen
            if off:
                copies.append(send(outbox.at[off], inbox(off), ssem.at[off], rsem.at[off], off, 0))
        return copies

    def block(m):
        return pl.ds(m * BS, BS)

    still_copies = scatter(
        lambda m, i: depth[0:ROWS, block(m)], 1, still_out, lambda off: still.at[off, pl.ds(0, 1)], ds, dr
    )

    lane8 = lax.broadcasted_iota(jnp.int32, (8, BS), 1)

    def pack(both):
        packed = jnp.zeros((8, BS), F32)
        for m in range(blocks):
            packed = jnp.where(((lane8 + 8) & 127) >> 4 == m, turned(both[m], 16 * m), packed)
        return packed

    def tiles(ref, r):
        return [ref[strip(r), block(m)] for m in range(blocks + 1)]

    def pack_ring(tile):
        return pack([jnp.where(lane8 < 64, tile[m + 1], tile[m - 1]) for m in range(blocks)])

    def pack_edges(tile):
        return pack([jnp.where(lane8 == 0, turned(tile[m], 1), turned(tile[m], -1)) for m in range(blocks)])

    for r in range(STRIPS):
        ring_d[strip(r), :] = pack_ring(tiles(depth, r))
        edge_d[strip(r), :] = pack_edges(tiles(depth, r))
        edge_s[strip(r), :] = (0.25 / HALF) * pack_edges(tiles(inv, r))

    def edge_columns(step, ring_x, ring_dx, scale, cols_m):
        inner_x = spread_rows(lambda r: ring_x[r], STRIPS, False)
        inner_dx = spread_rows(lambda r: ring_dx[r], STRIPS, False)
        for r in range(STRIPS):
            edge = scale(r) * (edge_d[strip(r), :] * inner_x[r] + inner_dx[r])
            for m in range(blocks):
                moved = turned(edge, 16 * r + 2 * step + 1 - 16 * m)
                cols_m[m] = jnp.where((lane8 >> 1) == 8 * r + step, moved, cols_m[m])

    def edge_lines(step, x, dx, scale, out_rows):
        beyond_x, beyond_dx = spread_cols(x), spread_cols(dx)
        for row, out, at in ((ROWS - 1, 0, 0), (0, 7, 1)):
            edge = scale(row) * (depth[row : row + 1, :] * beyond_x[out : out + 1] + beyond_dx[out : out + 1])
            out_rows[2 * step + at : 2 * step + at + 1, :] = edge[:, 0:COLS]

    def swapped(value):
        return jnp.where((lane8 & 1) == 1, turned(value, 1), turned(value, -1))

    def one_if(wet):
        return jnp.where(wet, 1.0, 0.0).astype(F32)

    ring_0 = [ring_d[strip(r), :] for r in range(STRIPS)]
    edge_cols = [jnp.zeros((8, BS), F32) for _ in range(blocks)]
    edge_columns(
        0, [one_if(v > 0.0) for v in ring_0], ring_0, lambda r: 0.25 * one_if(edge_d[strip(r), :] > 0.0), edge_cols
    )
    edge_rows0[...] = jnp.zeros((8, COLS), F32)
    edge_lines(
        0,
        ocean_of(STRIPS),
        depth[strip(STRIPS), :],
        lambda row: 0.25 * one_if(depth[row : row + 1, :] > 0.0),
        edge_rows0,
    )
    edge_cols0 = [swapped(v) for v in edge_cols]
    edge0_copies = scatter(
        lambda m, i: edge_cols0[m] if i else edge_rows0[:, block(m)], 2, edges0_out, lambda off: edges0.at[off], gs, gr
    )

    def second_step(k, carry):
        def put(r, value):
            tracer_out[k, strip(r), :] = value
            wet = k_x[strip(r), 0:COLS] > k
            rhs[strip(r), :] = rhs[strip(r), :] + jnp.where(wet, dz[k] * value, 0.0)

        advance(lambda r: c1[k, strip(r), :], k, put)
        return carry

    lax.fori_loop(0, levels, second_step, 0)

    for arrival in (from_s, from_n, from_w, from_e):
        arrival()
    rim_rows(rows1_recv[1], rows1_recv[0], rows1[0], rows1[1])
    flux_cols = rim_cols(cols1[...], cols1_recv[0], cols1_recv[1])
    dz_rows = jnp.zeros((levels, 128), F32)
    dz_cols = jnp.zeros((ROWS, 128), F32)
    for k in range(levels):
        dz_rows = jnp.where(level16[:, 0:128] == k, dz[k], dz_rows)
        dz_cols = jnp.where(group == k, dz[k], dz_cols)
    dz_rows = jnp.concatenate([dz_rows] * (COLS // 128), axis=1)
    weighted = dz_cols * flux_cols
    change_w = jnp.sum(jnp.where(slot == 0, weighted, 0.0), axis=1, keepdims=True)
    change_e = jnp.sum(jnp.where(slot == -1, weighted, 0.0), axis=1, keepdims=True)
    rhs[:, 0:128] = rhs[:, 0:128] + jnp.where(lane == 0, change_w, 0.0)
    rhs[:, COLS - 128 : COLS] = rhs[:, COLS - 128 : COLS] + jnp.where(lane == 127, change_e, 0.0)
    rhs[0:1, :] = rhs[0:1, :] + jnp.sum(dz_rows * row_flux[1], axis=0, keepdims=True)
    rhs[ROWS - 1 : ROWS, :] = rhs[ROWS - 1 : ROWS, :] - jnp.sum(dz_rows * row_flux[0], axis=0, keepdims=True)

    for r in range(STRIPS):
        start = jnp.where(k_x[strip(r), 0:COLS] > 0, rhs[strip(r), :], 0.0)
        basis[0, strip(r), 0:COLS] = start * inv[strip(r), 0:COLS]
    z_rims = rim_refs(zrim_row, zrim_col, zrim_corner)
    zends[...] = pack_ends(basis.at[0])
    z_sends = [
        send_rim(zends if SIDES[s][1] == 0 else rim(basis.at[0], s), z_rims[s], zs.at[s], zr.at[s], *SIDES[s])
        for s in range(8)
    ]
    first_copies = scatter(
        lambda m, i: basis[0, 0:ROWS, block(m)], 1, first_out, lambda off: slots.at[off, pl.ds(0, 1)], fs, fr
    )
    for k in range(levels):
        correct(tracer_out, k, flux_cols)

    for copy in still_copies + edge0_copies:
        copy.wait_recv()
    sub8 = lax.broadcasted_iota(jnp.int32, (8, BS), 0)
    sides = (lane8 == 0) | (lane8 == BS - 1)

    def spread(values):
        out = []
        for v in spread_rows(lambda r: values[r], STRIPS, False):
            east = jnp.where(lane8 == BS - 1, 0.0, pltpu.roll(v, BS - 1, 1))
            out.append(v + v + (east + jnp.where(lane8 == 0, 0.0, pltpu.roll(v, 1, 1))))
        return out

    def with_edges(value, r, step, packet, n):
        value = value + jnp.where(sides, pltpu.roll(packet[n, 1], BS - (16 * r + 2 * step + 1), 1), 0.0)
        if r == STRIPS - 1:
            value = value + jnp.where(sub8 == 7, packet[n, 0, 2 * step : 2 * step + 1, :], 0.0)
        if r == 0:
            value = value + jnp.where(sub8 == 0, packet[n, 0, 2 * step + 1 : 2 * step + 2, :], 0.0)
        return value

    def block_diagonal(n, carry):
        d = [still[n, 0, strip(r), :] for r in range(STRIPS)]
        o = [one_if(v > 0.0) for v in d]
        wide_o, wide_d = spread(o), spread(d)
        for r in range(STRIPS):
            total = d[r] * wide_o[r] + wide_d[r] - 8.0 * d[r]
            whole = with_edges(SIGMA + 0.25 * o[r] * total, r, 0, edges0, n)
            full[n, strip(r), :] = whole
            still[n, 1, strip(r), :] = o[r] / whole
        return carry

    lax.fori_loop(0, nx, block_diagonal, 0)

    for arrival in z_sends:
        arrival()
    extend(basis.at[0], z_rims)

    moments = [jnp.zeros((8, 128), F32) for _ in range(8)]

    def inner_products(j, others):
        totals = [jnp.zeros((8, 128), F32) for _ in others]
        for r in range(STRIPS):
            weighted = diag[strip(r), 0:COLS] * basis[j, strip(r), 0:COLS]
            for n, i in enumerate(others):
                product = weighted * basis[i, strip(r), 0:COLS]
                for m in range(COLS // 128):
                    totals[n] = totals[n] + product[:, 128 * m : 128 * (m + 1)]
        return totals

    moments[0] = inner_products(0, [0])[0]
    for step in range(ITERS):
        rows_x = spread_rows(lambda r: basis[step, strip(r), :], STRIPS + 1)
        rows_dx = spread_rows(lambda r: depth[strip(r), :] * basis[step, strip(r), :], STRIPS + 1)
        for r in range(STRIPS + 1 if step < ITERS - 1 else STRIPS):
            d, x = depth[strip(r), :], basis[step, strip(r), :]
            image = 2.0 * (d * rows_x[r] + rows_dx[r]) - 8.0 * (d * x)
            image = image + pltpu.roll(depth_e[strip(r), :] * rows_x[r] + rows_dx[r], 1, 1)
            image = image + pltpu.roll(depth_w[strip(r), :] * rows_x[r] + rows_dx[r], XC - 1, 1)
            scale = (0.25 / HALF) * inv[strip(r), :]
            following = scale * image - (CENTRE / HALF) * x
            if step:
                following = following + following - basis[step - 1, strip(r), :]
            if step < ITERS - 1:
                basis[step + 1, strip(r), :] = following
            else:
                basis[step + 1, strip(r), 0:COLS] = following[:, 0:COLS]
        both = [step, step + 1] if step < ITERS - 1 else [step]
        moments[2 * step + 1 : 2 * step + 1 + len(both)] = inner_products(step + 1, both)

    row8 = lax.broadcasted_iota(jnp.int32, (8, 128), 0)
    mine = jnp.zeros((8, 128), F32)
    for m in range(8):
        mine = jnp.where(row8 == m, jnp.sum(moments[m], axis=0, keepdims=True), mine)
    part[...] = mine
    x_sends = [send(part, sums_x.at[off], xs.at[off], xr.at[off], off, 0) for off in range(1, nx)]
    edge_cols = [jnp.zeros((8, BS), F32) for _ in range(blocks)]
    for step in range(ITERS):
        ring_x = [pack_ring(tiles(basis.at[step], r)) for r in range(STRIPS)]
        ring_dx = [ring_d[strip(r), :] * ring_x[r] for r in range(STRIPS)]
        edge_columns(step, ring_x, ring_dx, lambda r: edge_s[strip(r), :], edge_cols)
        x = basis[step, strip(STRIPS), :]
        edge_lines(
            step, x, depth[strip(STRIPS), :] * x, lambda row: (0.25 / HALF) * inv[row : row + 1, :], edge_rows
        )
    edge_cols = [swapped(v) for v in edge_cols]
    edge_copies = scatter(
        lambda m, i: edge_cols[m] if i else edge_rows[:, block(m)], 2, edges_out, lambda off: edges.at[off], es, er
    )
    total = mine
    for off in range(1, nx):
        x_sends[off - 1].wait_recv()
        total = total + sums_x[off]
    part2[...] = total
    y_sends = [send(part2, sums_y.at[off], ys.at[off], yr.at[off], 0, off) for off in range(1, ny)]

    for copy in first_copies + edge_copies:
        copy.wait_recv()

    def repeat(n, carry):
        x = [slots[n, 0, strip(r), :] for r in range(STRIPS)]
        before = x
        for step in range(ITERS):
            dx = [still[n, 0, strip(r), :] * x[r] for r in range(STRIPS)]
            wide_x, wide_dx = spread(x), spread(dx)
            after = []
            for r in range(STRIPS):
                image = still[n, 0, strip(r), :] * wide_x[r] + wide_dx[r] - 8.0 * dx[r]
                following = (0.25 / HALF) * still[n, 1, strip(r), :] * image - (CENTRE / HALF) * x[r]
                following = with_edges(following, r, step, edges, n)
                if step:
                    following = following + following - before[r]
                slots[n, step + 1, strip(r), :] = following
                after.append(following)
            before, x = x, after
        return carry

    lax.fori_loop(0, nx, repeat, 0)

    for off in range(1, ny):
        y_sends[off - 1].wait_recv()
        total = total + sums_y[off]
    total = jnp.sum(total, axis=1, keepdims=True)
    g = [total[m : m + 1, 0:1] for m in range(8)]

    nu = [g[0], g[1]]
    for m in range(2, 8):
        nu.append(g[m] + g[m] - nu[m % 2])
    gram = {}
    for i in range(ITERS):
        for j in range(ITERS + 1):
            gram[i, j] = 0.5 * (nu[i + j] + nu[abs(i - j)]) if i and j else nu[i + j]

    def dot(a, b):
        terms = []
        for i, first_c in enumerate(a):
            inside = None
            for j, second_c in enumerate(b):
                term = gram[min(i, j), max(i, j)] * second_c
                inside = term if inside is None else inside + term
            terms.append(first_c * inside)
        return functools.reduce(lambda p, q: p + q, terms)

    one = jnp.ones((1, 1), F32)
    zero = jnp.zeros((1, 1), F32)
    z, direction, x = [one], [one], [zero] * ITERS
    norm = dot(z, z)
    for step in range(ITERS):
        image = [(1.0 - CENTRE) * v for v in direction] + [zero]
        for i, v in enumerate(direction):
            if i == 0:
                image[1] = image[1] - HALF * v
            else:
                image[i + 1] = image[i + 1] - (0.5 * HALF) * v
                image[i - 1] = image[i - 1] - (0.5 * HALF) * v
        alpha = norm / dot(direction, image)
        for i, v in enumerate(direction):
            x[i] = x[i] + alpha * v
        z = [v - alpha * w for v, w in zip(z + [zero], image)]
        if step < ITERS - 1:
            following = dot(z, z)
            ratio = following / norm
            direction = [v + ratio * w for v, w in zip(z, direction + [zero])]
            norm = following

    for n in range(nx):
        place = pl.ds(pl.multiple_of(lax.rem(mx - n + nx, nx) * BS, BS), BS)
        for r in range(STRIPS):
            y = [slots[n, i, strip(r), :] for i in range(ITERS + 1)]
            barotropic[0, strip(r), place] = sum(x[i] * y[i] for i in range(ITERS))
            barotropic[1, strip(r), place] = full[n, strip(r), :] * sum(z[i] * y[i] for i in range(ITERS + 1))
    for copy in pending:
        copy.wait_send()
    for departure in pending_rims:
        departure()


def on_device(tracer, u_east, v_north, kmt, dest, dz, wind):
    nx, ny = lax.axis_size("bx"), lax.axis_size("by")
    levels = tracer.shape[0]
    slab = pltpu.VMEM((levels, ROWS, COLS), F32)
    ext = pltpu.VMEM((XR, XC), F32)
    flat = pltpu.VMEM((ROWS, COLS), F32)
    flat_i = pltpu.VMEM((ROWS, COLS), jnp.int32)
    rows = pltpu.VMEM((levels, COLS), F32)
    rows2 = pltpu.VMEM((2, levels, COLS), F32)
    cols = pltpu.VMEM((ROWS, 128), F32)
    cols2 = pltpu.VMEM((2, ROWS, 128), F32)

    def rims(dtype):
        return [
            pltpu.VMEM((2, 8, COLS), dtype),
            pltpu.VMEM((2, 8, 128), dtype),
            pltpu.VMEM((4, 8, 128), dtype),
        ]

    scratch = [slab] * 4 + [pltpu.VMEM((XR, XC), jnp.int32), flat_i, flat_i, flat] + [slab] * 4
    scratch += [ext, ext, ext, ext, ext, pltpu.VMEM((ITERS + 1, XR, XC), F32)]
    scratch += [pltpu.SMEM(dest.shape, jnp.int32), pltpu.SMEM(dz.shape, F32)]
    scratch += rims(F32) + rims(jnp.int32)
    scratch += [rows2, rows, cols, rows2, rows, cols2]
    scratch += [rows2, rows2, cols, cols2, rows2, cols]
    scratch += [pltpu.VMEM((8, 128), jnp.int32), pltpu.VMEM((8, 128), F32), rows2]
    scratch += [
        pltpu.VMEM((8, 128), F32),
        pltpu.VMEM((nx, 8, 128), F32),
        pltpu.VMEM((8, 128), F32),
        pltpu.VMEM((ny, 8, 128), F32),
        pltpu.VMEM((nx, 1, ROWS, BS), F32),
        pltpu.VMEM((nx, 2, ROWS, BS), F32),
        pltpu.VMEM((nx, 1, ROWS, BS), F32),
        pltpu.VMEM((nx, ITERS + 1, ROWS, BS), F32),
        cols,
        cols,
        cols,
        pltpu.VMEM((8, COLS), F32),
        pltpu.VMEM((nx, 2, 8, BS), F32),
        pltpu.VMEM((nx, 2, 8, BS), F32),
        pltpu.VMEM((8, COLS), F32),
        pltpu.VMEM((nx, 2, 8, BS), F32),
        pltpu.VMEM((nx, 2, 8, BS), F32),
        pltpu.VMEM((nx, ROWS, BS), F32),
    ]
    counts = [9] + [8] * 6 + [nx, nx, ny, ny] + [nx] * 8
    scratch += [pltpu.SemaphoreType.DMA((n,)) for n in counts]
    in_vmem = pl.BlockSpec(memory_space=pltpu.VMEM)
    hbm = pl.BlockSpec(memory_space=pltpu.HBM)
    return pl.pallas_call(
        functools.partial(kernel, nx, ny, levels),
        out_shape=(
            jax.ShapeDtypeStruct(tracer.shape, F32),
            jax.ShapeDtypeStruct((2, ROWS, nx * BS), F32),
        ),
        in_specs=[hbm] * 7,
        out_specs=(in_vmem, in_vmem),
        scratch_shapes=scratch,
        compiler_params=pltpu.CompilerParams(
            collective_id=0, has_side_effects=True, vmem_limit_bytes=32 * 1024 * 1024
        ),
    )(*[pltpu.with_memory_space_constraint(x, pltpu.HBM) for x in (tracer, u_east, v_north, kmt, dest, dz, wind)])


def solution(mesh):
    in_specs = (
        P(None, "by", "bx"),
        P(None, "by", "bx"),
        P(None, "by", "bx"),
        P("by", "bx"),
        P("by", "bx"),
        P(),
        P("by", "bx"),
    )
    out_specs = (P(None, "by", "bx"), P(None, "by", "bx"))
    return jax.shard_map(
        on_device, mesh=mesh, in_specs=in_specs, out_specs=out_specs, check_vma=False
    )
```

```python
import functools

import jax
import jax.numpy as jnp
from jax import lax
from jax.experimental import pallas as pl
from jax.experimental.pallas import tpu as pltpu
from jax.sharding import PartitionSpec as P

BS = 128
ITERS = 4
KAPPA = 0.12
SIGMA = 0.2
CENTRE = 1.0 / 3.0
HALF = 2.0 / 3.0
MESH = pl.DeviceIdType.MESH
ROWS = 64
COLS = 512
XR = ROWS + 8
XC = COLS + 128
STRIPS = ROWS // 8
F32 = jnp.float32
SIDES = ((0, 1), (0, -1), (1, 0), (-1, 0), (1, 1), (-1, 1), (1, -1), (-1, -1))


def strip(r):
    return pl.ds(8 * r, 8)


def rim(ref, side):
    dx, dy = SIDES[side]
    rows = {1: pl.ds(ROWS - 8, 8), -1: pl.ds(0, 8), 0: pl.ds(0, ROWS)}[dy]
    cols = {1: pl.ds(COLS - 128, 128), -1: pl.ds(0, 128), 0: pl.ds(0, COLS)}[dx]
    return ref.at[rows, cols]


def pack_ends(ext):
    lane = lax.broadcasted_iota(jnp.int32, (8, 128), 1)
    packed = jnp.zeros((8, 128), ext.dtype)
    for r in range(STRIPS):
        both = jnp.where(lane < 64, ext[strip(r), 0:128], ext[strip(r), COLS - 128 : COLS])
        both = pltpu.roll(both, 16 * r, 1) if r else both
        packed = jnp.where(((lane + 8) & 127) >> 4 == r, both, packed)
    return packed


def extend(ext, rims):
    from_s, from_n, from_w, from_e, from_sw, from_se, from_nw, from_ne = rims
    low = lax.broadcasted_iota(jnp.int32, (8, COLS), 0) < 4
    ext[ROWS:XR, 0:COLS] = jnp.where(low, from_n[...], from_s[...])
    lane = lax.broadcasted_iota(jnp.int32, (8, 128), 1)
    ends = jnp.where(((lane + 8) & 15) < 8, from_w[...], from_e[...])
    for r in range(STRIPS):
        ext[strip(r), COLS:XC] = pltpu.roll(ends, 128 - 16 * r, 1) if r else ends
    east8 = lane < 64
    low8 = lax.broadcasted_iota(jnp.int32, (8, 128), 0) < 4
    ext[ROWS:XR, COLS:XC] = jnp.where(
        low8,
        jnp.where(east8, from_ne[...], from_nw[...]),
        jnp.where(east8, from_se[...], from_sw[...]),
    )


def spread_rows(get, count, wrap=True):
    x = [get(r) for r in range(count)]
    sub = lax.broadcasted_iota(jnp.int32, x[0].shape, 0)
    up = [pltpu.roll(v, 7, 0) for v in x]
    down = [pltpu.roll(v, 1, 0) for v in x]
    out = []
    for r in range(count):
        north = jnp.where(sub == 7, up[(r + 1) % count] if wrap or r + 1 < count else 0.0, up[r])
        south = jnp.where(sub == 0, down[r - 1] if wrap or r else 0.0, down[r])
        out.append(x[r] + x[r] + (north + south))
    return out


def spread_cols(v):
    return v + v + (pltpu.roll(v, 1, 1) + pltpu.roll(v, XC - 1, 1))


def kernel(
    nx,
    ny,
    levels,
    tracer,
    u_east,
    v_north,
    kmt,
    dest_in,
    dz_in,
    wind,
    tracer_out,
    barotropic,
    c0,
    u0,
    v0,
    c1,
    k_x,
    ke,
    kn,
    rhs,
    ae,
    be,
    an,
    bn,
    depth,
    depth_e,
    depth_w,
    inv,
    diag,
    basis,
    dest,
    dz,
    zrim_row,
    zrim_col,
    zrim_corner,
    krim_row,
    krim_col,
    krim_corner,
    up_send,
    dn_send,
    col_send,
    up_recv,
    dn_recv,
    col_recv,
    rows1,
    rows1_recv,
    cols1,
    cols1_recv,
    rows_own,
    cols_own,
    kends,
    zends,
    row_flux,
    part,
    sums_x,
    part2,
    sums_y,
    still_out,
    still,
    first_out,
    slots,
    ring_d,
    edge_d,
    edge_s,
    edge_rows,
    edges_out,
    edges,
    edge_rows0,
    edges0_out,
    edges0,
    full,
    load_sem,
    ks,
    kr,
    rs,
    rr,
    zs,
    zr,
    xs,
    xr,
    ys,
    yr,
    ds,
    dr,
    fs,
    fr,
    es,
    er,
    gs,
    gr,
):
    mx = lax.axis_index("bx")
    my = lax.axis_index("by")
    pending, pending_rims = [], []

    def peer(dx, dy):
        return (lax.rem(mx + dx + nx, nx), lax.rem(my + dy + ny, ny))

    def send(src, dst, send_sem, recv_sem, dx, dy):
        copy = pltpu.make_async_remote_copy(
            src_ref=src, dst_ref=dst, send_sem=send_sem, recv_sem=recv_sem, device_id=peer(dx, dy), device_id_type=MESH
        )
        copy.start()
        pending.append(copy)
        return copy

    def send_rim(src, dst, send_sem, recv_sem, dx, dy):
        copy = pltpu.make_async_remote_copy(
            src_ref=src, dst_ref=dst, send_sem=send_sem, recv_sem=recv_sem, device_id=peer(dx, dy), device_id_type=MESH
        )
        goes, comes = {1: (has_n, has_s), -1: (has_s, has_n), 0: (None, None)}[dy]

        def guarded(action, guard):
            action() if guard is None else pl.when(guard)(action)

        guarded(copy.start, goes)
        pending_rims.append(lambda: guarded(copy.wait_send, goes))
        return lambda: guarded(copy.wait_recv, comes)

    has_n, has_s = my < ny - 1, my > 0
    barrier = pltpu.get_barrier_semaphore()

    def greet(dx, dy):
        pl.semaphore_signal(barrier, inc=1, device_id=peer(dx, dy), device_id_type=MESH)

    for off in sorted(range(1, ny), key=lambda o: -min(o, ny - o)):
        greet(0, off)
    for off in sorted(range(1, nx), key=lambda o: -min(o, nx - o)):
        greet(off, 0)
    for dx, dy in SIDES[4:]:
        pl.when(has_n if dy == 1 else has_s)(functools.partial(greet, dx, dy))
    n_peers = nx - 1 + ny - 1 + jnp.where(has_n, 2, 0) + jnp.where(has_s, 2, 0)

    last_cols = (slice(None), slice(None), pl.ds(COLS - 128, 128))
    other_cols = (slice(None), slice(None), pl.ds(0, COLS - 128))
    last_rows = (slice(None), pl.ds(ROWS - 8, 8))
    other_rows = (slice(None), pl.ds(0, ROWS - 8))
    loads = [
        pltpu.make_async_copy(kmt, k_x.at[pl.ds(0, ROWS), pl.ds(0, COLS)], load_sem.at[0]),
        pltpu.make_async_copy(dest_in, dest, load_sem.at[1]),
        pltpu.make_async_copy(dz_in, dz, load_sem.at[2]),
        pltpu.make_async_copy(tracer, c0, load_sem.at[3]),
        pltpu.make_async_copy(u_east.at[last_cols], u0.at[last_cols], load_sem.at[4]),
        pltpu.make_async_copy(v_north.at[last_rows], v0.at[last_rows], load_sem.at[5]),
        pltpu.make_async_copy(u_east.at[other_cols], u0.at[other_cols], load_sem.at[6]),
        pltpu.make_async_copy(v_north.at[other_rows], v0.at[other_rows], load_sem.at[7]),
        pltpu.make_async_copy(wind, rhs, load_sem.at[8]),
    ]
    for copy in loads:
        copy.start()

    def no_rim(at, corners):
        zrim_row[at] = jnp.zeros((8, COLS), F32)
        krim_row[at] = jnp.zeros((8, COLS), jnp.int32)
        for i in corners:
            zrim_corner[i] = jnp.zeros((8, 128), F32)
            krim_corner[i] = jnp.zeros((8, 128), jnp.int32)

    pl.when(jnp.logical_not(has_s))(lambda: no_rim(0, (0, 1)))
    pl.when(jnp.logical_not(has_n))(lambda: no_rim(1, (2, 3)))

    loads[0].wait()
    sub = lax.broadcasted_iota(jnp.int32, (8, COLS), 0)
    lane_row = lax.broadcasted_iota(jnp.int32, (8, COLS), 1)
    k_up = [pltpu.roll(k_x[strip(r), 0:COLS], 7, 0) for r in range(STRIPS)]
    for r in range(STRIPS):
        here = k_x[strip(r), 0:COLS]
        east = jnp.where(lane_row == COLS - 1, 0, pltpu.roll(here, COLS - 1, 1))
        north = jnp.where(sub == 7, k_up[r + 1] if r + 1 < STRIPS else 0, k_up[r])
        ke[strip(r), :] = jnp.minimum(here, east)
        kn[strip(r), :] = jnp.minimum(here, north)
    for copy in loads[1:6]:
        copy.wait()

    lane = lax.broadcasted_iota(jnp.int32, (ROWS, 128), 1)
    west = lane < 64
    group = ((lane + 4) & 127) >> 3
    slot = ((lane + 4) & 7) - 4

    def ends(field, k):
        return jnp.where(west, field[k, :, 0:128], field[k, :, COLS - 128 : COLS])

    def turned(value, lanes):
        return pltpu.roll(value, lanes % 128, 1) if lanes % 128 else value

    packed = jnp.zeros((ROWS, 128), F32)
    for k in range(levels):
        up_send[0, k : k + 1, :] = c0[k, ROWS - 1 : ROWS, :]
        up_send[1, k : k + 1, :] = v0[k, ROWS - 1 : ROWS, :]
        dn_send[k : k + 1, :] = c0[k, 0:1, :]
        both = jnp.where(slot == -2, turned(u0[k, :, COLS - 128 : COLS], 8 * k - 1), turned(ends(c0, k), 8 * k))
        packed = jnp.where(group == k, both, packed)
    col_send[...] = packed
    pl.semaphore_wait(barrier, n_peers)
    from_s = send_rim(up_send, up_recv, rs.at[0], rr.at[0], 0, 1)
    from_n = send_rim(dn_send, dn_recv, rs.at[1], rr.at[1], 0, -1)
    from_w = send_rim(col_send, col_recv.at[0], rs.at[2], rr.at[2], 1, 0)
    from_e = send_rim(col_send, col_recv.at[1], rs.at[3], rr.at[3], -1, 0)

    def rim_refs(row, col, corner):
        return [row.at[0], row.at[1], col.at[0], col.at[1]] + [corner.at[i] for i in range(4)]

    k_rims = rim_refs(krim_row, krim_col, krim_corner)
    kends[...] = pack_ends(k_x)
    k_sends = [
        send_rim(kends if SIDES[s][1] == 0 else rim(kmt, s), k_rims[s], ks.at[s], kr.at[s], *SIDES[s]) for s in range(8)
    ]

    def advance(get, k, put):
        def north_flux(r, c, up, nxt):
            return an[k, strip(r), :] * c + bn[k, strip(r), :] * jnp.where(sub == 7, nxt, up)

        below = jnp.zeros((8, COLS), F32)
        c, up = get(0), pltpu.roll(get(0), 7, 0)
        for r in range(STRIPS):
            if r + 1 < STRIPS:
                c_next = get(r + 1)
                up_next = pltpu.roll(c_next, 7, 0)
            flux = north_flux(r, c, up, up_next)
            down = pltpu.roll(flux, 1, 0)
            flux_e = ae[k, strip(r), :] * c + be[k, strip(r), :] * pltpu.roll(c, COLS - 1, 1)
            spread = flux_e - pltpu.roll(flux_e, 1, 1)
            spread = spread + (flux - jnp.where(sub == 0, below, down))
            put(r, c - spread)
            below, c, up = down, c_next, up_next

    def first_step(k, carry):
        for r in range(STRIPS):
            half_u, half_v = 0.5 * u0[k, strip(r), :], 0.5 * v0[k, strip(r), :]
            wet_e, wet_n = ke[strip(r), :] > k, kn[strip(r), :] > k
            ae[k, strip(r), :] = jnp.where(wet_e, half_u + KAPPA, 0.0)
            be[k, strip(r), :] = jnp.where(wet_e, half_u - KAPPA, 0.0)
            an[k, strip(r), :] = jnp.where(wet_n, half_v + KAPPA, 0.0)
            bn[k, strip(r), :] = jnp.where(wet_n, half_v - KAPPA, 0.0)

        def put(r, value):
            c1[k, strip(r), :] = value

        advance(lambda r: c0[k, strip(r), :], k, put)
        return carry

    for copy in loads[6:]:
        copy.wait()
    lax.fori_loop(0, levels, first_step, 0)
    packed = jnp.zeros((ROWS, 128), F32)
    for k in range(levels):
        rows_own[0, k : k + 1, :] = c1[k, ROWS - 1 : ROWS, :]
        rows_own[1, k : k + 1, :] = c1[k, 0:1, :]
        packed = jnp.where(group == k, turned(ends(c1, k), 8 * k), packed)
    cols_own[...] = packed

    for arrival in k_sends:
        arrival()
    extend(k_x, k_rims)
    level16 = lax.broadcasted_iota(jnp.int32, (levels, COLS), 0)
    wet_n = jnp.minimum(k_x[ROWS - 1 : ROWS, 0:COLS], k_x[ROWS : ROWS + 1, 0:COLS]) > level16
    wet_s = jnp.minimum(k_x[0:1, 0:COLS], k_x[XR - 1 : XR, 0:COLS]) > level16
    wet_e = jnp.minimum(k_x[0:ROWS, COLS - 1 : COLS], k_x[0:ROWS, COLS : COLS + 1]) > group
    wet_w = jnp.minimum(k_x[0:ROWS, 0:1], k_x[0:ROWS, XC - 1 : XC]) > group

    def face(velocity, here, there, wet):
        half = 0.5 * velocity
        return jnp.where(wet, (half + KAPPA) * here + (half - KAPPA) * there, 0.0)

    def rim_rows(north_row, south_row, own_north, own_south):
        row_flux[0] = face(up_send[1], own_north, north_row, wet_n)
        row_flux[1] = face(up_recv[1], south_row, own_south, wet_s)

    def rim_cols(own, westward, eastward):
        out = face(turned(col_send[...], 1), own, turned(eastward, -1), wet_e)
        into = face(turned(col_recv[0], 2), turned(westward, 1), own, wet_w)
        return jnp.where(slot == -1, -out, jnp.where(slot == 0, into, 0.0))

    for arrival in (from_s, from_n, from_w, from_e):
        arrival()
    rim_rows(dn_recv[...], up_recv[0], up_send[0], dn_send[...])
    flux_cols = rim_cols(col_send[...], col_recv[0], col_recv[1])

    def correct(field, k, flux):
        change = turned(flux, -8 * k)
        field[k, :, 0:128] = field[k, :, 0:128] + jnp.where(lane == 0, change, 0.0)
        field[k, :, COLS - 128 : COLS] = field[k, :, COLS - 128 : COLS] + jnp.where(lane == 127, change, 0.0)
        field[k, 0:1, :] = field[k, 0:1, :] + row_flux[1, k : k + 1, :]
        field[k, ROWS - 1 : ROWS, :] = field[k, ROWS - 1 : ROWS, :] - row_flux[0, k : k + 1, :]

    lane16 = lax.broadcasted_iota(jnp.int32, (levels, 128), 1)
    level8 = 8 * level16[:, 0:128]
    on_west, on_east = lane16 == level8, lane16 == ((level8 + 127) & 127)
    for at, row, sign in ((0, ROWS - 1, -1.0), (1, 0, 1.0)):
        line = jnp.broadcast_to(flux_cols[row : row + 1, :], (levels, 128))
        from_west = jnp.sum(jnp.where(on_west, line, 0.0), axis=1, keepdims=True)
        from_east = jnp.sum(jnp.where(on_east, line, 0.0), axis=1, keepdims=True)
        change = sign * row_flux[at]
        value = rows_own[at] + change
        rows1[at, :, 0:128] = value[:, 0:128] + jnp.where(lane16 == 0, from_west, 0.0)
        rows1[at, :, 128 : COLS - 128] = value[:, 128 : COLS - 128]
        rows1[at, :, COLS - 128 : COLS] = value[:, COLS - 128 : COLS] + jnp.where(lane16 == 127, from_east, 0.0)
        corner = jnp.where(on_west, change[:, 0:1], 0.0) + jnp.where(on_east, change[:, COLS - 1 : COLS], 0.0)
        cols_own[row : row + 1, :] = cols_own[row : row + 1, :] + jnp.sum(corner, axis=0, keepdims=True)
    cols1[...] = cols_own[...] + flux_cols
    from_s = send_rim(rows1.at[0], rows1_recv.at[0], rs.at[4], rr.at[4], 0, 1)
    from_n = send_rim(rows1.at[1], rows1_recv.at[1], rs.at[5], rr.at[5], 0, -1)
    from_w = send_rim(cols1, cols1_recv.at[0], rs.at[6], rr.at[6], 1, 0)
    from_e = send_rim(cols1, cols1_recv.at[1], rs.at[7], rr.at[7], -1, 0)
    for k in range(levels):
        correct(c1, k, flux_cols)

    subx = lax.broadcasted_iota(jnp.int32, (8, XC), 0)
    for r in range(STRIPS + 1):
        here = k_x[strip(r), :]
        total = jnp.zeros((8, XC), F32)
        for k in range(levels):
            total = total + jnp.where(here > k, dz[k], 0.0)
        depth[strip(r), :] = total
        depth_e[strip(r), :] = pltpu.roll(total, XC - 1, 1)
        depth_w[strip(r), :] = pltpu.roll(total, 1, 1)

    def ocean_of(r):
        return jnp.where(k_x[strip(r), :] > 0, 1.0, 0.0).astype(F32)

    rows_o = spread_rows(ocean_of, STRIPS + 1)
    rows_d = spread_rows(lambda r: depth[strip(r), :], STRIPS + 1)
    for r in range(STRIPS + 1):
        d = depth[strip(r), :]
        o = ocean_of(r)
        total = d * spread_cols(rows_o[r]) + spread_cols(rows_d[r]) - 8.0 * d
        whole = SIGMA + 0.25 * o * total
        diag[strip(r), :] = whole
        inv[strip(r), :] = o / whole

    blocks = COLS // BS

    def scatter(get, parts, outbox, inbox, ssem, rsem):
        copies = []
        for off in sorted(range(nx), key=lambda o: -min(o, nx - o)):
            target = lax.rem(mx + off, nx)
            hits = [dest[0, m] == target for m in range(blocks)]
            here = outbox.at[off] if off else inbox(0)
            for i in range(parts):
                chosen = None
                for m in range(blocks):
                    piece = get(m, i)
                    chosen = jnp.where(hits[m], piece, jnp.zeros_like(piece) if chosen is None else chosen)
                here[i] = chosen
            if off:
                copies.append(send(outbox.at[off], inbox(off), ssem.at[off], rsem.at[off], off, 0))
        return copies

    def block(m):
        return pl.ds(m * BS, BS)

    still_copies = scatter(
        lambda m, i: depth[0:ROWS, block(m)], 1, still_out, lambda off: still.at[off, pl.ds(0, 1)], ds, dr
    )

    lane8 = lax.broadcasted_iota(jnp.int32, (8, BS), 1)

    def pack(both):
        packed = jnp.zeros((8, BS), F32)
        for m in range(blocks):
            packed = jnp.where(((lane8 + 8) & 127) >> 4 == m, turned(both[m], 16 * m), packed)
        return packed

    def tiles(ref, r):
        return [ref[strip(r), block(m)] for m in range(blocks + 1)]

    def pack_ring(tile):
        return pack([jnp.where(lane8 < 64, tile[m + 1], tile[m - 1]) for m in range(blocks)])

    def pack_edges(tile):
        return pack([jnp.where(lane8 == 0, turned(tile[m], 1), turned(tile[m], -1)) for m in range(blocks)])

    for r in range(STRIPS):
        ring_d[strip(r), :] = pack_ring(tiles(depth, r))
        edge_d[strip(r), :] = pack_edges(tiles(depth, r))
        edge_s[strip(r), :] = (0.25 / HALF) * pack_edges(tiles(inv, r))

    def edge_columns(step, ring_x, ring_dx, scale, cols_m):
        inner_x = spread_rows(lambda r: ring_x[r], STRIPS, False)
        inner_dx = spread_rows(lambda r: ring_dx[r], STRIPS, False)
        for r in range(STRIPS):
            edge = scale(r) * (edge_d[strip(r), :] * inner_x[r] + inner_dx[r])
            for m in range(blocks):
                moved = turned(edge, 16 * r + 2 * step + 1 - 16 * m)
                cols_m[m] = jnp.where((lane8 >> 1) == 8 * r + step, moved, cols_m[m])

    def edge_lines(step, x, dx, scale, out_rows):
        beyond_x, beyond_dx = spread_cols(x), spread_cols(dx)
        for row, out, at in ((ROWS - 1, 0, 0), (0, 7, 1)):
            edge = scale(row) * (depth[row : row + 1, :] * beyond_x[out : out + 1] + beyond_dx[out : out + 1])
            out_rows[2 * step + at : 2 * step + at + 1, :] = edge[:, 0:COLS]

    def swapped(value):
        return jnp.where((lane8 & 1) == 1, turned(value, 1), turned(value, -1))

    def one_if(wet):
        return jnp.where(wet, 1.0, 0.0).astype(F32)

    ring_0 = [ring_d[strip(r), :] for r in range(STRIPS)]
    edge_cols = [jnp.zeros((8, BS), F32) for _ in range(blocks)]
    edge_columns(
        0, [one_if(v > 0.0) for v in ring_0], ring_0, lambda r: 0.25 * one_if(edge_d[strip(r), :] > 0.0), edge_cols
    )
    edge_rows0[...] = jnp.zeros((8, COLS), F32)
    edge_lines(
        0,
        ocean_of(STRIPS),
        depth[strip(STRIPS), :],
        lambda row: 0.25 * one_if(depth[row : row + 1, :] > 0.0),
        edge_rows0,
    )
    edge_cols0 = [swapped(v) for v in edge_cols]
    edge0_copies = scatter(
        lambda m, i: edge_cols0[m] if i else edge_rows0[:, block(m)], 2, edges0_out, lambda off: edges0.at[off], gs, gr
    )

    def second_step(k, carry):
        def put(r, value):
            tracer_out[k, strip(r), :] = value
            wet = k_x[strip(r), 0:COLS] > k
            rhs[strip(r), :] = rhs[strip(r), :] + jnp.where(wet, dz[k] * value, 0.0)

        advance(lambda r: c1[k, strip(r), :], k, put)
        return carry

    lax.fori_loop(0, levels, second_step, 0)

    for arrival in (from_s, from_n, from_w, from_e):
        arrival()
    rim_rows(rows1_recv[1], rows1_recv[0], rows1[0], rows1[1])
    flux_cols = rim_cols(cols1[...], cols1_recv[0], cols1_recv[1])
    dz_rows = jnp.zeros((levels, 128), F32)
    dz_cols = jnp.zeros((ROWS, 128), F32)
    for k in range(levels):
        dz_rows = jnp.where(level16[:, 0:128] == k, dz[k], dz_rows)
        dz_cols = jnp.where(group == k, dz[k], dz_cols)
    dz_rows = jnp.concatenate([dz_rows] * (COLS // 128), axis=1)
    weighted = dz_cols * flux_cols
    change_w = jnp.sum(jnp.where(slot == 0, weighted, 0.0), axis=1, keepdims=True)
    change_e = jnp.sum(jnp.where(slot == -1, weighted, 0.0), axis=1, keepdims=True)
    rhs[:, 0:128] = rhs[:, 0:128] + jnp.where(lane == 0, change_w, 0.0)
    rhs[:, COLS - 128 : COLS] = rhs[:, COLS - 128 : COLS] + jnp.where(lane == 127, change_e, 0.0)
    rhs[0:1, :] = rhs[0:1, :] + jnp.sum(dz_rows * row_flux[1], axis=0, keepdims=True)
    rhs[ROWS - 1 : ROWS, :] = rhs[ROWS - 1 : ROWS, :] - jnp.sum(dz_rows * row_flux[0], axis=0, keepdims=True)

    for r in range(STRIPS):
        start = jnp.where(k_x[strip(r), 0:COLS] > 0, rhs[strip(r), :], 0.0)
        basis[0, strip(r), 0:COLS] = start * inv[strip(r), 0:COLS]
    z_rims = rim_refs(zrim_row, zrim_col, zrim_corner)
    zends[...] = pack_ends(basis.at[0])
    z_sends = [
        send_rim(zends if SIDES[s][1] == 0 else rim(basis.at[0], s), z_rims[s], zs.at[s], zr.at[s], *SIDES[s])
        for s in (4, 5, 6, 7, 0, 1, 2, 3)
    ]
    first_copies = scatter(
        lambda m, i: basis[0, 0:ROWS, block(m)], 1, first_out, lambda off: slots.at[off, pl.ds(0, 1)], fs, fr
    )
    for k in range(levels):
        correct(tracer_out, k, flux_cols)

    for copy in still_copies + edge0_copies:
        copy.wait_recv()
    sub8 = lax.broadcasted_iota(jnp.int32, (8, BS), 0)
    sides = (lane8 == 0) | (lane8 == BS - 1)

    def spread(values):
        out = []
        for v in spread_rows(lambda r: values[r], STRIPS, False):
            east = jnp.where(lane8 == BS - 1, 0.0, pltpu.roll(v, BS - 1, 1))
            out.append(v + v + (east + jnp.where(lane8 == 0, 0.0, pltpu.roll(v, 1, 1))))
        return out

    def with_edges(value, r, step, packet, n):
        value = value + jnp.where(sides, pltpu.roll(packet[n, 1], BS - (16 * r + 2 * step + 1), 1), 0.0)
        if r == STRIPS - 1:
            value = value + jnp.where(sub8 == 7, packet[n, 0, 2 * step : 2 * step + 1, :], 0.0)
        if r == 0:
            value = value + jnp.where(sub8 == 0, packet[n, 0, 2 * step + 1 : 2 * step + 2, :], 0.0)
        return value

    def block_diagonal(n, carry):
        d = [still[n, 0, strip(r), :] for r in range(STRIPS)]
        o = [one_if(v > 0.0) for v in d]
        wide_o, wide_d = spread(o), spread(d)
        for r in range(STRIPS):
            total = d[r] * wide_o[r] + wide_d[r] - 8.0 * d[r]
            whole = with_edges(SIGMA + 0.25 * o[r] * total, r, 0, edges0, n)
            full[n, strip(r), :] = whole
            still[n, 1, strip(r), :] = o[r] / whole
        return carry

    lax.fori_loop(0, nx, block_diagonal, 0)

    for arrival in z_sends:
        arrival()
    extend(basis.at[0], z_rims)

    moments = [jnp.zeros((8, 128), F32) for _ in range(8)]

    def inner_products(j, others):
        totals = [jnp.zeros((8, 128), F32) for _ in others]
        for r in range(STRIPS):
            weighted = diag[strip(r), 0:COLS] * basis[j, strip(r), 0:COLS]
            for n, i in enumerate(others):
                product = weighted * basis[i, strip(r), 0:COLS]
                for m in range(COLS // 128):
                    totals[n] = totals[n] + product[:, 128 * m : 128 * (m + 1)]
        return totals

    moments[0] = inner_products(0, [0])[0]
    for step in range(ITERS):
        rows_x = spread_rows(lambda r: basis[step, strip(r), :], STRIPS + 1)
        rows_dx = spread_rows(lambda r: depth[strip(r), :] * basis[step, strip(r), :], STRIPS + 1)
        for r in range(STRIPS + 1 if step < ITERS - 1 else STRIPS):
            d, x = depth[strip(r), :], basis[step, strip(r), :]
            image = 2.0 * (d * rows_x[r] + rows_dx[r]) - 8.0 * (d * x)
            image = image + pltpu.roll(depth_e[strip(r), :] * rows_x[r] + rows_dx[r], 1, 1)
            image = image + pltpu.roll(depth_w[strip(r), :] * rows_x[r] + rows_dx[r], XC - 1, 1)
            scale = (0.25 / HALF) * inv[strip(r), :]
            following = scale * image - (CENTRE / HALF) * x
            if step:
                following = following + following - basis[step - 1, strip(r), :]
            if step < ITERS - 1:
                basis[step + 1, strip(r), :] = following
            else:
                basis[step + 1, strip(r), 0:COLS] = following[:, 0:COLS]
        both = [step, step + 1] if step < ITERS - 1 else [step]
        moments[2 * step + 1 : 2 * step + 1 + len(both)] = inner_products(step + 1, both)

    row8 = lax.broadcasted_iota(jnp.int32, (8, 128), 0)
    mine = jnp.zeros((8, 128), F32)
    for m in range(8):
        mine = jnp.where(row8 == m, jnp.sum(moments[m], axis=0, keepdims=True), mine)
    part[...] = mine
    x_sends = [send(part, sums_x.at[off], xs.at[off], xr.at[off], off, 0) for off in range(1, nx)]
    edge_cols = [jnp.zeros((8, BS), F32) for _ in range(blocks)]
    for step in range(ITERS):
        ring_x = [pack_ring(tiles(basis.at[step], r)) for r in range(STRIPS)]
        ring_dx = [ring_d[strip(r), :] * ring_x[r] for r in range(STRIPS)]
        edge_columns(step, ring_x, ring_dx, lambda r: edge_s[strip(r), :], edge_cols)
        x = basis[step, strip(STRIPS), :]
        edge_lines(
            step, x, depth[strip(STRIPS), :] * x, lambda row: (0.25 / HALF) * inv[row : row + 1, :], edge_rows
        )
    edge_cols = [swapped(v) for v in edge_cols]
    edge_copies = scatter(
        lambda m, i: edge_cols[m] if i else edge_rows[:, block(m)], 2, edges_out, lambda off: edges.at[off], es, er
    )
    total = mine
    for off in range(1, nx):
        x_sends[off - 1].wait_recv()
        total = total + sums_x[off]
    part2[...] = total
    y_sends = [send(part2, sums_y.at[off], ys.at[off], yr.at[off], 0, off) for off in range(1, ny)]

    for copy in first_copies + edge_copies:
        copy.wait_recv()

    def repeat(n, carry):
        x = [slots[n, 0, strip(r), :] for r in range(STRIPS)]
        before = x
        for step in range(ITERS):
            dx = [still[n, 0, strip(r), :] * x[r] for r in range(STRIPS)]
            wide_x, wide_dx = spread(x), spread(dx)
            after = []
            for r in range(STRIPS):
                image = still[n, 0, strip(r), :] * wide_x[r] + wide_dx[r] - 8.0 * dx[r]
                following = (0.25 / HALF) * still[n, 1, strip(r), :] * image - (CENTRE / HALF) * x[r]
                following = with_edges(following, r, step, edges, n)
                if step:
                    following = following + following - before[r]
                slots[n, step + 1, strip(r), :] = following
                after.append(following)
            before, x = x, after
        return carry

    lax.fori_loop(0, nx, repeat, 0)

    for off in range(1, ny):
        y_sends[off - 1].wait_recv()
        total = total + sums_y[off]
    total = jnp.sum(total, axis=1, keepdims=True)
    g = [total[m : m + 1, 0:1] for m in range(8)]

    nu = [g[0], g[1]]
    for m in range(2, 8):
        nu.append(g[m] + g[m] - nu[m % 2])
    gram = {}
    for i in range(ITERS):
        for j in range(ITERS + 1):
            gram[i, j] = 0.5 * (nu[i + j] + nu[abs(i - j)]) if i and j else nu[i + j]

    def dot(a, b):
        terms = []
        for i, first_c in enumerate(a):
            inside = None
            for j, second_c in enumerate(b):
                term = gram[min(i, j), max(i, j)] * second_c
                inside = term if inside is None else inside + term
            terms.append(first_c * inside)
        return functools.reduce(lambda p, q: p + q, terms)

    one = jnp.ones((1, 1), F32)
    zero = jnp.zeros((1, 1), F32)
    z, direction, x = [one], [one], [zero] * ITERS
    norm = dot(z, z)
    for step in range(ITERS):
        image = [(1.0 - CENTRE) * v for v in direction] + [zero]
        for i, v in enumerate(direction):
            if i == 0:
                image[1] = image[1] - HALF * v
            else:
                image[i + 1] = image[i + 1] - (0.5 * HALF) * v
                image[i - 1] = image[i - 1] - (0.5 * HALF) * v
        alpha = norm / dot(direction, image)
        for i, v in enumerate(direction):
            x[i] = x[i] + alpha * v
        z = [v - alpha * w for v, w in zip(z + [zero], image)]
        if step < ITERS - 1:
            following = dot(z, z)
            ratio = following / norm
            direction = [v + ratio * w for v, w in zip(z, direction + [zero])]
            norm = following

    for n in range(nx):
        place = pl.ds(pl.multiple_of(lax.rem(mx - n + nx, nx) * BS, BS), BS)
        for r in range(STRIPS):
            y = [slots[n, i, strip(r), :] for i in range(ITERS + 1)]
            barotropic[0, strip(r), place] = sum(x[i] * y[i] for i in range(ITERS))
            barotropic[1, strip(r), place] = full[n, strip(r), :] * sum(z[i] * y[i] for i in range(ITERS + 1))
    for copy in pending:
        copy.wait_send()
    for departure in pending_rims:
        departure()


def on_device(tracer, u_east, v_north, kmt, dest, dz, wind):
    nx, ny = lax.axis_size("bx"), lax.axis_size("by")
    levels = tracer.shape[0]
    slab = pltpu.VMEM((levels, ROWS, COLS), F32)
    ext = pltpu.VMEM((XR, XC), F32)
    flat = pltpu.VMEM((ROWS, COLS), F32)
    flat_i = pltpu.VMEM((ROWS, COLS), jnp.int32)
    rows = pltpu.VMEM((levels, COLS), F32)
    rows2 = pltpu.VMEM((2, levels, COLS), F32)
    cols = pltpu.VMEM((ROWS, 128), F32)
    cols2 = pltpu.VMEM((2, ROWS, 128), F32)

    def rims(dtype):
        return [
            pltpu.VMEM((2, 8, COLS), dtype),
            pltpu.VMEM((2, 8, 128), dtype),
            pltpu.VMEM((4, 8, 128), dtype),
        ]

    scratch = [slab] * 4 + [pltpu.VMEM((XR, XC), jnp.int32), flat_i, flat_i, flat] + [slab] * 4
    scratch += [ext, ext, ext, ext, ext, pltpu.VMEM((ITERS + 1, XR, XC), F32)]
    scratch += [pltpu.SMEM(dest.shape, jnp.int32), pltpu.SMEM(dz.shape, F32)]
    scratch += rims(F32) + rims(jnp.int32)
    scratch += [rows2, rows, cols, rows2, rows, cols2]
    scratch += [rows2, rows2, cols, cols2, rows2, cols]
    scratch += [pltpu.VMEM((8, 128), jnp.int32), pltpu.VMEM((8, 128), F32), rows2]
    scratch += [
        pltpu.VMEM((8, 128), F32),
        pltpu.VMEM((nx, 8, 128), F32),
        pltpu.VMEM((8, 128), F32),
        pltpu.VMEM((ny, 8, 128), F32),
        pltpu.VMEM((nx, 1, ROWS, BS), F32),
        pltpu.VMEM((nx, 2, ROWS, BS), F32),
        pltpu.VMEM((nx, 1, ROWS, BS), F32),
        pltpu.VMEM((nx, ITERS + 1, ROWS, BS), F32),
        cols,
        cols,
        cols,
        pltpu.VMEM((8, COLS), F32),
        pltpu.VMEM((nx, 2, 8, BS), F32),
        pltpu.VMEM((nx, 2, 8, BS), F32),
        pltpu.VMEM((8, COLS), F32),
        pltpu.VMEM((nx, 2, 8, BS), F32),
        pltpu.VMEM((nx, 2, 8, BS), F32),
        pltpu.VMEM((nx, ROWS, BS), F32),
    ]
    counts = [9] + [8] * 6 + [nx, nx, ny, ny] + [nx] * 8
    scratch += [pltpu.SemaphoreType.DMA((n,)) for n in counts]
    in_vmem = pl.BlockSpec(memory_space=pltpu.VMEM)
    hbm = pl.BlockSpec(memory_space=pltpu.HBM)
    return pl.pallas_call(
        functools.partial(kernel, nx, ny, levels),
        out_shape=(
            jax.ShapeDtypeStruct(tracer.shape, F32),
            jax.ShapeDtypeStruct((2, ROWS, nx * BS), F32),
        ),
        in_specs=[hbm] * 7,
        out_specs=(in_vmem, in_vmem),
        scratch_shapes=scratch,
        compiler_params=pltpu.CompilerParams(
            collective_id=0, has_side_effects=True, vmem_limit_bytes=32 * 1024 * 1024
        ),
    )(*[pltpu.with_memory_space_constraint(x, pltpu.HBM) for x in (tracer, u_east, v_north, kmt, dest, dz, wind)])


def solution(mesh):
    in_specs = (
        P(None, "by", "bx"),
        P(None, "by", "bx"),
        P(None, "by", "bx"),
        P("by", "bx"),
        P("by", "bx"),
        P(),
        P("by", "bx"),
    )
    out_specs = (P(None, "by", "bx"), P(None, "by", "bx"))
    return jax.shard_map(
        on_device, mesh=mesh, in_specs=in_specs, out_specs=out_specs, check_vma=False
    )
```
